32 devices in a mesh: groups: 1, expert: 32 (over z, y, x, core).
Axes of the slice: x: 2, y: 2, z: 4, core: 2. Of those that a mesh axis runs over, the one named last changes fastest.
Arguments:
- tokens: bfloat16 [512, 3584], P(('groups', 'expert')), may hold values from -6 to 6
- expert_ids: int32 [512, 8], P(('groups', 'expert')), may hold values from 0 to 15, all different within a row; in each aligned block of 16 rows (0 to 15, 16 to 31, ...) at most 10 rows name the same one
- gate_values: float32 [512, 8], P(('groups', 'expert')), may hold values from 0.1 to 1
- cotangent: bfloat16 [512, 3584], P(('groups', 'expert')), may hold values from -6 to 6
- gate_weight: bfloat16 [32, 3584, 512], P('expert'), may hold values from -0.09375 to 0.09375
- up_weight: bfloat16 [32, 3584, 512], P('expert'), may hold values from -0.09375 to 0.09375
- down_weight: bfloat16 [32, 512, 3584], P('expert'), may hold values from -0.1875 to 0.1875
Outputs:
- layer_out: bfloat16 [512, 3584], P(('groups', 'expert'))
- token_grad: bfloat16 [512, 3584], P(('groups', 'expert'))
The draws below stay inside these ranges and needn't reach their ends.
Inputs may be any that keep to these rules, and one draw needn't show every extreme that they name: `expert_ids`: each row names 8 different experts; among the rows of one device no expert is named by more than 10 rows, a bound that some block reaches of them.
All inputs are finite; a program needn't handle non-finite values.
Results may differ from the reference program's by a relative error of at most 0.012.
Values may be sent and summed in bfloat16 or wider, within the bound.
No kernel may reach another device: no remote copies, remote signals or barrier semaphores. Data moves between devices by JAX's collectives and lax.ppermute only.
A program may use at most 128 MiB of HBM per device.

```python
import math
import jax
import jax.numpy as jnp
import numpy as np
from jax import lax

D = 3584
FF = 1024
TOP = 8
TOK_DEV = 16
HALF = 512
EXPERTS = 16
CAP = 10
BLOCKS = 28
TOKENS = 512
N_EXPERT = 32


def shard_levels(rng, extent, shards, low, top_value):
    gain, own = 1.0, jax.random.fold_in(rng, 6)
    for axis_at, blocks in shards:
        steps = jnp.exp(jax.random.uniform(jax.random.fold_in(own, axis_at), (blocks,), jnp.float32, low / len(shards), top_value / len(shards)))
        gain = gain * jnp.repeat(steps, extent[axis_at] // blocks).reshape([-1 if axis == axis_at else 1 for axis in range(len(extent))])
    return gain


def deal_out(stream_key, own, number, rows, number_of, top, reach, slope):
    sequence = jax.random.permutation(stream_key, number_of)
    packed, usual = load_shares(number_of, rows * top, reach, slope, True), load_shares(number_of, rows * top, reach, slope, False)
    places = jnp.arange(number_of)

    def named(sizes, rotation):
        used = int((sizes > 0).sum())
        fixed = max(1, used // 4)
        passed = fixed + (places - fixed + rotation * (used - fixed)) % max(1, number_of - fixed)
        return jnp.zeros((number_of,), jnp.int32).at[sequence[jnp.where(places < fixed, places, passed)]].set(jnp.asarray(sizes, jnp.int32))

    sizes = jnp.where(number % 4 == 0, named(packed, number // 4), named(usual, number - number // 4 - 1))
    mixed = jax.random.permutation(jax.random.fold_in(own, 3), number_of)
    donor, sink = mixed[0:number_of // 2 * 2:2], mixed[1:number_of // 2 * 2:2]
    margin = jnp.minimum(sizes[donor] - 1, reach - sizes[sink]) // 2
    margin = jnp.where((donor == sequence[0]) | (sink == sequence[0]) | (sizes[sink] == 0), 0, jnp.maximum(margin, 0))
    passed = jax.random.randint(jax.random.fold_in(own, 4), (number_of // 2,), 0, 1 << 20) % (margin + 1)
    sizes = sizes.at[donor].add(-passed).at[sink].add(passed)
    labels = jnp.searchsorted(jnp.cumsum(sizes), jnp.arange(rows * top), side="right").astype(jnp.int32)
    grid = labels.reshape(top, rows).T
    grid = grid[jax.random.permutation(jax.random.fold_in(own, 1), rows)]
    rotation = jax.random.randint(jax.random.fold_in(own, 2), (rows, 1), 0, top)
    return jnp.take_along_axis(grid, (jnp.arange(top)[None, :] + rotation) % top, axis=1)


def load_shares(amount, total, limit, skew, full):
    weights = [(1 << 20) // math.isqrt(rank ** skew) + 1 for rank in range(1, amount + 1)]
    largest = limit if full else min(limit, max(-(-total // amount), total * weights[0] // sum(weights)))
    least = 1 if total - largest >= amount - 1 else 0
    holding, surplus = [largest] + [least] * (amount - 1), total - largest - least * (amount - 1)
    while surplus > 0:
        free = [i for i in range(1, amount) if holding[i] < largest] or [i for i in range(1, amount) if holding[i] < limit]
        whole, left = sum([weights[i] for i in free]), surplus
        for i in free:
            addition = min(limit - holding[i], max(1, left * weights[i] // whole), surplus)
            holding[i] = holding[i] + addition
            surplus = surplus - addition
    return np.array(holding)


def bell_draw(key, extent, spread, bound, shards=(), kind=jnp.bfloat16):
    level = shard_levels(key, extent, shards, -0.22, 0.18) if shards else 1.0
    result = jax.random.normal(key, extent, jnp.float32) * spread * level
    return jnp.minimum(jnp.maximum(result, -bound), bound).astype(kind)


def setup_inputs(seed: int = 0, part: int = 0) -> dict:
    key_of = jax.random.split(jax.random.key(seed), 8)
    part_keys = jax.random.split(jax.random.fold_in(key_of[7], part), 8)
    tokens = bell_draw(part_keys[0], (TOKENS, D), 1.0, 6.0, ((0, 32),))
    expert_ids_keys = jax.random.split(jax.random.fold_in(part_keys[1], 1), TOKENS // TOK_DEV)
    expert_ids_turns = jax.random.permutation(jax.random.fold_in(part_keys[1], 3), TOKENS // TOK_DEV)
    expert_ids = jax.vmap(lambda own, number: deal_out(jax.random.fold_in(part_keys[1], 2), own, number, TOK_DEV, EXPERTS, TOP, CAP, 2))(expert_ids_keys, expert_ids_turns).reshape((TOKENS, TOP))
    gate_values = jnp.clip(jnp.exp(math.log(1.0) - 2.3025851 * jax.random.uniform(part_keys[2], (TOKENS, TOP), jnp.float32) ** shard_levels(part_keys[2], (TOKENS, TOP), ((0, 32),), -0.2, 0.2)), 0.1, 1.0)
    cotangent = bell_draw(part_keys[3], (TOKENS, D), 1.0, 6.0, ((0, 32),))
    gate_weight = bell_draw(key_of[4], (2 * EXPERTS, D, HALF), D ** -0.5, 0.09375, ((0, 32),))
    up_weight = bell_draw(key_of[5], (2 * EXPERTS, D, HALF), D ** -0.5, 0.09375, ((0, 32),))
    down_weight = bell_draw(key_of[6], (2 * EXPERTS, HALF, D), FF ** -0.5, 0.1875, ((0, 32),))
    return dict(tokens=tokens, expert_ids=expert_ids, gate_values=gate_values, cotangent=cotangent, gate_weight=gate_weight, up_weight=up_weight, down_weight=down_weight)


def silu_parts(values):
    sigma = jax.nn.sigmoid(values)
    return values * sigma, sigma * (1.0 + values * (1.0 - sigma))


def reference(tokens, expert_ids, gate_values, cotangent, gate_weight, up_weight, down_weight):
    route_rows = TOK_DEV * TOP
    blocked = tokens.astype(jnp.float32).reshape(TOKENS, BLOCKS, 128)
    block_scale = (jnp.max(jnp.abs(blocked), axis=2) + 1e-6).astype(jnp.bfloat16)
    wide_scale = block_scale.astype(jnp.float32)[:, :, None]
    quantized = (blocked / wide_scale).astype(jnp.bfloat16)
    quantized = lax.optimization_barrier(quantized)
    dequant = (quantized.astype(jnp.float32) * wide_scale).astype(jnp.bfloat16).reshape(TOKENS, D)

    device_ids = expert_ids.reshape(N_EXPERT, route_rows).astype(jnp.int32)
    onehot = (device_ids[:, :, None] == jnp.arange(EXPERTS, dtype=jnp.int32)[None, None, :]).astype(jnp.int32)
    earlier = (jnp.cumsum(onehot, axis=1) - onehot).astype(jnp.int32)
    slot_index = jnp.sum(earlier * onehot, axis=2).astype(jnp.int32)
    source_dev = jnp.arange(N_EXPERT, dtype=jnp.int32)[:, None]
    global_slot = ((device_ids * N_EXPERT + source_dev) * CAP + slot_index).astype(jnp.int32)
    flat_slot = global_slot.reshape(TOKENS * TOP)
    route_table = jnp.full((EXPERTS * N_EXPERT * CAP,), -1, jnp.int32)
    route_table = route_table.at[flat_slot].set(jnp.arange(TOKENS * TOP, dtype=jnp.int32))

    route_grad = (gate_values[:, :, None] * cotangent.astype(jnp.float32)[:, None, :]).astype(jnp.bfloat16)
    route_grad = route_grad.reshape(TOKENS * TOP, D)

    def one_expert(expert_index):
        start = (expert_index * N_EXPERT * CAP).astype(jnp.int32)
        route_index = lax.dynamic_slice_in_dim(route_table, start, N_EXPERT * CAP)
        valid = (route_index >= 0)[:, None]
        safe_index = jnp.where(route_index >= 0, route_index, 0).astype(jnp.int32)
        rows_in = jnp.where(valid, dequant[safe_index // TOP], jnp.zeros_like(dequant[:1]))
        grads_in = jnp.where(valid, route_grad[safe_index], jnp.zeros_like(route_grad[:1]))
        outs_list = []
        backs_list = []
        for slab_index in range(2):
            slab = (2 * expert_index + slab_index).astype(jnp.int32)
            gate_slab = lax.dynamic_index_in_dim(gate_weight, slab, 0, keepdims=False)
            up_slab = lax.dynamic_index_in_dim(up_weight, slab, 0, keepdims=False)
            down_slab = lax.dynamic_index_in_dim(down_weight, slab, 0, keepdims=False)
            pre_gate = jnp.dot(rows_in, gate_slab, preferred_element_type=jnp.float32)
            pre_up = jnp.dot(rows_in, up_slab, preferred_element_type=jnp.float32)
            activated, silu_slope = silu_parts(pre_gate)
            hidden = (activated * pre_up).astype(jnp.bfloat16)
            outs_list.append(jnp.dot(hidden, down_slab, preferred_element_type=jnp.float32).astype(jnp.bfloat16))
            hidden_grad = jnp.dot(grads_in, down_slab.T, preferred_element_type=jnp.float32)
            gate_grad = (hidden_grad * pre_up * silu_slope).astype(jnp.bfloat16)
            up_grad = (hidden_grad * activated).astype(jnp.bfloat16)
            back_part = jnp.dot(gate_grad, gate_slab.T, preferred_element_type=jnp.float32)
            back_part = back_part + jnp.dot(up_grad, up_slab.T, preferred_element_type=jnp.float32)
            backs_list.append(back_part.astype(jnp.bfloat16))
        out_rows = (outs_list[0].astype(jnp.float32) + outs_list[1].astype(jnp.float32)).astype(jnp.bfloat16)
        back_rows = (backs_list[0].astype(jnp.float32) + backs_list[1].astype(jnp.float32)).astype(jnp.bfloat16)
        return out_rows, back_rows

    out_all, back_all = lax.map(one_expert, jnp.arange(EXPERTS, dtype=jnp.int32))
    expert_out = out_all.reshape(EXPERTS * N_EXPERT * CAP, D)[flat_slot].reshape(TOKENS, TOP, D)
    layer_out = jnp.sum(expert_out.astype(jnp.float32) * gate_values[:, :, None], axis=1).astype(jnp.bfloat16)
    row_grad = back_all.reshape(EXPERTS * N_EXPERT * CAP, D)[flat_slot].reshape(TOKENS, TOP, D)
    token_grad = jnp.sum(row_grad.astype(jnp.float32), axis=1).astype(jnp.bfloat16)
    return layer_out, token_grad
```

```python
import jax
import jax.numpy as jnp
from jax import lax
from jax.sharding import PartitionSpec as P


def code_rows(tokens, blocks):
    blocked = tokens.astype(jnp.float32).reshape(tokens.shape[0], blocks, 128)
    scale = lax.reduce_precision(jnp.max(jnp.abs(blocked), axis=2) + 1e-06, 8, 7)[:, :, None]
    quantized = lax.reduce_precision(blocked / scale, 8, 7)
    dequant = (quantized * scale).astype(jnp.bfloat16)
    return dequant.reshape(tokens.shape)


def gate_columns(expert_ids, gate_values, experts):
    named = expert_ids[:, :, None] == jnp.arange(experts, dtype=jnp.int32)[None, None, :]
    rest = jnp.sum(jnp.where(named, gate_values[:, :, None], 0.0), axis=1)
    pieces = []
    for _ in range(3):
        piece = lax.reduce_precision(rest, 8, 7)
        pieces.append(piece.astype(jnp.bfloat16))
        rest = rest - piece
    return jnp.concatenate(pieces, axis=1)


def on_device(tokens, expert_ids, gate_values, cotangent, gate_weight, up_weight, down_weight):
    width = tokens.shape[1]
    devices = lax.axis_size("expert")
    experts = devices // 2
    expert = lax.axis_index("expert") // 2
    dequant = code_rows(tokens, width // 128)
    columns = gate_columns(expert_ids, gate_values, experts)
    padding = -columns.shape[1] % 128
    columns = jnp.pad(columns, ((0, 0), (0, padding)))
    rows = lax.all_gather(jnp.concatenate([dequant, columns], axis=1), "expert", tiled=True)
    cots = lax.all_gather(cotangent, "expert", tiled=True)
    x = rows[:, :width]
    pieces = rows[:, width : width + 3 * experts].astype(jnp.float32)
    pieces = pieces.reshape(-1, 3, experts)
    mine = (jnp.arange(experts, dtype=jnp.int32) == expert).astype(jnp.float32)
    gate = jnp.sum(jnp.sum(pieces, axis=1) * mine, axis=1, keepdims=True)

    gate_slab, up_slab, down_slab = gate_weight[0], up_weight[0], down_weight[0]
    f32 = jnp.float32
    pre_gate = jnp.dot(x, gate_slab, preferred_element_type=f32)
    pre_up = jnp.dot(x, up_slab, preferred_element_type=f32)
    sigma = jax.nn.sigmoid(pre_gate)
    activated = pre_gate * sigma
    slope = sigma * (1.0 + pre_gate * (1.0 - sigma))
    hidden = (activated * pre_up).astype(jnp.bfloat16)
    partial = jnp.dot(hidden, down_slab, preferred_element_type=f32)
    layer_out = lax.psum_scatter(
        (partial * gate).astype(jnp.bfloat16), "expert", scatter_dimension=0, tiled=True
    )
    contract_cols = (((1,), (1,)), ((), ()))
    hidden_grad = gate * lax.dot_general(cots, down_slab, contract_cols, preferred_element_type=f32)
    gate_grad = (hidden_grad * pre_up * slope).astype(jnp.bfloat16)
    up_grad = (hidden_grad * activated).astype(jnp.bfloat16)
    back = lax.dot_general(gate_grad, gate_slab, contract_cols, preferred_element_type=f32)
    back = back + lax.dot_general(up_grad, up_slab, contract_cols, preferred_element_type=f32)
    token_grad = lax.psum_scatter(
        back.astype(jnp.bfloat16), "expert", scatter_dimension=0, tiled=True
    )
    return layer_out, token_grad


def solution(mesh):
    rows = P(("groups", "expert"), None)
    slabs = P("expert", None, None)
    return jax.shard_map(
        on_device,
        mesh=mesh,
        in_specs=(rows, rows, rows, rows, slabs, slabs, slabs),
        out_specs=(rows, rows),
        check_vma=False,
    )
```

```python
import jax
import jax.numpy as jnp
from jax import lax
from jax.sharding import PartitionSpec as P

CORE, X, Y, Z = 1, 2, 4, 8
f32, bf16 = jnp.float32, jnp.bfloat16
CONTRACT_COLS = (((1,), (1,)), ((), ()))


def swap(value, offset):
    devices = lax.axis_size("expert")
    return lax.ppermute(value, "expert", [(i, i ^ offset) for i in range(devices)])


def far_offsets():
    return range(Z, lax.axis_size("expert"), Z)


def gather_half(block, first, second):
    held = jnp.concatenate([block] + [swap(block, offset) for offset in far_offsets()], axis=0)
    held = jnp.concatenate([held, swap(held, first)], axis=0)
    return jnp.concatenate([held, swap(held, second)], axis=0)


def scatter_half(sums, first, second):
    for offset in (second, first):
        half = sums.shape[0] // 2
        sums = (sums[:half].astype(f32) + swap(sums[half:], offset).astype(f32)).astype(bf16)
    blocks = lax.axis_size("expert") // Z
    rows = sums.shape[0] // blocks
    total = sums[:rows].astype(f32)
    for at, offset in enumerate(far_offsets()):
        total = total + swap(sums[(at + 1) * rows : (at + 2) * rows], offset).astype(f32)
    return total.astype(bf16)


def reorder(rows_yx):
    quarter = rows_yx.shape[0] // 4
    parts = [rows_yx[i * quarter : (i + 1) * quarter] for i in (0, 2, 1, 3)]
    return jnp.concatenate(parts, axis=0)


def code_rows(tokens, blocks):
    blocked = tokens.astype(f32).reshape(tokens.shape[0], blocks, 128)
    scale = lax.reduce_precision(jnp.max(jnp.abs(blocked), axis=2) + 1e-06, 8, 7)[:, :, None]
    quantized = lax.reduce_precision(blocked / scale, 8, 7)
    dequant = (quantized * scale).astype(bf16)
    return dequant.reshape(tokens.shape)


def gate_columns(expert_ids, gate_values, experts):
    named = expert_ids[:, :, None] == jnp.arange(experts, dtype=jnp.int32)[None, None, :]
    rest = jnp.sum(jnp.where(named, gate_values[:, :, None], 0.0), axis=1)
    pieces = []
    for _ in range(3):
        piece = lax.reduce_precision(rest, 8, 7)
        pieces.append(piece.astype(bf16))
        rest = rest - piece
    columns = jnp.concatenate(pieces, axis=1)
    return jnp.pad(columns, ((0, 0), (0, -columns.shape[1] % 128)))


def on_device(tokens, expert_ids, gate_values, cotangent, gate_weight, up_weight, down_weight):
    width = tokens.shape[1]
    cut = width // 256 * 128
    devices = lax.axis_size("expert")
    experts = devices // 2
    expert = lax.axis_index("expert") // 2
    gate_slab, up_slab, down_slab = gate_weight[0], up_weight[0], down_weight[0]
    dequant = code_rows(tokens, width // 128)
    columns = gate_columns(expert_ids, gate_values, experts)
    low = gather_half(jnp.concatenate([dequant[:, :cut], columns], axis=1), X, Y)
    high = gather_half(dequant[:, cut:], Y, X)
    slabs = [
        (gate_slab, up_slab, down_slab),
        (swap(gate_slab, CORE), swap(up_slab, CORE), swap(down_slab, CORE)),
    ]
    cot_low = gather_half(cotangent[:, :cut], X, Y)
    cot_high = gather_half(cotangent[:, cut:], Y, X)
    cots = jnp.concatenate([cot_low, reorder(cot_high)], axis=1)

    x = jnp.concatenate([low[:, :cut], reorder(high)], axis=1)
    pieces = low[:, cut : cut + 3 * experts].astype(f32).reshape(-1, 3, experts)
    mine = (jnp.arange(experts, dtype=jnp.int32) == expert).astype(f32)
    gate = jnp.sum(jnp.sum(pieces, axis=1) * mine, axis=1, keepdims=True)

    kept, partial = [], 0.0
    for gate_w, up_w, down_w in slabs:
        pre_gate = jnp.dot(x, gate_w, preferred_element_type=f32)
        pre_up = jnp.dot(x, up_w, preferred_element_type=f32)
        sigma = jax.nn.sigmoid(pre_gate)
        activated = pre_gate * sigma
        slope = sigma * (1.0 + pre_gate * (1.0 - sigma))
        kept.append((activated * gate, pre_up * slope * gate))
        hidden = (activated * pre_up).astype(bf16)
        partial = partial + jnp.dot(hidden, down_w, preferred_element_type=f32)
    out = (partial * gate).astype(bf16)
    layer_out = jnp.concatenate(
        [
            scatter_half(out[:, :cut], X, Y),
            scatter_half(reorder(out[:, cut:]), Y, X),
        ],
        axis=1,
    )

    back = 0.0
    for (gate_w, up_w, down_w), (for_up, for_gate) in zip(slabs, kept):
        hidden_grad = lax.dot_general(cots, down_w, CONTRACT_COLS, preferred_element_type=f32)
        gate_grad = (hidden_grad * for_gate).astype(bf16)
        up_grad = (hidden_grad * for_up).astype(bf16)
        back = back + lax.dot_general(gate_grad, gate_w, CONTRACT_COLS, preferred_element_type=f32)
        back = back + lax.dot_general(up_grad, up_w, CONTRACT_COLS, preferred_element_type=f32)
    back = back.astype(bf16)
    token_grad = jnp.concatenate(
        [
            scatter_half(back[:, :cut], X, Y),
            scatter_half(reorder(back[:, cut:]), Y, X),
        ],
        axis=1,
    )
    return layer_out, token_grad


def solution(mesh):
    rows = P(("groups", "expert"), None)
    slabs = P("expert", None, None)
    return jax.shard_map(
        on_device,
        mesh=mesh,
        in_specs=(rows, rows, rows, rows, slabs, slabs, slabs),
        out_specs=(rows, rows),
        check_vma=False,
    )
```

```python
import functools
import math

import jax
import jax.numpy as jnp
from jax import lax
from jax.experimental import pallas as pl
from jax.experimental.pallas import tpu as pltpu
from jax.sharding import PartitionSpec as P

CORE, PLANE, FAR = 1, (0, 2, 4, 6), 8
f32, bf16 = jnp.float32, jnp.bfloat16
CONTRACT_COLS = (((1,), (1,)), ((), ()))
LANES = 128
PIECES = 3
VMEM_LIMIT = 48 * 1024 * 1024


def swap(value, offset):
    devices = lax.axis_size("expert")
    return lax.ppermute(value, "expert", [(i, i ^ offset) for i in range(devices)])


def padded(count):
    return -(-count // LANES) * LANES


def column_chunks(width):
    step = 512 if width % 512 == 0 else LANES
    return [slice(at, at + step) for at in range(0, width, step)]


def call(body, outs, args, flops=0, scratch=(), grid=(), in_specs=None, out_specs=None):
    size = sum(math.prod(a.shape) * a.dtype.itemsize for a in (*args, *outs))
    whole = pl.BlockSpec(memory_space=pltpu.VMEM)
    return pl.pallas_call(
        body,
        out_shape=outs,
        grid=grid,
        in_specs=[whole] * len(args) if in_specs is None else in_specs,
        out_specs=[whole] * len(outs) if out_specs is None else out_specs,
        scratch_shapes=scratch,
        compiler_params=pltpu.CompilerParams(vmem_limit_bytes=VMEM_LIMIT),
        cost_estimate=pl.CostEstimate(flops=flops, bytes_accessed=size, transcendentals=0),
    )(*args)


def code_kernel(experts, tokens, ids, gates, out):
    rows, width = tokens.shape
    for at in range(0, width, LANES):
        block = tokens[:, at : at + LANES].astype(f32)
        scale = jnp.max(jnp.abs(block), axis=1, keepdims=True) + 1e-06
        scale = scale.astype(bf16).astype(f32)
        quantized = (block / scale).astype(bf16).astype(f32)
        out[:, at : at + LANES] = (quantized * scale).astype(bf16)
    lane = lax.broadcasted_iota(jnp.int32, (rows, out.shape[1] - width), 1)
    rest = jnp.zeros(lane.shape, f32)
    for k in range(ids.shape[1]):
        rest = jnp.where(ids[:, k : k + 1] == lane % experts, gates[:, k : k + 1], rest)
    columns = jnp.zeros(lane.shape, f32)
    for number in range(PIECES):
        piece = rest.astype(bf16).astype(f32)
        columns = jnp.where(lane // experts == number, piece, columns)
        rest = rest - piece
    out[:, width:] = columns.astype(bf16)


def pack_tokens_kernel(experts, capacity, chip, *refs):
    *blocks, first, second, third, fourth, by_row, by_slot = refs
    tok_dev = blocks[0].shape[0]
    rows, slots = by_row.shape
    width = first.shape[1]
    taken = slots_of(len(blocks), capacity)
    columns = jnp.concatenate([block[:, width:].astype(f32) for block in blocks], axis=0)
    lane = lax.broadcasted_iota(jnp.int32, columns.shape, 1)
    pick = lax.broadcasted_iota(jnp.int32, (rows, LANES), 1)
    gates, named = [], jnp.zeros((rows, LANES), f32)
    for number in range(len(PLANE)):
        mine = (lane % experts == (chip[0] ^ number)) & (lane < PIECES * experts)
        gates.append(jnp.sum(jnp.where(mine, columns, 0.0), axis=1, keepdims=True))
        named = jnp.where((pick == number) & (gates[-1] > 0.0), 1.0, named)
    row = lax.broadcasted_iota(jnp.int32, (rows, rows), 0)
    other = lax.broadcasted_iota(jnp.int32, (rows, rows), 1)
    earlier = (row // tok_dev == other // tok_dev) & (other < row)
    earlier = jnp.where(earlier, 1.0, 0.0).astype(bf16)
    counts = jnp.dot(earlier, named.astype(bf16), preferred_element_type=f32)
    slot = lax.broadcasted_iota(jnp.int32, (rows, slots), 1)
    start = lax.broadcasted_iota(jnp.int32, (rows, 1), 0) // tok_dev * capacity
    weights = jnp.zeros((rows, slots), f32)
    for number, gate in enumerate(gates):
        count = jnp.sum(jnp.where(pick == number, counts, 0.0), axis=1, keepdims=True)
        place = number * taken + start + count.astype(jnp.int32)
        weights = jnp.where(slot == place, gate, weights)
    by_row[...] = weights
    by_slot[...] = weights.T
    chosen = jnp.where(by_slot[...] > 0.0, 1.0, 0.0).astype(bf16)
    for part in column_chunks(width):
        held = jnp.concatenate([block[:, part] for block in blocks], axis=0)
        packed = jnp.dot(chosen, held, preferred_element_type=f32)
        for number, out in enumerate((first, second, third, fourth)):
            out[:, part] = packed[number * taken : (number + 1) * taken].astype(bf16)


def pack_cots_kernel(capacity, by_slot, *refs):
    *blocks, first, second, third, fourth = refs
    width = first.shape[1]
    taken = slots_of(len(blocks), capacity)
    gate = jnp.sum(by_slot[...], axis=1, keepdims=True)
    chosen = jnp.where(by_slot[...] > 0.0, 1.0, 0.0).astype(bf16)
    for part in column_chunks(width):
        held = jnp.concatenate([block[:, part] for block in blocks], axis=0)
        packed = gate * jnp.dot(chosen, held, preferred_element_type=f32)
        for number, out in enumerate((first, second, third, fourth)):
            out[:, part] = packed[number * taken : (number + 1) * taken].astype(bf16)


def slots_of(blocks, capacity):
    return blocks * capacity


def joined(refs, part, height):
    taken = [ref[:, part].astype(f32) for ref in refs]
    rest = height - sum(value.shape[0] for value in taken)
    if rest:
        taken.append(jnp.zeros((rest, taken[0].shape[1]), f32))
    return jnp.concatenate(taken, axis=0).astype(bf16)


def unpack_kernel(weighted, by_row, first, second, third, fourth, *outs):
    rows, slots = by_row.shape
    tok_dev = outs[0].shape[0]
    if weighted:
        matrices, rest = [], by_row[...]
        for _ in range(PIECES):
            matrices.append(rest.astype(bf16))
            rest = rest - matrices[-1].astype(f32)
    else:
        matrices = [jnp.where(by_row[...] > 0.0, 1.0, 0.0).astype(bf16)]
    for part in column_chunks(first.shape[1]):
        packed = joined((first, second, third, fourth), part, slots)
        total = jnp.dot(matrices[0], packed, preferred_element_type=f32)
        for matrix in matrices[1:]:
            total = total + jnp.dot(matrix, packed, preferred_element_type=f32)
        for number, out in enumerate(outs):
            out[:, part] = total[number * tok_dev : (number + 1) * tok_dev].astype(bf16)


def sum_kernel(*refs):
    *blocks, out = refs
    for part in column_chunks(out.shape[1]):
        total = blocks[0][:, part].astype(f32)
        for block in blocks[1:]:
            total = total + block[:, part].astype(f32)
        out[:, part] = total.astype(bf16)


def each_slab(step, steps, own, other, work):
    pl.when(step < steps)(functools.partial(work, *own))
    pl.when(step >= steps)(functools.partial(work, *other))


def forward_kernel(steps, x0, x1, x2, x3, g0, u0, d0, g1, u1, d1, *refs):
    o0, o1, o2, o3, for_up, for_gate, x, total = refs
    step = pl.program_id(0)
    rows = x.shape[0]

    @pl.when(step == 0)
    def _():
        for part in column_chunks(x.shape[1]):
            x[:, part] = joined((x0, x1, x2, x3), part, rows)
        total[...] = jnp.zeros_like(total)

    def work(gate_w, up_w, down_w):
        pre_gate = jnp.dot(x[...], gate_w[0], preferred_element_type=f32)
        pre_up = jnp.dot(x[...], up_w[0], preferred_element_type=f32)
        sigma = jax.nn.sigmoid(pre_gate)
        activated = pre_gate * sigma
        for_up[...] = activated
        for_gate[...] = pre_up * sigma * (1.0 + pre_gate * (1.0 - sigma))
        hidden = (activated * pre_up).astype(bf16)
        for part in column_chunks(x.shape[1]):
            total[:, part] += jnp.dot(hidden, down_w[0, :, part], preferred_element_type=f32)

    each_slab(step, steps, (g0, u0, d0), (g1, u1, d1), work)

    @pl.when(step == 2 * steps - 1)
    def _():
        store_packed(total, (o0, o1, o2, o3))


def store_packed(total, outs):
    taken = outs[0].shape[0]
    for number, out in enumerate(outs):
        for part in column_chunks(out.shape[1]):
            out[:, part] = total[number * taken : (number + 1) * taken, part].astype(bf16)


def backward_kernel(steps, x0, x1, x2, x3, for_up, for_gate, g0, u0, d0, g1, u1, d1, *refs):
    o0, o1, o2, o3, x, total = refs
    step = pl.program_id(0)
    rows = x.shape[0]

    @pl.when(step == 0)
    def _():
        for part in column_chunks(x.shape[1]):
            x[:, part] = joined((x0, x1, x2, x3), part, rows)
        total[...] = jnp.zeros_like(total)

    def work(gate_w, up_w, down_w):
        hidden_grad = lax.dot_general(x[...], down_w[0], CONTRACT_COLS, preferred_element_type=f32)
        gate_grad = (hidden_grad * for_gate[...]).astype(bf16)
        up_grad = (hidden_grad * for_up[...]).astype(bf16)
        for part in column_chunks(x.shape[1]):
            total[:, part] += lax.dot_general(
                gate_grad, gate_w[0, part], CONTRACT_COLS, preferred_element_type=f32
            ) + lax.dot_general(
                up_grad, up_w[0, part], CONTRACT_COLS, preferred_element_type=f32
            )

    each_slab(step, steps, (g0, u0, d0), (g1, u1, d1), work)

    @pl.when(step == 2 * steps - 1)
    def _():
        store_packed(total, (o0, o1, o2, o3))


def expert_specs(width, hidden, tile):
    steps = hidden // tile
    own = lambda i: jnp.minimum(i, steps - 1)
    other = lambda i: jnp.maximum(i - steps, 0)
    specs = []
    for place in (own, other):
        into = pl.BlockSpec((1, width, tile), lambda i, place=place: (0, 0, place(i)))
        back = pl.BlockSpec((1, tile, width), lambda i, place=place: (0, place(i), 0))
        specs += [into, into, back]
    return specs, steps


def on_device(tokens, expert_ids, gate_values, cotangent, gate_weight, up_weight, down_weight):
    tok_dev, top = expert_ids.shape
    width, hidden = gate_weight.shape[1:]
    devices = lax.axis_size("expert")
    experts = devices // 2
    capacity = min(tok_dev, tok_dev * top * 5 // (4 * experts))
    far = range(FAR, devices, FAR)
    blocks = devices // FAR
    taken = slots_of(blocks, capacity)
    rows, slots = blocks * tok_dev, padded(len(PLANE) * taken)
    chip = (lax.axis_index("expert") // 2).reshape(1).astype(jnp.int32)
    shape = jax.ShapeDtypeStruct
    packed_shapes = [shape((taken, width), bf16)] * len(PLANE)

    own = (gate_weight, up_weight, down_weight)
    other = tuple(swap(slab, CORE) for slab in own)

    (coded,) = call(
        functools.partial(code_kernel, experts),
        [shape((tok_dev, width + padded(PIECES * experts)), bf16)],
        (tokens, expert_ids, gate_values),
    )
    held = [coded] + [swap(coded, offset) for offset in far]
    cots = [cotangent] + [swap(cotangent, offset) for offset in far]

    whole = pl.BlockSpec(memory_space=pltpu.VMEM)
    *packed, by_row, by_slot = call(
        functools.partial(pack_tokens_kernel, experts, capacity),
        packed_shapes + [shape((rows, slots), f32), shape((slots, rows), f32)],
        (chip, *held),
        in_specs=[pl.BlockSpec(memory_space=pltpu.SMEM)] + [whole] * blocks,
        flops=2 * rows * slots * width,
    )
    x = [packed[0]] + [swap(value, offset) for value, offset in zip(packed[1:], PLANE[1:])]

    packed = call(
        functools.partial(pack_cots_kernel, capacity),
        packed_shapes,
        (by_slot, *cots),
        flops=2 * rows * slots * width,
    )
    grads = [packed[0]] + [swap(value, offset) for value, offset in zip(packed[1:], PLANE[1:])]

    all_taken = len(PLANE) * taken
    tile = 256
    weight_specs, steps = expert_specs(width, hidden, tile)
    kept_spec = pl.BlockSpec((all_taken, tile), lambda i: (0, i))
    kept_shapes = [shape((all_taken, 2 * hidden), f32)] * 2
    scratch = [pltpu.VMEM((all_taken, width), bf16), pltpu.VMEM((all_taken, width), f32)]
    flops = 2 * 3 * all_taken * width * 2 * hidden
    *outs, for_up, for_gate = call(
        functools.partial(forward_kernel, steps),
        packed_shapes + kept_shapes,
        (*x, *own, *other),
        flops=flops,
        grid=(2 * steps,),
        in_specs=[whole] * 4 + weight_specs,
        out_specs=[whole] * 4 + [kept_spec] * 2,
        scratch=scratch,
    )

    def go_home(values, weighted):
        back = [values[0]] + [swap(value, offset) for value, offset in zip(values[1:], PLANE[1:])]
        sums = call(
            functools.partial(unpack_kernel, weighted),
            [shape((tok_dev, width), bf16)] * blocks,
            (by_row, *back),
            flops=2 * rows * slots * width * (PIECES if weighted else 1),
        )
        home = [sums[0]] + [swap(value, offset) for value, offset in zip(sums[1:], far)]
        (result,) = call(sum_kernel, [shape((tok_dev, width), bf16)], home)
        return result

    layer_out = go_home(outs, True)
    backs = call(
        functools.partial(backward_kernel, steps),
        packed_shapes,
        (*grads, for_up, for_gate, *own, *other),
        flops=flops,
        grid=(2 * steps,),
        in_specs=[whole] * 4 + [kept_spec] * 2 + weight_specs,
        scratch=scratch,
    )
    token_grad = go_home(backs, False)
    return layer_out, token_grad


def solution(mesh):
    rows = P(("groups", "expert"), None)
    slabs = P("expert", None, None)
    return jax.shard_map(
        on_device,
        mesh=mesh,
        in_specs=(rows, rows, rows, rows, slabs, slabs, slabs),
        out_specs=(rows, rows),
        check_vma=False,
    )
```

```python
import functools
import math

import jax
import jax.numpy as jnp
from jax import lax
from jax.experimental import pallas as pl
from jax.experimental.pallas import tpu as pltpu
from jax.sharding import PartitionSpec as P

CORE, PLANE, FAR = 1, (0, 2, 4, 6), 8
f32, bf16 = jnp.float32, jnp.bfloat16
CONTRACT_COLS = (((1,), (1,)), ((), ()))
LANES = 128
PIECES = 3
VMEM_LIMIT = 16 * 1024 * 1024
VMEM_LIMIT_EXPERT = 48 * 1024 * 1024


def swap(value, offset):
    devices = lax.axis_size("expert")
    return lax.ppermute(value, "expert", [(i, i ^ offset) for i in range(devices)])


def gather_far(block):
    held, offset = {0: block}, lax.axis_size("expert") // 2
    while offset >= FAR:
        held.update({at ^ offset: swap(value, offset) for at, value in held.items()})
        offset //= 2
    return [held[at] for at in sorted(held)]


def padded(count):
    return -(-count // LANES) * LANES


def chunk_of(width):
    return 512 if width % 512 == 0 else LANES


def column_chunks(width):
    step = chunk_of(width)
    return [slice(at, at + step) for at in range(0, width, step)]


def call(body, outs, args, flops=0, scratch=(), in_specs=None, limit=VMEM_LIMIT):
    size = sum(math.prod(a.shape) * a.dtype.itemsize for a in (*args, *outs))
    whole = pl.BlockSpec(memory_space=pltpu.VMEM)
    return pl.pallas_call(
        body,
        out_shape=outs,
        in_specs=[whole] * len(args) if in_specs is None else in_specs,
        out_specs=[whole] * len(outs),
        scratch_shapes=scratch,
        compiler_params=pltpu.CompilerParams(vmem_limit_bytes=limit),
        cost_estimate=pl.CostEstimate(flops=flops, bytes_accessed=size, transcendentals=0),
    )(*args)


def code_kernel(experts, tokens, ids, gates, out):
    rows, width = tokens.shape
    for at in range(0, width, LANES):
        block = tokens[:, at : at + LANES].astype(f32)
        scale = jnp.max(jnp.abs(block), axis=1, keepdims=True) + 1e-06
        scale = scale.astype(bf16).astype(f32)
        quantized = (block / scale).astype(bf16).astype(f32)
        out[:, at : at + LANES] = (quantized * scale).astype(bf16)
    line = lax.broadcasted_iota(jnp.int32, (out.shape[1] - width, rows), 0)
    rest = jnp.zeros(line.shape, f32)
    for k in range(ids.shape[0]):
        rest = jnp.where(ids[k : k + 1] == line % experts, gates[k : k + 1], rest)
    columns = jnp.zeros(line.shape, f32)
    for number in range(PIECES):
        piece = rest.astype(bf16).astype(f32)
        columns = jnp.where(line // experts == number, piece, columns)
        rest = rest - piece
    out[:, width:] = columns.T.astype(bf16)


def pack_tokens_kernel(experts, capacity, chip, *refs):
    *blocks, first, second, third, fourth, by_row, by_slot = refs
    tok_dev = blocks[0].shape[0]
    rows, slots = by_row.shape
    width = first.shape[1]
    taken = slots_of(len(blocks), capacity)
    columns = jnp.concatenate([block[:, width:].astype(f32) for block in blocks], axis=0)
    lane = lax.broadcasted_iota(jnp.int32, columns.shape, 1)
    pick = lax.broadcasted_iota(jnp.int32, (rows, LANES), 1)
    gates, named = [], jnp.zeros((rows, LANES), f32)
    for number in range(len(PLANE)):
        mine = (lane % experts == (chip[0] ^ number)) & (lane < PIECES * experts)
        gates.append(jnp.sum(jnp.where(mine, columns, 0.0), axis=1, keepdims=True))
        named = jnp.where((pick == number) & (gates[-1] > 0.0), 1.0, named)
    row = lax.broadcasted_iota(jnp.int32, (rows, rows), 0)
    other = lax.broadcasted_iota(jnp.int32, (rows, rows), 1)
    earlier = (row // tok_dev == other // tok_dev) & (other < row)
    earlier = jnp.where(earlier, 1.0, 0.0).astype(bf16)
    counts = jnp.dot(earlier, named.astype(bf16), preferred_element_type=f32)
    slot = lax.broadcasted_iota(jnp.int32, (rows, slots), 1)
    start = lax.broadcasted_iota(jnp.int32, (rows, 1), 0) // tok_dev * capacity
    weights = jnp.zeros((rows, slots), f32)
    for number, gate in enumerate(gates):
        count = jnp.sum(jnp.where(pick == number, counts, 0.0), axis=1, keepdims=True)
        place = number * taken + start + count.astype(jnp.int32)
        weights = jnp.where(slot == place, gate, weights)
    by_row[...] = weights
    by_slot[...] = weights.T
    chosen = jnp.where(by_slot[...] > 0.0, 1.0, 0.0).astype(bf16)
    for part in column_chunks(width):
        held = jnp.concatenate([block[:, part] for block in blocks], axis=0)
        packed = jnp.dot(chosen, held, preferred_element_type=f32)
        for number, out in enumerate((first, second, third, fourth)):
            out[:, part] = packed[number * taken : (number + 1) * taken].astype(bf16)


def pack_cots_kernel(capacity, by_slot, *refs):
    *blocks, first, second, third, fourth = refs
    width = first.shape[1]
    taken = slots_of(len(blocks), capacity)
    gate = jnp.sum(by_slot[...], axis=1, keepdims=True)
    chosen = jnp.where(by_slot[...] > 0.0, 1.0, 0.0).astype(bf16)
    for part in column_chunks(width):
        held = jnp.concatenate([block[:, part] for block in blocks], axis=0)
        packed = gate * jnp.dot(chosen, held, preferred_element_type=f32)
        for number, out in enumerate((first, second, third, fourth)):
            out[:, part] = packed[number * taken : (number + 1) * taken].astype(bf16)


def slots_of(blocks, capacity):
    return blocks * capacity


def joined(refs, part, height, kind=bf16):
    taken = [ref[:, part].astype(f32) for ref in refs]
    rest = height - sum(value.shape[0] for value in taken)
    if rest:
        taken.append(jnp.zeros((rest, taken[0].shape[1]), f32))
    return jnp.concatenate(taken, axis=0).astype(kind)


def unpack_kernel(weighted, by_row, first, second, third, fourth, *outs):
    rows, slots = by_row.shape
    tok_dev = outs[0].shape[0]
    if weighted:
        matrices, rest = [], by_row[...]
        for _ in range(PIECES):
            matrices.append(rest.astype(bf16))
            rest = rest - matrices[-1].astype(f32)
    else:
        matrices = [jnp.where(by_row[...] > 0.0, 1.0, 0.0).astype(bf16)]
    for part in column_chunks(first.shape[1]):
        packed = joined((first, second, third, fourth), part, slots)
        total = jnp.dot(matrices[0], packed, preferred_element_type=f32)
        for matrix in matrices[1:]:
            total = total + jnp.dot(matrix, packed, preferred_element_type=f32)
        for number, out in enumerate(outs):
            out[:, part] = total[number * tok_dev : (number + 1) * tok_dev].astype(bf16)


def sum_kernel(*refs):
    *blocks, out = refs
    for part in column_chunks(out.shape[1]):
        total = blocks[0][:, part].astype(f32)
        for block in blocks[1:]:
            total = total + block[:, part].astype(f32)
        out[:, part] = total.astype(bf16)


def streams(pairs, sems):
    copies = [
        pltpu.make_async_copy(source, place, sems.at[number])
        for number, (source, place) in enumerate(pairs)
    ]
    for copy in copies:
        copy.start()
    return copies


def forward_kernel(tile, x0, x1, x2, x3, *refs):
    *slabs, o0, o1, o2, o3, for_up, for_gate, x, hidden, g0, u0, d0, g1, u1, d1, sems = refs
    places = (g0, u0, d0, g1, u1, d1)
    rows, width = x.shape
    units = g0.shape[2]
    step, chunk = min(tile, units), chunk_of(width)
    pairs, tiles = [], []
    for slab in (0, 3):
        for at in range(0, units, step):
            tiles.append((slab, at))
            for matrix in (slab, slab + 1):
                pairs.append([ref.at[0, :, pl.ds(at, step)] for ref in (slabs[matrix], places[matrix])])
    for at in range(0, width, chunk):
        for matrix in (2, 5):
            pairs.append([ref.at[0, :, pl.ds(at, chunk)] for ref in (slabs[matrix], places[matrix])])
    copies = iter(streams(pairs, sems))
    for part in column_chunks(width):
        x[:, part] = joined((x0, x1, x2, x3), part, rows)

    for slab, at in tiles:
        gate_w, up_w = places[slab : slab + 2]
        next(copies).wait()
        pre_gate = jnp.dot(x[...], gate_w[0, :, at : at + step], preferred_element_type=f32)
        next(copies).wait()
        pre_up = jnp.dot(x[...], up_w[0, :, at : at + step], preferred_element_type=f32)
        sigma = jax.nn.sigmoid(pre_gate)
        activated = pre_gate * sigma
        slope = pre_up * sigma * (1.0 + pre_gate * (1.0 - sigma))
        into = slice(slab // 3 * units + at, slab // 3 * units + at + step)
        hidden[:, into] = (activated * pre_up).astype(bf16)
        for_up[into] = activated.T
        for_gate[into] = slope.T

    for part in column_chunks(width):
        next(copies).wait()
        total = jnp.dot(hidden[:, :units], d0[0, :, part], preferred_element_type=f32)
        next(copies).wait()
        total = total + jnp.dot(hidden[:, units:], d1[0, :, part], preferred_element_type=f32)
        store_packed(total, (o0, o1, o2, o3), part)


def store_packed(total, outs, at):
    taken = outs[0].shape[0]
    for number, out in enumerate(outs):
        out[:, at] = total[number * taken : (number + 1) * taken].astype(bf16)


def backward_kernel(tile, x0, x1, x2, x3, for_up, for_gate, *refs):
    *slabs, o0, o1, o2, o3, x, gate_grad, up_grad, g0, u0, d0, g1, u1, d1, sems = refs
    places = (g0, u0, d0, g1, u1, d1)
    width, rows = x.shape
    units = g0.shape[2]
    step, chunk = min(tile, units), chunk_of(width)
    pairs, tiles = [], []
    for slab in (0, 3):
        for at in range(0, units, step):
            tiles.append((slab, at))
            pairs.append([ref.at[0, pl.ds(at, step)] for ref in (slabs[slab + 2], places[slab + 2])])
    for at in range(0, width, chunk):
        for matrix in (0, 1, 3, 4):
            pairs.append([ref.at[0, pl.ds(at, chunk)] for ref in (slabs[matrix], places[matrix])])
    copies = iter(streams(pairs, sems))
    for part in column_chunks(width):
        x[part] = joined((x0, x1, x2, x3), part, rows, f32).T.astype(bf16)

    for slab, at in tiles:
        next(copies).wait()
        into = slice(slab // 3 * units + at, slab // 3 * units + at + step)
        down_w = places[slab + 2]
        hidden_grad = jnp.dot(down_w[0, at : at + step], x[...], preferred_element_type=f32)
        gate_grad[into] = (hidden_grad * for_gate[into]).astype(bf16)
        up_grad[into] = (hidden_grad * for_up[into]).astype(bf16)

    own, other = slice(0, units), slice(units, 2 * units)
    for part in column_chunks(width):
        total = jnp.zeros((chunk, rows), f32)
        for matrix, grad in ((g0, gate_grad[own]), (u0, up_grad[own]), (g1, gate_grad[other]), (u1, up_grad[other])):
            next(copies).wait()
            total = total + jnp.dot(matrix[0, part], grad, preferred_element_type=f32)
        store_packed(total.T, (o0, o1, o2, o3), part)


def after(value, *others):
    return lax.optimization_barrier((value, *others))[0]


def on_device(tokens, expert_ids, gate_values, cotangent, gate_weight, up_weight, down_weight):
    tok_dev, top = expert_ids.shape
    width, hidden = gate_weight.shape[1:]
    devices = lax.axis_size("expert")
    experts = devices // 2
    capacity = min(tok_dev, tok_dev * top * 5 // (4 * experts))
    far = range(FAR, devices, FAR)
    blocks = devices // FAR
    taken = slots_of(blocks, capacity)
    rows, slots = blocks * tok_dev, padded(len(PLANE) * taken)
    chip = (lax.axis_index("expert") // 2).reshape(1).astype(jnp.int32)
    shape = jax.ShapeDtypeStruct
    packed_shapes = [shape((taken, width), bf16)] * len(PLANE)

    (coded,) = call(
        functools.partial(code_kernel, experts),
        [shape((tok_dev, width + padded(PIECES * experts)), bf16)],
        (tokens, expert_ids.T, gate_values.T),
    )
    held = gather_far(coded)
    gate_other, up_other = swap(gate_weight, CORE), swap(up_weight, CORE)

    whole = pl.BlockSpec(memory_space=pltpu.VMEM)
    *packed, by_row, by_slot = call(
        functools.partial(pack_tokens_kernel, experts, capacity),
        packed_shapes + [shape((rows, slots), f32), shape((slots, rows), f32)],
        (chip, *held),
        in_specs=[pl.BlockSpec(memory_space=pltpu.SMEM)] + [whole] * blocks,
        flops=2 * rows * slots * width,
    )
    x = [packed[0]] + [swap(value, offset) for value, offset in zip(packed[1:], PLANE[1:])]

    down_other = swap(after(down_weight, gate_other, up_other, packed[0]), CORE)
    own = (gate_weight, up_weight, down_weight)
    other = (gate_other, up_other, down_other)
    cots = gather_far(after(cotangent, held[len(held) // 2]))

    packed = call(
        functools.partial(pack_cots_kernel, capacity),
        packed_shapes,
        (by_slot, *cots),
        flops=2 * rows * slots * width,
    )
    grads = [packed[0]] + [swap(value, offset) for value, offset in zip(packed[1:], PLANE[1:])]

    all_taken = len(PLANE) * taken
    in_place = pl.BlockSpec(memory_space=pl.ANY)
    tile = 256 if hidden % 256 == 0 else LANES
    tiles, chunks = 2 * hidden // tile, width // chunk_of(width)
    slab_room = [pltpu.VMEM(slab.shape, bf16) for slab in (*own, *other)]
    flops = 2 * 3 * all_taken * width * 2 * hidden
    *outs, for_up, for_gate = call(
        functools.partial(forward_kernel, tile),
        packed_shapes + [shape((2 * hidden, all_taken), f32)] * 2,
        (*x, *own, *other),
        flops=flops,
        in_specs=[whole] * 4 + [in_place] * 6,
        limit=VMEM_LIMIT_EXPERT,
        scratch=[
            pltpu.VMEM((all_taken, width), bf16),
            pltpu.VMEM((all_taken, 2 * hidden), bf16),
            *slab_room,
            pltpu.SemaphoreType.DMA((2 * tiles + 2 * chunks,)),
        ],
    )

    def go_home(values, weighted):
        back = [values[0]] + [swap(value, offset) for value, offset in zip(values[1:], PLANE[1:])]
        sums = call(
            functools.partial(unpack_kernel, weighted),
            [shape((tok_dev, width), bf16)] * blocks,
            (by_row, *back),
            flops=2 * rows * slots * width * (PIECES if weighted else 1),
        )
        home = [sums[0]] + [swap(value, offset) for value, offset in zip(sums[1:], far)]
        (result,) = call(sum_kernel, [shape((tok_dev, width), bf16)], home)
        return result

    layer_out = go_home(outs, True)
    backs = call(
        functools.partial(backward_kernel, tile),
        packed_shapes,
        (*grads, for_up, for_gate, *own, *other),
        flops=flops,
        in_specs=[whole] * 6 + [in_place] * 6,
        limit=VMEM_LIMIT_EXPERT,
        scratch=[
            pltpu.VMEM((width, all_taken), bf16),
            *[pltpu.VMEM((2 * hidden, all_taken), bf16)] * 2,
            *slab_room,
            pltpu.SemaphoreType.DMA((tiles + 4 * chunks,)),
        ],
    )
    token_grad = go_home(backs, False)
    return layer_out, token_grad


def solution(mesh):
    rows = P(("groups", "expert"), None)
    slabs = P("expert", None, None)
    return jax.shard_map(
        on_device,
        mesh=mesh,
        in_specs=(rows, rows, rows, rows, slabs, slabs, slabs),
        out_specs=(rows, rows),
        check_vma=False,
    )
```

```python
import functools
import math

import jax
import jax.numpy as jnp
from jax import lax
from jax.experimental import pallas as pl
from jax.experimental.pallas import tpu as pltpu
from jax.sharding import PartitionSpec as P

CORE, PLANE, FAR = 1, (0, 2, 4, 6), 8
f32, bf16 = jnp.float32, jnp.bfloat16
CONTRACT_COLS = (((1,), (1,)), ((), ()))
LANES = 128
PIECES = 3
VMEM_LIMIT = 16 * 1024 * 1024
VMEM_LIMIT_EXPERT = 48 * 1024 * 1024


def swap(value, offset):
    devices = lax.axis_size("expert")
    return lax.ppermute(value, "expert", [(i, i ^ offset) for i in range(devices)])


def after(value, *others):
    return lax.optimization_barrier((value, *others))[0]


def double(held, offset, wait):
    ready = {at: after(value, wait) for at, value in held.items()}
    return held | {at ^ offset: swap(value, offset) for at, value in ready.items()}


def padded(count):
    return -(-count // LANES) * LANES


def chunk_of(width):
    return 512 if width % 512 == 0 else LANES


def column_chunks(width):
    step = chunk_of(width)
    return [slice(at, at + step) for at in range(0, width, step)]


def call(body, outs, args, flops=0, scratch=(), in_specs=None, limit=VMEM_LIMIT):
    size = sum(math.prod(a.shape) * a.dtype.itemsize for a in (*args, *outs))
    whole = pl.BlockSpec(memory_space=pltpu.VMEM)
    return pl.pallas_call(
        body,
        out_shape=outs,
        in_specs=[whole] * len(args) if in_specs is None else in_specs,
        out_specs=[whole] * len(outs),
        scratch_shapes=scratch,
        compiler_params=pltpu.CompilerParams(vmem_limit_bytes=limit),
        cost_estimate=pl.CostEstimate(flops=flops, bytes_accessed=size, transcendentals=0),
    )(*args)


def code_kernel(experts, tokens, ids, gates, out):
    rows, width = tokens.shape
    for at in range(0, width, LANES):
        block = tokens[:, at : at + LANES].astype(f32)
        scale = jnp.max(jnp.abs(block), axis=1, keepdims=True) + 1e-06
        scale = scale.astype(bf16).astype(f32)
        quantized = (block / scale).astype(bf16).astype(f32)
        out[:, at : at + LANES] = (quantized * scale).astype(bf16)
    line = lax.broadcasted_iota(jnp.int32, (out.shape[1] - width, rows), 0)
    rest = jnp.zeros(line.shape, f32)
    for k in range(ids.shape[0]):
        rest = jnp.where(ids[k : k + 1] == line % experts, gates[k : k + 1], rest)
    columns = jnp.zeros(line.shape, f32)
    for number in range(PIECES):
        piece = rest.astype(bf16).astype(f32)
        columns = jnp.where(line // experts == number, piece, columns)
        rest = rest - piece
    out[:, width:] = columns.T.astype(bf16)


def pack_tokens_kernel(experts, capacity, chip, *refs):
    *blocks, first, second, third, fourth, by_row, by_slot = refs
    tok_dev = blocks[0].shape[0]
    rows, slots = by_row.shape
    width = first.shape[1]
    taken = slots_of(len(blocks), capacity)
    columns = jnp.concatenate([block[:, width:].astype(f32) for block in blocks], axis=0)
    lane = lax.broadcasted_iota(jnp.int32, columns.shape, 1)
    pick = lax.broadcasted_iota(jnp.int32, (rows, LANES), 1)
    gates, named = [], jnp.zeros((rows, LANES), f32)
    for number in range(len(PLANE)):
        mine = (lane % experts == (chip[0] ^ number)) & (lane < PIECES * experts)
        gates.append(jnp.sum(jnp.where(mine, columns, 0.0), axis=1, keepdims=True))
        named = jnp.where((pick == number) & (gates[-1] > 0.0), 1.0, named)
    row = lax.broadcasted_iota(jnp.int32, (rows, rows), 0)
    other = lax.broadcasted_iota(jnp.int32, (rows, rows), 1)
    earlier = (row // tok_dev == other // tok_dev) & (other < row)
    earlier = jnp.where(earlier, 1.0, 0.0).astype(bf16)
    counts = jnp.dot(earlier, named.astype(bf16), preferred_element_type=f32)
    slot = lax.broadcasted_iota(jnp.int32, (rows, slots), 1)
    start = lax.broadcasted_iota(jnp.int32, (rows, 1), 0) // tok_dev * capacity
    weights = jnp.zeros((rows, slots), f32)
    for number, gate in enumerate(gates):
        count = jnp.sum(jnp.where(pick == number, counts, 0.0), axis=1, keepdims=True)
        place = number * taken + start + count.astype(jnp.int32)
        weights = jnp.where(slot == place, gate, weights)
    by_row[...] = weights
    by_slot[...] = weights.T
    chosen = jnp.where(by_slot[...] > 0.0, 1.0, 0.0).astype(bf16)
    for part in column_chunks(width):
        held = jnp.concatenate([block[:, part] for block in blocks], axis=0)
        packed = jnp.dot(chosen, held, preferred_element_type=f32)
        for number, out in enumerate((first, second, third, fourth)):
            out[:, part] = packed[number * taken : (number + 1) * taken].astype(bf16)


def pack_cots_kernel(capacity, by_slot, *refs):
    *blocks, first, second, third, fourth = refs
    width = first.shape[1]
    taken = slots_of(len(blocks), capacity)
    gate = jnp.sum(by_slot[...], axis=1, keepdims=True)
    chosen = jnp.where(by_slot[...] > 0.0, 1.0, 0.0).astype(bf16)
    for part in column_chunks(width):
        held = jnp.concatenate([block[:, part] for block in blocks], axis=0)
        packed = gate * jnp.dot(chosen, held, preferred_element_type=f32)
        for number, out in enumerate((first, second, third, fourth)):
            out[:, part] = packed[number * taken : (number + 1) * taken].astype(bf16)


def slots_of(blocks, capacity):
    return blocks * capacity


def joined(refs, part, height, kind=bf16):
    taken = [ref[:, part].astype(f32) for ref in refs]
    rest = height - sum(value.shape[0] for value in taken)
    if rest:
        taken.append(jnp.zeros((rest, taken[0].shape[1]), f32))
    return jnp.concatenate(taken, axis=0).astype(kind)


def unpack_kernel(weighted, by_row, first, second, third, fourth, *outs):
    rows, slots = by_row.shape
    tok_dev = outs[0].shape[0]
    if weighted:
        matrices, rest = [], by_row[...]
        for _ in range(PIECES):
            matrices.append(rest.astype(bf16))
            rest = rest - matrices[-1].astype(f32)
    else:
        matrices = [jnp.where(by_row[...] > 0.0, 1.0, 0.0).astype(bf16)]
    for part in column_chunks(first.shape[1]):
        packed = joined((first, second, third, fourth), part, slots)
        total = jnp.dot(matrices[0], packed, preferred_element_type=f32)
        for matrix in matrices[1:]:
            total = total + jnp.dot(matrix, packed, preferred_element_type=f32)
        for number, out in enumerate(outs):
            out[:, part] = total[number * tok_dev : (number + 1) * tok_dev].astype(bf16)


def sum_kernel(*refs):
    *blocks, out = refs
    for part in column_chunks(out.shape[1]):
        total = blocks[0][:, part].astype(f32)
        for block in blocks[1:]:
            total = total + block[:, part].astype(f32)
        out[:, part] = total.astype(bf16)


def streams(pairs, sems):
    copies = [
        pltpu.make_async_copy(source, place, sems.at[number])
        for number, (source, place) in enumerate(pairs)
    ]
    for copy in copies:
        copy.start()
    return copies


def forward_kernel(tile, x0, x1, x2, x3, *refs):
    *slabs, o0, o1, o2, o3, for_up, for_gate, x, hidden, into, back, sems = refs
    rows, width = x.shape
    units = back.shape[0] // 2
    chunk, tiles = chunk_of(width), 2 * units // tile
    pairs = []
    for number in range(tiles):
        slab, at = divmod(number * tile, units)
        for half, source in enumerate(slabs[3 * slab : 3 * slab + 2]):
            place = into.at[:, pl.ds((2 * number + half) * tile, tile)]
            pairs.append((source.at[0, :, pl.ds(at, tile)], place))
    for at in range(0, width, chunk):
        for slab in range(2):
            place = back.at[pl.ds(slab * units, units), pl.ds(at, chunk)]
            pairs.append((slabs[3 * slab + 2].at[0, :, pl.ds(at, chunk)], place))
    copies = iter(streams(pairs, sems))
    for part in column_chunks(width):
        x[:, part] = joined((x0, x1, x2, x3), part, rows)

    for number in range(tiles):
        next(copies).wait()
        next(copies).wait()
        columns = slice(2 * number * tile, 2 * (number + 1) * tile)
        pre = jnp.dot(x[...], into[:, columns], preferred_element_type=f32)
        pre_gate, pre_up = pre[:, :tile], pre[:, tile:]
        sigma = jax.nn.sigmoid(pre_gate)
        activated = pre_gate * sigma
        at = slice(number * tile, (number + 1) * tile)
        hidden[:, at] = (activated * pre_up).astype(bf16)
        for_up[:, at] = activated
        for_gate[:, at] = pre_up * sigma * (1.0 + pre_gate * (1.0 - sigma))

    for part in column_chunks(width):
        next(copies).wait()
        next(copies).wait()
        total = jnp.dot(hidden[...], back[:, part], preferred_element_type=f32)
        store_packed(total, (o0, o1, o2, o3), part)


def store_packed(total, outs, at):
    taken = outs[0].shape[0]
    for number, out in enumerate(outs):
        out[:, at] = total[number * taken : (number + 1) * taken].astype(bf16)


def backward_kernel(x0, x1, x2, x3, for_up, for_gate, *refs):
    *slabs, o0, o1, o2, o3, x, grads, into, back, sems = refs
    rows, width = x.shape
    units = back.shape[0] // 2
    chunk = chunk_of(width)
    pairs = []
    for slab in range(2):
        pairs.append((slabs[3 * slab + 2].at[0], back.at[pl.ds(slab * units, units)]))
    for at in range(0, width, chunk):
        for number, matrix in enumerate((0, 1, 3, 4)):
            place = into.at[pl.ds(at, chunk), pl.ds(number * units, units)]
            pairs.append((slabs[matrix].at[0, pl.ds(at, chunk)], place))
    copies = iter(streams(pairs, sems))
    for part in column_chunks(width):
        x[:, part] = joined((x0, x1, x2, x3), part, rows)

    for slab in range(2):
        next(copies).wait()
        at = slice(slab * units, (slab + 1) * units)
        hidden_grad = lax.dot_general(x[...], back[at], CONTRACT_COLS, preferred_element_type=f32)
        start = 2 * slab * units
        grads[:, start : start + units] = (hidden_grad * for_gate[:, at]).astype(bf16)
        grads[:, start + units : start + 2 * units] = (hidden_grad * for_up[:, at]).astype(bf16)

    for part in column_chunks(width):
        for _ in range(4):
            next(copies).wait()
        total = lax.dot_general(
            grads[...], into[part], CONTRACT_COLS, preferred_element_type=f32
        )
        store_packed(total, (o0, o1, o2, o3), part)


def on_device(tokens, expert_ids, gate_values, cotangent, gate_weight, up_weight, down_weight):
    tok_dev, top = expert_ids.shape
    width, hidden = gate_weight.shape[1:]
    devices = lax.axis_size("expert")
    experts = devices // 2
    capacity = min(tok_dev, tok_dev * top * 5 // (4 * experts))
    far = range(FAR, devices, FAR)
    blocks = devices // FAR
    taken = slots_of(blocks, capacity)
    rows, slots = blocks * tok_dev, padded(len(PLANE) * taken)
    chip = (lax.axis_index("expert") // 2).reshape(1).astype(jnp.int32)
    shape = jax.ShapeDtypeStruct
    packed_shapes = [shape((taken, width), bf16)] * len(PLANE)

    (coded,) = call(
        functools.partial(code_kernel, experts),
        [shape((tok_dev, width + padded(PIECES * experts)), bf16)],
        (tokens, expert_ids.T, gate_values.T),
    )
    held, cots = {0: coded}, {0: cotangent}
    offset = devices // 2
    while offset > FAR:
        cots = double(cots, offset, cotangent)
        held = double(held, offset, coded)
        offset //= 2
    held = double(held, FAR, cots[max(cots)])
    held = [held[at] for at in sorted(held)]
    gate_other, up_other = swap(gate_weight, CORE), swap(up_weight, CORE)

    whole = pl.BlockSpec(memory_space=pltpu.VMEM)
    *packed, by_row, by_slot = call(
        functools.partial(pack_tokens_kernel, experts, capacity),
        packed_shapes + [shape((rows, slots), f32), shape((slots, rows), f32)],
        (chip, *held),
        in_specs=[pl.BlockSpec(memory_space=pltpu.SMEM)] + [whole] * blocks,
        flops=2 * rows * slots * width,
    )
    x = [packed[0]] + [swap(value, offset) for value, offset in zip(packed[1:], PLANE[1:])]

    down_other = swap(after(down_weight, gate_other, up_other, packed[0]), CORE)
    own = (gate_weight, up_weight, down_weight)
    other = (gate_other, up_other, down_other)
    cots = double(cots, FAR, packed[0])
    cots = [cots[at] for at in sorted(cots)]

    packed = call(
        functools.partial(pack_cots_kernel, capacity),
        packed_shapes,
        (by_slot, *cots),
        flops=2 * rows * slots * width,
    )
    grads = [packed[0]] + [swap(value, offset) for value, offset in zip(packed[1:], PLANE[1:])]

    all_taken = len(PLANE) * taken
    in_place = pl.BlockSpec(memory_space=pl.ANY)
    tile = 256 if hidden % 256 == 0 else LANES
    tiles, chunks = 2 * hidden // tile, width // chunk_of(width)
    slab_room = [pltpu.VMEM((width, 4 * hidden), bf16), pltpu.VMEM((2 * hidden, width), bf16)]
    flops = 2 * 3 * all_taken * width * 2 * hidden
    *outs, for_up, for_gate = call(
        functools.partial(forward_kernel, tile),
        packed_shapes + [shape((all_taken, 2 * hidden), f32)] * 2,
        (*x, *own, *other),
        flops=flops,
        in_specs=[whole] * 4 + [in_place] * 6,
        limit=VMEM_LIMIT_EXPERT,
        scratch=[
            pltpu.VMEM((all_taken, width), bf16),
            pltpu.VMEM((all_taken, 2 * hidden), bf16),
            *slab_room,
            pltpu.SemaphoreType.DMA((2 * tiles + 2 * chunks,)),
        ],
    )

    def go_home(values, weighted):
        back = [values[0]] + [swap(value, offset) for value, offset in zip(values[1:], PLANE[1:])]
        sums = call(
            functools.partial(unpack_kernel, weighted),
            [shape((tok_dev, width), bf16)] * blocks,
            (by_row, *back),
            flops=2 * rows * slots * width * (PIECES if weighted else 1),
        )
        home = [sums[0]] + [swap(value, offset) for value, offset in zip(sums[1:], far)]
        (result,) = call(sum_kernel, [shape((tok_dev, width), bf16)], home)
        return result

    layer_out = go_home(outs, True)
    backs = call(
        backward_kernel,
        packed_shapes,
        (*grads, for_up, for_gate, *own, *other),
        flops=flops,
        in_specs=[whole] * 6 + [in_place] * 6,
        limit=VMEM_LIMIT_EXPERT,
        scratch=[
            pltpu.VMEM((all_taken, width), bf16),
            pltpu.VMEM((all_taken, 4 * hidden), bf16),
            *slab_room,
            pltpu.SemaphoreType.DMA((2 + 4 * chunks,)),
        ],
    )
    token_grad = go_home(backs, False)
    return layer_out, token_grad


def solution(mesh):
    rows = P(("groups", "expert"), None)
    slabs = P("expert", None, None)
    return jax.shard_map(
        on_device,
        mesh=mesh,
        in_specs=(rows, rows, rows, rows, slabs, slabs, slabs),
        out_specs=(rows, rows),
        check_vma=False,
    )
```

```python
import functools
import math

import jax
import jax.numpy as jnp
from jax import lax
from jax.experimental import pallas as pl
from jax.experimental.pallas import tpu as pltpu
from jax.sharding import PartitionSpec as P

CORE, PLANE, FAR = 1, (0, 2, 4, 6), 8
f32, bf16 = jnp.float32, jnp.bfloat16
CONTRACT_COLS = (((1,), (1,)), ((), ()))
LANES = 128
PIECES = 3
CHUNK = 512
VMEM_LIMIT = 16 * 1024 * 1024
VMEM_LIMIT_EXPERT = 48 * 1024 * 1024
VMEM_LIMIT_ALL = 58 * 1024 * 1024


def after(value, *others):
    return lax.optimization_barrier((value, *others))[0]


def swap(value, offset):
    devices = lax.axis_size("expert")
    return lax.ppermute(value, "expert", [(i, i ^ offset) for i in range(devices)])


def padded(count):
    return -(-count // LANES) * LANES


def column_chunks(width):
    return [slice(at, min(at + CHUNK, width)) for at in range(0, width, CHUNK)]


def call(body, outs, args, flops=0, scratch=(), in_specs=None, limit=VMEM_LIMIT):
    size = sum(math.prod(a.shape) * a.dtype.itemsize for a in (*args, *outs))
    whole = pl.BlockSpec(memory_space=pltpu.VMEM)
    return pl.pallas_call(
        body,
        out_shape=outs,
        in_specs=[whole] * len(args) if in_specs is None else in_specs,
        out_specs=[whole] * len(outs),
        scratch_shapes=scratch,
        compiler_params=pltpu.CompilerParams(vmem_limit_bytes=limit),
        cost_estimate=pl.CostEstimate(flops=flops, bytes_accessed=size, transcendentals=0),
    )(*args)


def streams(pairs, sems):
    copies = [
        pltpu.make_async_copy(source, place, sems.at[number])
        for number, (source, place) in enumerate(pairs)
    ]
    for copy in copies:
        copy.start()
    return copies


def code_kernel(experts, tokens_in, ids_in, gates_in, cots_in, out, tokens, ids, gates, sems):
    rows, width = tokens.shape
    copies = streams(((ids_in, ids), (gates_in, gates), (tokens_in, tokens)), sems)
    gate_width = out.shape[1] - 2 * width
    place = out.at[:, pl.ds(width + gate_width, width)]
    cots_copy = pltpu.make_async_copy(cots_in, place, sems.at[len(copies)])
    cots_copy.start()
    copies[0].wait()
    copies[1].wait()
    line = lax.broadcasted_iota(jnp.int32, (gate_width, rows), 0)
    rest = jnp.zeros(line.shape, f32)
    for k in range(ids.shape[0]):
        rest = jnp.where(ids[k : k + 1] == line % experts, gates[k : k + 1], rest)
    columns = jnp.zeros(line.shape, f32)
    for number in range(PIECES):
        piece = rest.astype(bf16).astype(f32)
        columns = jnp.where(line // experts == number, piece, columns)
        rest = rest - piece
    out[:, width : width + gate_width] = columns.T.astype(bf16)
    copies[2].wait()
    for at in range(0, width, LANES):
        block = tokens[:, at : at + LANES].astype(f32)
        scale = jnp.max(jnp.abs(block), axis=1, keepdims=True) + 1e-06
        scale = scale.astype(bf16).astype(f32)
        quantized = (block / scale).astype(bf16).astype(f32)
        out[:, at : at + LANES] = (quantized * scale).astype(bf16)
    cots_copy.wait()


def pack_tokens_kernel(experts, capacity, chip, *refs):
    *blocks, first, second, third, fourth, by_row, by_slot = refs
    tok_dev = blocks[0].shape[0]
    rows, slots = by_row.shape
    width = first.shape[1]
    taken = slots_of(len(blocks), capacity)
    gate_columns = slice(width, blocks[0].shape[1] - width)
    columns = jnp.concatenate([block[:, gate_columns].astype(f32) for block in blocks], axis=0)
    lane = lax.broadcasted_iota(jnp.int32, columns.shape, 1)
    pick = lax.broadcasted_iota(jnp.int32, (rows, LANES), 1)
    gates, named = [], jnp.zeros((rows, LANES), f32)
    for number in range(len(PLANE)):
        mine = (lane % experts == (chip[0] ^ number)) & (lane < PIECES * experts)
        gates.append(jnp.sum(jnp.where(mine, columns, 0.0), axis=1, keepdims=True))
        named = jnp.where((pick == number) & (gates[-1] > 0.0), 1.0, named)
    row = lax.broadcasted_iota(jnp.int32, (rows, rows), 0)
    other = lax.broadcasted_iota(jnp.int32, (rows, rows), 1)
    earlier = (row // tok_dev == other // tok_dev) & (other < row)
    earlier = jnp.where(earlier, 1.0, 0.0).astype(bf16)
    counts = jnp.dot(earlier, named.astype(bf16), preferred_element_type=f32)
    slot = lax.broadcasted_iota(jnp.int32, (rows, slots), 1)
    start = lax.broadcasted_iota(jnp.int32, (rows, 1), 0) // tok_dev * capacity
    weights = jnp.zeros((rows, slots), f32)
    for number, gate in enumerate(gates):
        count = jnp.sum(jnp.where(pick == number, counts, 0.0), axis=1, keepdims=True)
        place = number * taken + start + count.astype(jnp.int32)
        weights = jnp.where(slot == place, gate, weights)
    by_row[...] = weights
    by_slot[...] = weights.T
    chosen = jnp.where(by_slot[...] > 0.0, 1.0, 0.0).astype(bf16)
    for part in column_chunks(width):
        held = jnp.concatenate([block[:, part] for block in blocks], axis=0)
        packed = jnp.dot(chosen, held, preferred_element_type=f32)
        for number, out in enumerate((first, second, third, fourth)):
            out[:, part] = packed[number * taken : (number + 1) * taken].astype(bf16)


def pack_cots_kernel(capacity, by_slot, *refs):
    *blocks, first, second, third, fourth = refs
    width = first.shape[1]
    taken = slots_of(len(blocks), capacity)
    gate = jnp.sum(by_slot[...], axis=1, keepdims=True)
    chosen = jnp.where(by_slot[...] > 0.0, 1.0, 0.0).astype(bf16)
    first_column = blocks[0].shape[1] - width
    for part in column_chunks(width):
        source = slice(first_column + part.start, first_column + part.stop)
        held = jnp.concatenate([block[:, source] for block in blocks], axis=0)
        packed = gate * jnp.dot(chosen, held, preferred_element_type=f32)
        for number, out in enumerate((first, second, third, fourth)):
            out[:, part] = packed[number * taken : (number + 1) * taken].astype(bf16)


def slots_of(blocks, capacity):
    return blocks * capacity


def joined(refs, part, height, kind=bf16):
    taken = [ref[:, part].astype(f32) for ref in refs]
    rest = height - sum(value.shape[0] for value in taken)
    if rest:
        taken.append(jnp.zeros((rest, taken[0].shape[1]), f32))
    return jnp.concatenate(taken, axis=0).astype(kind)


def unpack_kernel(weighted, by_row, first, second, third, fourth, *outs):
    rows, slots = by_row.shape
    tok_dev = outs[0].shape[0]
    if weighted:
        matrices, rest = [], by_row[...]
        for _ in range(PIECES):
            matrices.append(rest.astype(bf16))
            rest = rest - matrices[-1].astype(f32)
    else:
        matrices = [jnp.where(by_row[...] > 0.0, 1.0, 0.0).astype(bf16)]
    for part in column_chunks(first.shape[1]):
        packed = joined((first, second, third, fourth), part, slots)
        total = jnp.dot(matrices[0], packed, preferred_element_type=f32)
        for matrix in matrices[1:]:
            total = total + jnp.dot(matrix, packed, preferred_element_type=f32)
        for number, out in enumerate(outs):
            out[:, part] = total[number * tok_dev : (number + 1) * tok_dev].astype(bf16)


def sum_kernel(count, *refs):
    *blocks, out = refs
    start = 0
    for at in range(0, len(blocks), count):
        columns = blocks[at].shape[1]
        for part in column_chunks(columns):
            total = blocks[at][:, part].astype(f32)
            for block in blocks[at + 1 : at + count]:
                total = total + block[:, part].astype(f32)
            out[:, start + part.start : start + part.stop] = total.astype(bf16)
        start += columns


def forward_kernel(tile, x0, x1, x2, x3, *refs):
    *slabs, o0, o1, o2, o3, for_up, for_gate, x, hidden, into, back, sems = refs
    rows, width = x.shape
    units = back.shape[0] // 2
    tiles = 2 * units // tile
    pairs = []
    for number in range(tiles):
        slab, at = divmod(number * tile, units)
        for half, source in enumerate(slabs[3 * slab : 3 * slab + 2]):
            place = into.at[:, pl.ds((2 * number + half) * tile, tile)]
            pairs.append((source.at[0, :, pl.ds(at, tile)], place))
    for part in column_chunks(width):
        columns = pl.ds(part.start, part.stop - part.start)
        for slab in range(2):
            place = back.at[pl.ds(slab * units, units), columns]
            pairs.append((slabs[3 * slab + 2].at[0, :, columns], place))
    copies = iter(streams(pairs, sems))
    for part in column_chunks(width):
        x[:, part] = joined((x0, x1, x2, x3), part, rows)

    for number in range(tiles):
        next(copies).wait()
        next(copies).wait()
        columns = slice(2 * number * tile, 2 * (number + 1) * tile)
        pre = jnp.dot(x[...], into[:, columns], preferred_element_type=f32)
        pre_gate, pre_up = pre[:, :tile], pre[:, tile:]
        sigma = jax.nn.sigmoid(pre_gate)
        activated = pre_gate * sigma
        at = slice(number * tile, (number + 1) * tile)
        hidden[:, at] = (activated * pre_up).astype(bf16)
        for_up[:, at] = activated
        for_gate[:, at] = pre_up * sigma * (1.0 + pre_gate * (1.0 - sigma))

    for part in column_chunks(width):
        next(copies).wait()
        next(copies).wait()
        total = jnp.dot(hidden[...], back[:, part], preferred_element_type=f32)
        store_packed(total, (o0, o1, o2, o3), part)


def store_packed(total, outs, at):
    taken = outs[0].shape[0]
    for number, out in enumerate(outs):
        out[:, at] = total[number * taken : (number + 1) * taken].astype(bf16)


def into_pairs(slabs, into, first):
    pairs, units = [], into.shape[1] // len(slabs)
    for part in column_chunks(into.shape[0]):
        height = part.stop - part.start
        for number, source in enumerate(slabs):
            place = into.at[pl.ds(part.start, height), pl.ds(number * units, units)]
            pairs.append((source.at[0, pl.ds(first + part.start, height)], place))
    return pairs


def project_back(copies, matrices, grads, into, outs):
    for part in column_chunks(into.shape[0]):
        for _ in range(matrices):
            next(copies).wait()
        total = lax.dot_general(
            grads[...], into[part], CONTRACT_COLS, preferred_element_type=f32
        )
        store_packed(total, outs, part)


def backward_kernel(x0, x1, x2, x3, for_up, for_gate, *refs):
    *slabs, o0, o1, o2, o3, grads, x, into, back, sems = refs
    rows, width = x.shape
    units = back.shape[0] // 2
    into_slabs = (*slabs[:2], *slabs[3:5])
    pairs = []
    for slab in range(2):
        pairs.append((slabs[3 * slab + 2].at[0], back.at[pl.ds(slab * units, units)]))
    copies = iter(streams(pairs + into_pairs(into_slabs, into, 0), sems))
    for part in column_chunks(width):
        x[:, part] = joined((x0, x1, x2, x3), part, rows)

    for slab in range(2):
        next(copies).wait()
        at = slice(slab * units, (slab + 1) * units)
        hidden_grad = lax.dot_general(x[...], back[at], CONTRACT_COLS, preferred_element_type=f32)
        start = 2 * slab * units
        grads[:, start : start + units] = (hidden_grad * for_gate[:, at]).astype(bf16)
        grads[:, start + units : start + 2 * units] = (hidden_grad * for_up[:, at]).astype(bf16)

    project_back(copies, len(into_slabs), grads, into, (o0, o1, o2, o3))


def backward_rest_kernel(first, grads, *refs):
    *slabs, o0, o1, o2, o3, into, sems = refs
    copies = iter(streams(into_pairs(slabs, into, first), sems))
    project_back(copies, len(slabs), grads, into, (o0, o1, o2, o3))


def on_device(tokens, expert_ids, gate_values, cotangent, gate_weight, up_weight, down_weight):
    tok_dev, top = expert_ids.shape
    width, hidden = gate_weight.shape[1:]
    devices = lax.axis_size("expert")
    experts = devices // 2
    capacity = min(tok_dev, tok_dev * top * 5 // (4 * experts))
    far = range(FAR, devices, FAR)
    blocks = devices // FAR
    taken = slots_of(blocks, capacity)
    rows, slots = blocks * tok_dev, padded(len(PLANE) * taken)
    chip = (lax.axis_index("expert") // 2).reshape(1).astype(jnp.int32)
    shape = jax.ShapeDtypeStruct
    packed_shapes = [shape((taken, width), bf16)] * len(PLANE)

    own = (gate_weight, up_weight, down_weight)
    other = tuple(swap(slab, CORE) for slab in own)

    in_place = pl.BlockSpec(memory_space=pl.ANY)
    (coded,) = call(
        functools.partial(code_kernel, experts),
        [shape((tok_dev, 2 * width + padded(PIECES * experts)), bf16)],
        (tokens, expert_ids.T, gate_values.T, cotangent),
        in_specs=[in_place] * 4,
        scratch=[
            pltpu.VMEM((tok_dev, width), bf16),
            pltpu.VMEM((top, tok_dev), jnp.int32),
            pltpu.VMEM((top, tok_dev), f32),
            pltpu.SemaphoreType.DMA((4,)),
        ],
        limit=VMEM_LIMIT_ALL,
    )
    held, offset = {0: coded}, devices // 2
    while offset >= FAR:
        held.update({at ^ offset: swap(value, offset) for at, value in held.items()})
        offset //= 2
    held = [held[at] for at in sorted(held)]

    whole = pl.BlockSpec(memory_space=pltpu.VMEM)
    *packed, by_row, by_slot = call(
        functools.partial(pack_tokens_kernel, experts, capacity),
        packed_shapes + [shape((rows, slots), f32), shape((slots, rows), f32)],
        (chip, *held),
        in_specs=[pl.BlockSpec(memory_space=pltpu.SMEM)] + [whole] * blocks,
        flops=2 * rows * slots * width,
    )
    packed = [after(value, *other[:2]) for value in packed]
    x = [packed[0]] + [swap(value, offset) for value, offset in zip(packed[1:], PLANE[1:])]

    packed = call(
        functools.partial(pack_cots_kernel, capacity),
        packed_shapes,
        (by_slot, *held),
        flops=2 * rows * slots * width,
    )
    grads = [packed[0]] + [swap(value, offset) for value, offset in zip(packed[1:], PLANE[1:])]

    all_taken = len(PLANE) * taken
    tile = 256 if hidden % 256 == 0 else LANES
    tiles, chunks = 2 * hidden // tile, len(column_chunks(width))
    slab_room = [pltpu.VMEM((width, 4 * hidden), bf16), pltpu.VMEM((2 * hidden, width), bf16)]
    flops = 2 * 3 * all_taken * width * 2 * hidden
    *outs, for_up, for_gate = call(
        functools.partial(forward_kernel, tile),
        packed_shapes + [shape((all_taken, 2 * hidden), f32)] * 2,
        (*x, *own, *other),
        flops=flops,
        in_specs=[whole] * 4 + [in_place] * 6,
        limit=VMEM_LIMIT_EXPERT,
        scratch=[
            pltpu.VMEM((all_taken, width), bf16),
            pltpu.VMEM((all_taken, 2 * hidden), bf16),
            *slab_room,
            pltpu.SemaphoreType.DMA((2 * tiles + 2 * chunks,)),
        ],
    )

    def go_home(values, weighted):
        back = [values[0]] + [swap(value, offset) for value, offset in zip(values[1:], PLANE[1:])]
        columns = values[0].shape[1]
        sums = call(
            functools.partial(unpack_kernel, weighted),
            [shape((tok_dev, columns), bf16)] * blocks,
            (by_row, *back),
            flops=2 * rows * slots * columns * (PIECES if weighted else 1),
        )
        return [sums[0]] + [swap(value, offset) for value, offset in zip(sums[1:], far)]

    result_shape = [shape((tok_dev, width), bf16)]
    out_homes = go_home(outs, True)
    (layer_out,) = call(functools.partial(sum_kernel, blocks), result_shape, out_homes)

    half = padded(width // 2)
    grads_shape = shape((all_taken, 4 * hidden), bf16)
    *backs, unit_grads = call(
        backward_kernel,
        [shape((taken, half), bf16)] * len(PLANE) + [grads_shape],
        (*grads, for_up, for_gate, *own, *other),
        flops=2 * all_taken * 2 * hidden * (width + 2 * half),
        in_specs=[whole] * 6 + [in_place] * 6,
        limit=VMEM_LIMIT_EXPERT,
        scratch=[
            pltpu.VMEM((all_taken, width), bf16),
            pltpu.VMEM((half, 4 * hidden), bf16),
            pltpu.VMEM((2 * hidden, width), bf16),
            pltpu.SemaphoreType.DMA((2 + 4 * len(column_chunks(half)),)),
        ],
    )
    homes = go_home(backs, False)
    backs = call(
        functools.partial(backward_rest_kernel, half),
        [shape((taken, width - half), bf16)] * len(PLANE),
        (after(unit_grads, out_homes[0]), *own[:2], *other[:2]),
        flops=2 * all_taken * 2 * hidden * 2 * (width - half),
        in_specs=[whole] + [in_place] * 4,
        limit=VMEM_LIMIT_EXPERT,
        scratch=[
            pltpu.VMEM((width - half, 4 * hidden), bf16),
            pltpu.SemaphoreType.DMA((4 * len(column_chunks(width - half)),)),
        ],
    )
    homes = homes + go_home(backs, False)
    (token_grad,) = call(functools.partial(sum_kernel, blocks), result_shape, homes)
    return layer_out, token_grad


def solution(mesh):
    rows = P(("groups", "expert"), None)
    slabs = P("expert", None, None)
    return jax.shard_map(
        on_device,
        mesh=mesh,
        in_specs=(rows, rows, rows, rows, slabs, slabs, slabs),
        out_specs=(rows, rows),
        check_vma=False,
    )
```

```python
import functools
import math

import jax
import jax.numpy as jnp
from jax import lax
from jax.experimental import pallas as pl
from jax.experimental.pallas import tpu as pltpu
from jax.sharding import PartitionSpec as P

CORE, PLANE, FAR = 1, (0, 2, 4, 6), 8
f32, bf16 = jnp.float32, jnp.bfloat16
CONTRACT_COLS = (((1,), (1,)), ((), ()))
LANES = 128
PIECES = 3
VMEM_LIMIT = 16 * 1024 * 1024
VMEM_LIMIT_EXPERT = 48 * 1024 * 1024
VMEM_LIMIT_ALL = 58 * 1024 * 1024


def swap(value, offset):
    devices = lax.axis_size("expert")
    return lax.ppermute(value, "expert", [(i, i ^ offset) for i in range(devices)])


def after(value, *others):
    return lax.optimization_barrier((value, *others))[0]


def padded(count):
    return -(-count // LANES) * LANES


def chunk_of(width):
    return 512 if width % 512 == 0 else LANES


def column_chunks(width):
    return [slice(at, at + chunk_of(width)) for at in range(0, width, chunk_of(width))]


def call(body, outs, args, flops=0, scratch=(), in_specs=None, limit=VMEM_LIMIT):
    size = sum(math.prod(a.shape) * a.dtype.itemsize for a in (*args, *outs))
    whole = pl.BlockSpec(memory_space=pltpu.VMEM)
    return pl.pallas_call(
        body,
        out_shape=outs,
        in_specs=[whole] * len(args) if in_specs is None else in_specs,
        out_specs=[whole] * len(outs),
        scratch_shapes=scratch,
        compiler_params=pltpu.CompilerParams(vmem_limit_bytes=limit),
        cost_estimate=pl.CostEstimate(flops=flops, bytes_accessed=size, transcendentals=0),
    )(*args)


def streams(triples):
    copies = [pltpu.make_async_copy(*triple) for triple in triples]
    for copy in copies:
        copy.start()
    return copies


def await_place(place, sem):
    pltpu.make_async_copy(place, place, sem).wait()


def code_kernel(experts, tokens_in, ids_in, gates_in, out, tokens, ids, gates, sems):
    rows, width = tokens.shape
    sources, places = (ids_in, gates_in, tokens_in), (ids, gates, tokens)
    copies = streams(zip(sources, places, (sems.at[number] for number in range(3))))
    gate_width = out.shape[1] - width
    copies[0].wait()
    copies[1].wait()
    line = lax.broadcasted_iota(jnp.int32, (gate_width, rows), 0)
    rest = jnp.zeros(line.shape, f32)
    for k in range(ids.shape[0]):
        rest = jnp.where(ids[k : k + 1] == line % experts, gates[k : k + 1], rest)
    columns = jnp.zeros(line.shape, f32)
    for number in range(PIECES):
        piece = rest.astype(bf16).astype(f32)
        columns = jnp.where(line // experts == number, piece, columns)
        rest = rest - piece
    out[:, width:] = columns.T.astype(bf16)
    copies[2].wait()
    for at in range(0, width, LANES):
        block = tokens[:, at : at + LANES].astype(f32)
        scale = jnp.max(jnp.abs(block), axis=1, keepdims=True) + 1e-06
        scale = scale.astype(bf16).astype(f32)
        quantized = (block / scale).astype(bf16).astype(f32)
        out[:, at : at + LANES] = (quantized * scale).astype(bf16)


def pack_tokens_kernel(experts, capacity, chip, *refs):
    *blocks, first, second, third, fourth, by_row, by_slot = refs
    tok_dev = blocks[0].shape[0]
    rows, slots = by_row.shape
    width = first.shape[1]
    taken = slots_of(len(blocks), capacity)
    columns = jnp.concatenate([block[:, width:].astype(f32) for block in blocks], axis=0)
    lane = lax.broadcasted_iota(jnp.int32, columns.shape, 1)
    pick = lax.broadcasted_iota(jnp.int32, (rows, LANES), 1)
    gates, named = [], jnp.zeros((rows, LANES), f32)
    for number in range(len(PLANE)):
        mine = (lane % experts == (chip[0] ^ number)) & (lane < PIECES * experts)
        gates.append(jnp.sum(jnp.where(mine, columns, 0.0), axis=1, keepdims=True))
        named = jnp.where((pick == number) & (gates[-1] > 0.0), 1.0, named)
    row = lax.broadcasted_iota(jnp.int32, (rows, rows), 0)
    other = lax.broadcasted_iota(jnp.int32, (rows, rows), 1)
    earlier = (row // tok_dev == other // tok_dev) & (other < row)
    earlier = jnp.where(earlier, 1.0, 0.0).astype(bf16)
    counts = jnp.dot(earlier, named.astype(bf16), preferred_element_type=f32)
    slot = lax.broadcasted_iota(jnp.int32, (rows, slots), 1)
    start = lax.broadcasted_iota(jnp.int32, (rows, 1), 0) // tok_dev * capacity
    weights = jnp.zeros((rows, slots), f32)
    for number, gate in enumerate(gates):
        count = jnp.sum(jnp.where(pick == number, counts, 0.0), axis=1, keepdims=True)
        place = number * taken + start + count.astype(jnp.int32)
        weights = jnp.where(slot == place, gate, weights)
    by_row[...] = weights
    by_slot[...] = weights.T
    chosen = jnp.where(by_slot[...] > 0.0, 1.0, 0.0).astype(bf16)
    for part in column_chunks(width):
        held = jnp.concatenate([block[:, part] for block in blocks], axis=0)
        packed = jnp.dot(chosen, held, preferred_element_type=f32)
        for number, out in enumerate((first, second, third, fourth)):
            out[:, part] = packed[number * taken : (number + 1) * taken].astype(bf16)


def pack_cots_kernel(capacity, by_slot, *refs):
    *blocks, first, second, third, fourth = refs
    width = first.shape[1]
    taken = slots_of(len(blocks), capacity)
    gate = jnp.sum(by_slot[...], axis=1, keepdims=True)
    chosen = jnp.where(by_slot[...] > 0.0, 1.0, 0.0).astype(bf16)
    for part in column_chunks(width):
        held = jnp.concatenate([block[:, part] for block in blocks], axis=0)
        packed = gate * jnp.dot(chosen, held, preferred_element_type=f32)
        for number, out in enumerate((first, second, third, fourth)):
            out[:, part] = packed[number * taken : (number + 1) * taken].astype(bf16)


def slots_of(blocks, capacity):
    return blocks * capacity


def joined(refs, part, height, kind=bf16):
    taken = [ref[:, part].astype(f32) for ref in refs]
    rest = height - sum(value.shape[0] for value in taken)
    if rest:
        taken.append(jnp.zeros((rest, taken[0].shape[1]), f32))
    return jnp.concatenate(taken, axis=0).astype(kind)


def unpack_kernel(weighted, by_row, first, second, third, fourth, *outs):
    rows, slots = by_row.shape
    tok_dev = outs[0].shape[0]
    if weighted:
        matrices, rest = [], by_row[...]
        for _ in range(PIECES):
            matrices.append(rest.astype(bf16))
            rest = rest - matrices[-1].astype(f32)
    else:
        matrices = [jnp.where(by_row[...] > 0.0, 1.0, 0.0).astype(bf16)]
    for part in column_chunks(first.shape[1]):
        packed = joined((first, second, third, fourth), part, slots)
        total = jnp.dot(matrices[0], packed, preferred_element_type=f32)
        for matrix in matrices[1:]:
            total = total + jnp.dot(matrix, packed, preferred_element_type=f32)
        for number, out in enumerate(outs):
            out[:, part] = total[number * tok_dev : (number + 1) * tok_dev].astype(bf16)


def sum_kernel(*refs):
    *blocks, out = refs
    for part in column_chunks(out.shape[1]):
        total = blocks[0][:, part].astype(f32)
        for block in blocks[1:]:
            total = total + block[:, part].astype(f32)
        out[:, part] = total.astype(bf16)


def forward_kernel(tile, x0, x1, x2, x3, *refs):
    *slabs, o0, o1, o2, o3, for_up, for_gate, x, hidden, into, back, sems = refs
    rows, width = x.shape
    units = back.shape[0] // 2
    chunk, tiles, chunks = chunk_of(width), 2 * units // tile, width // chunk_of(width)
    triples = []
    for number in range(tiles):
        slab, at = divmod(number * tile, units)
        for half, source in enumerate(slabs[3 * slab : 3 * slab + 2]):
            place = into.at[:, pl.ds((2 * number + half) * tile, tile)]
            triples.append((source.at[0, :, pl.ds(at, tile)], place, sems.at[number]))
    for number in range(chunks):
        columns = pl.ds(number * chunk, chunk)
        for slab in range(2):
            place = back.at[pl.ds(slab * units, units), columns]
            source = slabs[3 * slab + 2].at[0, :, columns]
            triples.append((source, place, sems.at[tiles + number]))
    streams(triples)
    for part in column_chunks(width):
        x[:, part] = joined((x0, x1, x2, x3), part, rows)

    @pl.loop(0, tiles)
    def _(number):
        columns = pl.ds(pl.multiple_of(number * 2 * tile, 2 * tile), 2 * tile)
        await_place(into.at[:, columns], sems.at[number])
        pre = jnp.dot(x[...], into[:, columns], preferred_element_type=f32)
        pre_gate, pre_up = pre[:, :tile], pre[:, tile:]
        sigma = jax.nn.sigmoid(pre_gate)
        activated = pre_gate * sigma
        at = pl.ds(pl.multiple_of(number * tile, tile), tile)
        hidden[:, at] = (activated * pre_up).astype(bf16)
        for_up[:, at] = activated
        for_gate[:, at] = pre_up * sigma * (1.0 + pre_gate * (1.0 - sigma))

    @pl.loop(0, chunks)
    def _(number):
        part = pl.ds(pl.multiple_of(number * chunk, chunk), chunk)
        await_place(back.at[:, part], sems.at[tiles + number])
        total = jnp.dot(hidden[...], back[:, part], preferred_element_type=f32)
        store_packed(total, (o0, o1, o2, o3), part)


def store_packed(total, outs, at):
    taken = outs[0].shape[0]
    for number, out in enumerate(outs):
        out[:, at] = total[number * taken : (number + 1) * taken].astype(bf16)


def backward_kernel(x0, x1, x2, x3, for_up, for_gate, *refs):
    *slabs, o0, o1, o2, o3, x, grads, into, back, sems = refs
    rows, width = x.shape
    units = back.shape[0] // 2
    chunk, chunks = chunk_of(width), width // chunk_of(width)
    triples = []
    for slab in range(2):
        place = back.at[pl.ds(slab * units, units)]
        triples.append((slabs[3 * slab + 2].at[0], place, sems.at[slab]))
    for number in range(chunks):
        lines = pl.ds(number * chunk, chunk)
        for column, matrix in enumerate((0, 1, 3, 4)):
            place = into.at[lines, pl.ds(column * units, units)]
            triples.append((slabs[matrix].at[0, lines], place, sems.at[2 + number]))
    streams(triples)
    for part in column_chunks(width):
        x[:, part] = joined((x0, x1, x2, x3), part, rows)

    @pl.loop(0, 2)
    def _(slab):
        at = pl.ds(pl.multiple_of(slab * units, units), units)
        await_place(back.at[at], sems.at[slab])
        hidden_grad = lax.dot_general(x[...], back[at], CONTRACT_COLS, preferred_element_type=f32)
        start = pl.multiple_of(2 * slab * units, 2 * units)
        gate_at, up_at = pl.ds(start, units), pl.ds(start + units, units)
        grads[:, gate_at] = (hidden_grad * for_gate[:, at]).astype(bf16)
        grads[:, up_at] = (hidden_grad * for_up[:, at]).astype(bf16)

    @pl.loop(0, chunks)
    def _(number):
        part = pl.ds(pl.multiple_of(number * chunk, chunk), chunk)
        await_place(into.at[part], sems.at[2 + number])
        total = lax.dot_general(
            grads[...], into[part], CONTRACT_COLS, preferred_element_type=f32
        )
        store_packed(total, (o0, o1, o2, o3), part)


def on_device(tokens, expert_ids, gate_values, cotangent, gate_weight, up_weight, down_weight):
    tok_dev, top = expert_ids.shape
    width, hidden = gate_weight.shape[1:]
    devices = lax.axis_size("expert")
    experts = devices // 2
    capacity = min(tok_dev, tok_dev * top * 5 // (4 * experts))
    far = range(FAR, devices, FAR)
    blocks = devices // FAR
    taken = slots_of(blocks, capacity)
    rows, slots = blocks * tok_dev, padded(len(PLANE) * taken)
    chip = (lax.axis_index("expert") // 2).reshape(1).astype(jnp.int32)
    shape = jax.ShapeDtypeStruct
    packed_shapes = [shape((taken, width), bf16)] * len(PLANE)

    own = (gate_weight, up_weight, down_weight)
    other = tuple(swap(slab, CORE) for slab in own)

    in_place = pl.BlockSpec(memory_space=pl.ANY)
    (coded,) = call(
        functools.partial(code_kernel, experts),
        [shape((tok_dev, width + padded(PIECES * experts)), bf16)],
        (tokens, expert_ids.T, gate_values.T),
        in_specs=[in_place] * 3,
        scratch=[
            pltpu.VMEM((tok_dev, width), bf16),
            pltpu.VMEM((top, tok_dev), jnp.int32),
            pltpu.VMEM((top, tok_dev), f32),
            pltpu.SemaphoreType.DMA((3,)),
        ],
        limit=VMEM_LIMIT_ALL,
    )
    held, offset = {0: coded}, devices // 2
    while offset >= FAR:
        held.update({at ^ offset: swap(value, offset) for at, value in held.items()})
        offset //= 2
    held = [held[at] for at in sorted(held)]

    whole = pl.BlockSpec(memory_space=pltpu.VMEM)
    *packed, by_row, by_slot = call(
        functools.partial(pack_tokens_kernel, experts, capacity),
        packed_shapes + [shape((rows, slots), f32), shape((slots, rows), f32)],
        (chip, *held),
        in_specs=[pl.BlockSpec(memory_space=pltpu.SMEM)] + [whole] * blocks,
        flops=2 * rows * slots * width,
    )
    packed = [after(value, *other[:2]) for value in packed]
    x = [packed[0]] + [swap(value, offset) for value, offset in zip(packed[1:], PLANE[1:])]

    cots, offset = {0: after(cotangent, held[blocks // 2])}, devices // 2
    while offset >= FAR:
        wait = other[2] if offset == FAR else cotangent
        ready = {at: after(value, wait) for at, value in cots.items()}
        cots.update({at ^ offset: swap(value, offset) for at, value in ready.items()})
        offset //= 2
    cots = [cots[at] for at in sorted(cots)]

    packed = call(
        functools.partial(pack_cots_kernel, capacity),
        packed_shapes,
        (by_slot, *cots),
        flops=2 * rows * slots * width,
    )
    grads = [packed[0]] + [swap(value, offset) for value, offset in zip(packed[1:], PLANE[1:])]

    all_taken = len(PLANE) * taken
    tile = 256 if hidden % 256 == 0 else LANES
    tiles, chunks = 2 * hidden // tile, width // chunk_of(width)
    slab_room = [pltpu.VMEM((width, 4 * hidden), bf16), pltpu.VMEM((2 * hidden, width), bf16)]
    flops = 2 * 3 * all_taken * width * 2 * hidden
    *outs, for_up, for_gate = call(
        functools.partial(forward_kernel, tile),
        packed_shapes + [shape((all_taken, 2 * hidden), f32)] * 2,
        (*x, *own, *other),
        flops=flops,
        in_specs=[whole] * 4 + [in_place] * 6,
        limit=VMEM_LIMIT_EXPERT,
        scratch=[
            pltpu.VMEM((all_taken, width), bf16),
            pltpu.VMEM((all_taken, 2 * hidden), bf16),
            *slab_room,
            pltpu.SemaphoreType.DMA((tiles + chunks,)),
        ],
    )

    def go_home(values, weighted):
        back = [values[0]] + [swap(value, offset) for value, offset in zip(values[1:], PLANE[1:])]
        sums = call(
            functools.partial(unpack_kernel, weighted),
            [shape((tok_dev, width), bf16)] * blocks,
            (by_row, *back),
            flops=2 * rows * slots * width * (PIECES if weighted else 1),
        )
        home = [sums[0]] + [swap(value, offset) for value, offset in zip(sums[1:], far)]
        (result,) = call(sum_kernel, [shape((tok_dev, width), bf16)], home)
        return result

    layer_out = go_home(outs, True)
    backs = call(
        backward_kernel,
        packed_shapes,
        (*grads, for_up, for_gate, *own, *other),
        flops=flops,
        in_specs=[whole] * 6 + [in_place] * 6,
        limit=VMEM_LIMIT_EXPERT,
        scratch=[
            pltpu.VMEM((all_taken, width), bf16),
            pltpu.VMEM((all_taken, 4 * hidden), bf16),
            *slab_room,
            pltpu.SemaphoreType.DMA((2 + chunks,)),
        ],
    )
    token_grad = go_home(backs, False)
    return layer_out, token_grad


def solution(mesh):
    rows = P(("groups", "expert"), None)
    slabs = P("expert", None, None)
    return jax.shard_map(
        on_device,
        mesh=mesh,
        in_specs=(rows, rows, rows, rows, slabs, slabs, slabs),
        out_specs=(rows, rows),
        check_vma=False,
    )
```

```python
import functools
import math

import jax
import jax.numpy as jnp
from jax import lax
from jax.experimental import pallas as pl
from jax.experimental.pallas import tpu as pltpu
from jax.sharding import PartitionSpec as P

CORE, PLANE, FAR = 1, (0, 2, 4, 6), 8
f32, bf16 = jnp.float32, jnp.bfloat16
CONTRACT_COLS = (((1,), (1,)), ((), ()))
LANES = 128
PIECES = 3
VMEM_LIMIT = 16 * 1024 * 1024
VMEM_LIMIT_EXPERT = 48 * 1024 * 1024


def swap(value, offset):
    devices = lax.axis_size("expert")
    return lax.ppermute(value, "expert", [(i, i ^ offset) for i in range(devices)])


def after(value, *others):
    return lax.optimization_barrier((value, *others))[0]


def padded(count):
    return -(-count // LANES) * LANES


def chunk_of(width):
    return 512 if width % 512 == 0 else LANES


def column_chunks(width):
    return [slice(at, at + chunk_of(width)) for at in range(0, width, chunk_of(width))]


def call(body, outs, args, flops=0, scratch=(), in_specs=None, limit=VMEM_LIMIT):
    size = sum(math.prod(a.shape) * a.dtype.itemsize for a in (*args, *outs))
    whole = pl.BlockSpec(memory_space=pltpu.VMEM)
    return pl.pallas_call(
        body,
        out_shape=outs,
        in_specs=[whole] * len(args) if in_specs is None else in_specs,
        out_specs=[whole] * len(outs),
        scratch_shapes=scratch,
        compiler_params=pltpu.CompilerParams(vmem_limit_bytes=limit),
        cost_estimate=pl.CostEstimate(flops=flops, bytes_accessed=size, transcendentals=0),
    )(*args)


def streams(triples):
    copies = [pltpu.make_async_copy(*triple) for triple in triples]
    for copy in copies:
        copy.start()
    return copies


def await_place(place, sem):
    pltpu.make_async_copy(place, place, sem).wait()


def code_kernel(experts, tokens, ids, gates, out):
    rows, width = tokens.shape
    gate_width = out.shape[1] - width
    line = lax.broadcasted_iota(jnp.int32, (gate_width, rows), 0)
    rest = jnp.zeros(line.shape, f32)
    for k in range(ids.shape[0]):
        rest = jnp.where(ids[k : k + 1] == line % experts, gates[k : k + 1], rest)
    columns = jnp.zeros(line.shape, f32)
    for number in range(PIECES):
        piece = rest.astype(bf16).astype(f32)
        columns = jnp.where(line // experts == number, piece, columns)
        rest = rest - piece
    out[:, width:] = columns.T.astype(bf16)
    for at in range(0, width, LANES):
        block = tokens[:, at : at + LANES].astype(f32)
        scale = jnp.max(jnp.abs(block), axis=1, keepdims=True) + 1e-06
        scale = scale.astype(bf16).astype(f32)
        quantized = (block / scale).astype(bf16).astype(f32)
        out[:, at : at + LANES] = (quantized * scale).astype(bf16)


def pack_tokens_kernel(experts, capacity, chip, *refs):
    *blocks, first, second, third, fourth, by_row, by_slot = refs
    tok_dev = blocks[0].shape[0]
    rows, slots = by_row.shape
    width = first.shape[1]
    taken = slots_of(len(blocks), capacity)
    columns = jnp.concatenate([block[:, width:].astype(f32) for block in blocks], axis=0)
    lane = lax.broadcasted_iota(jnp.int32, columns.shape, 1)
    pick = lax.broadcasted_iota(jnp.int32, (rows, LANES), 1)
    gates, named = [], jnp.zeros((rows, LANES), f32)
    for number in range(len(PLANE)):
        mine = (lane % experts == (chip[0] ^ number)) & (lane < PIECES * experts)
        gates.append(jnp.sum(jnp.where(mine, columns, 0.0), axis=1, keepdims=True))
        named = jnp.where((pick == number) & (gates[-1] > 0.0), 1.0, named)
    row = lax.broadcasted_iota(jnp.int32, (rows, rows), 0)
    other = lax.broadcasted_iota(jnp.int32, (rows, rows), 1)
    earlier = (row // tok_dev == other // tok_dev) & (other < row)
    earlier = jnp.where(earlier, 1.0, 0.0).astype(bf16)
    counts = jnp.dot(earlier, named.astype(bf16), preferred_element_type=f32)
    slot = lax.broadcasted_iota(jnp.int32, (rows, slots), 1)
    start = lax.broadcasted_iota(jnp.int32, (rows, 1), 0) // tok_dev * capacity
    weights = jnp.zeros((rows, slots), f32)
    for number, gate in enumerate(gates):
        count = jnp.sum(jnp.where(pick == number, counts, 0.0), axis=1, keepdims=True)
        place = number * taken + start + count.astype(jnp.int32)
        weights = jnp.where(slot == place, gate, weights)
    by_row[...] = weights
    by_slot[...] = weights.T
    chosen = jnp.where(by_slot[...] > 0.0, 1.0, 0.0).astype(bf16)
    for part in column_chunks(width):
        held = jnp.concatenate([block[:, part] for block in blocks], axis=0)
        packed = jnp.dot(chosen, held, preferred_element_type=f32)
        for number, out in enumerate((first, second, third, fourth)):
            out[:, part] = packed[number * taken : (number + 1) * taken].astype(bf16)


def pack_cots_kernel(capacity, by_slot, *refs):
    *blocks, first, second, third, fourth = refs
    width = first.shape[1]
    taken = slots_of(len(blocks), capacity)
    gate = jnp.sum(by_slot[...], axis=1, keepdims=True)
    chosen = jnp.where(by_slot[...] > 0.0, 1.0, 0.0).astype(bf16)
    for part in column_chunks(width):
        held = jnp.concatenate([block[:, part] for block in blocks], axis=0)
        packed = gate * jnp.dot(chosen, held, preferred_element_type=f32)
        for number, out in enumerate((first, second, third, fourth)):
            out[:, part] = packed[number * taken : (number + 1) * taken].astype(bf16)


def slots_of(blocks, capacity):
    return blocks * capacity


def joined(refs, part, height, kind=bf16):
    taken = [ref[:, part].astype(f32) for ref in refs]
    rest = height - sum(value.shape[0] for value in taken)
    if rest:
        taken.append(jnp.zeros((rest, taken[0].shape[1]), f32))
    return jnp.concatenate(taken, axis=0).astype(kind)


def unpack_kernel(weighted, by_row, first, second, third, fourth, *outs):
    rows, slots = by_row.shape
    tok_dev = outs[0].shape[0]
    if weighted:
        matrices, rest = [], by_row[...]
        for _ in range(PIECES):
            matrices.append(rest.astype(bf16))
            rest = rest - matrices[-1].astype(f32)
    else:
        matrices = [jnp.where(by_row[...] > 0.0, 1.0, 0.0).astype(bf16)]
    for part in column_chunks(first.shape[1]):
        packed = joined((first, second, third, fourth), part, slots)
        total = jnp.dot(matrices[0], packed, preferred_element_type=f32)
        for matrix in matrices[1:]:
            total = total + jnp.dot(matrix, packed, preferred_element_type=f32)
        for number, out in enumerate(outs):
            out[:, part] = total[number * tok_dev : (number + 1) * tok_dev].astype(bf16)


def sum_kernel(*refs):
    *blocks, out = refs
    for part in column_chunks(out.shape[1]):
        total = blocks[0][:, part].astype(f32)
        for block in blocks[1:]:
            total = total + block[:, part].astype(f32)
        out[:, part] = total.astype(bf16)


def forward_kernel(tile, x0, x1, x2, x3, *refs):
    *slabs, o0, o1, o2, o3, for_up, for_gate, x, hidden, into, back, sems = refs
    rows, width = x.shape
    units = back.shape[0] // 2
    chunk, tiles, chunks = chunk_of(width), 2 * units // tile, width // chunk_of(width)
    triples = []
    for number in range(tiles):
        slab, at = divmod(number * tile, units)
        for half, source in enumerate(slabs[3 * slab : 3 * slab + 2]):
            place = into.at[:, pl.ds((2 * number + half) * tile, tile)]
            triples.append((source.at[0, :, pl.ds(at, tile)], place, sems.at[number]))
    for number in range(chunks):
        columns = pl.ds(number * chunk, chunk)
        for slab in range(2):
            place = back.at[pl.ds(slab * units, units), columns]
            source = slabs[3 * slab + 2].at[0, :, columns]
            triples.append((source, place, sems.at[tiles + number]))
    streams(triples)
    for part in column_chunks(width):
        x[:, part] = joined((x0, x1, x2, x3), part, rows)

    @pl.loop(0, tiles)
    def _(number):
        columns = pl.ds(pl.multiple_of(number * 2 * tile, 2 * tile), 2 * tile)
        await_place(into.at[:, columns], sems.at[number])
        pre = jnp.dot(x[...], into[:, columns], preferred_element_type=f32)
        pre_gate, pre_up = pre[:, :tile], pre[:, tile:]
        sigma = jax.nn.sigmoid(pre_gate)
        activated = pre_gate * sigma
        at = pl.ds(pl.multiple_of(number * tile, tile), tile)
        hidden[:, at] = (activated * pre_up).astype(bf16)
        for_up[:, at] = activated
        for_gate[:, at] = pre_up * sigma * (1.0 + pre_gate * (1.0 - sigma))

    @pl.loop(0, chunks)
    def _(number):
        part = pl.ds(pl.multiple_of(number * chunk, chunk), chunk)
        await_place(back.at[:, part], sems.at[tiles + number])
        total = jnp.dot(hidden[...], back[:, part], preferred_element_type=f32)
        store_packed(total, (o0, o1, o2, o3), part)


def store_packed(total, outs, at):
    taken = outs[0].shape[0]
    for number, out in enumerate(outs):
        out[:, at] = total[number * taken : (number + 1) * taken].astype(bf16)


def backward_kernel(x0, x1, x2, x3, for_up, for_gate, *refs):
    *slabs, o0, o1, o2, o3, x, grads, into, back, sems = refs
    rows, width = x.shape
    units = back.shape[0] // 2
    chunk, chunks = chunk_of(width), width // chunk_of(width)
    triples = []
    for slab in range(2):
        place = back.at[pl.ds(slab * units, units)]
        triples.append((slabs[3 * slab + 2].at[0], place, sems.at[slab]))
    for number in range(chunks):
        lines = pl.ds(number * chunk, chunk)
        for column, matrix in enumerate((0, 1, 3, 4)):
            place = into.at[lines, pl.ds(column * units, units)]
            triples.append((slabs[matrix].at[0, lines], place, sems.at[2 + number]))
    streams(triples)
    for part in column_chunks(width):
        x[:, part] = joined((x0, x1, x2, x3), part, rows)

    @pl.loop(0, 2)
    def _(slab):
        at = pl.ds(pl.multiple_of(slab * units, units), units)
        await_place(back.at[at], sems.at[slab])
        hidden_grad = lax.dot_general(x[...], back[at], CONTRACT_COLS, preferred_element_type=f32)
        start = pl.multiple_of(2 * slab * units, 2 * units)
        gate_at, up_at = pl.ds(start, units), pl.ds(start + units, units)
        grads[:, gate_at] = (hidden_grad * for_gate[:, at]).astype(bf16)
        grads[:, up_at] = (hidden_grad * for_up[:, at]).astype(bf16)

    @pl.loop(0, chunks)
    def _(number):
        part = pl.ds(pl.multiple_of(number * chunk, chunk), chunk)
        await_place(into.at[part], sems.at[2 + number])
        total = lax.dot_general(
            grads[...], into[part], CONTRACT_COLS, preferred_element_type=f32
        )
        store_packed(total, (o0, o1, o2, o3), part)


def on_device(tokens, expert_ids, gate_values, cotangent, gate_weight, up_weight, down_weight):
    tok_dev, top = expert_ids.shape
    width, hidden = gate_weight.shape[1:]
    devices = lax.axis_size("expert")
    experts = devices // 2
    capacity = min(tok_dev, tok_dev * top * 5 // (4 * experts))
    far = range(FAR, devices, FAR)
    blocks = devices // FAR
    taken = slots_of(blocks, capacity)
    rows, slots = blocks * tok_dev, padded(len(PLANE) * taken)
    chip = (lax.axis_index("expert") // 2).reshape(1).astype(jnp.int32)
    shape = jax.ShapeDtypeStruct
    packed_shapes = [shape((taken, width), bf16)] * len(PLANE)

    own = (gate_weight, up_weight, down_weight)
    other = tuple(swap(slab, CORE) for slab in own)

    in_place = pl.BlockSpec(memory_space=pltpu.HBM)
    (coded,) = call(
        functools.partial(code_kernel, experts),
        [shape((tok_dev, width + padded(PIECES * experts)), bf16)],
        (tokens, expert_ids.T, gate_values.T),
    )
    held, offset = {0: coded}, devices // 2
    while offset >= FAR:
        held.update({at ^ offset: swap(value, offset) for at, value in held.items()})
        offset //= 2
    held = [held[at] for at in sorted(held)]

    whole = pl.BlockSpec(memory_space=pltpu.VMEM)
    *packed, by_row, by_slot = call(
        functools.partial(pack_tokens_kernel, experts, capacity),
        packed_shapes + [shape((rows, slots), f32), shape((slots, rows), f32)],
        (chip, *held),
        in_specs=[pl.BlockSpec(memory_space=pltpu.SMEM)] + [whole] * blocks,
        flops=2 * rows * slots * width,
    )
    far_cots = swap(after(cotangent, held[blocks // 2], other[0]), devices // 2)
    packed = [after(value, far_cots, *other[:2]) for value in packed]
    x = [packed[0]] + [swap(value, offset) for value, offset in zip(packed[1:], PLANE[1:])]

    cots, offset = {0: cotangent, blocks // 2: far_cots}, devices // 4
    while offset >= FAR:
        wait = other[2] if offset == FAR else cotangent
        ready = {at: after(value, wait) for at, value in cots.items()}
        cots.update({at ^ offset // FAR: swap(value, offset) for at, value in ready.items()})
        offset //= 2
    cots = [cots[at] for at in sorted(cots)]

    packed = call(
        functools.partial(pack_cots_kernel, capacity),
        packed_shapes,
        (by_slot, *cots),
        flops=2 * rows * slots * width,
    )
    grads = [packed[0]] + [swap(value, offset) for value, offset in zip(packed[1:], PLANE[1:])]

    all_taken = len(PLANE) * taken
    tile = 256 if hidden % 256 == 0 else LANES
    tiles, chunks = 2 * hidden // tile, width // chunk_of(width)
    slab_room = [pltpu.VMEM((width, 4 * hidden), bf16), pltpu.VMEM((2 * hidden, width), bf16)]
    flops = 2 * 3 * all_taken * width * 2 * hidden
    *outs, for_up, for_gate = call(
        functools.partial(forward_kernel, tile),
        packed_shapes + [shape((all_taken, 2 * hidden), f32)] * 2,
        (*x, *own, *other),
        flops=flops,
        in_specs=[whole] * 4 + [in_place] * 6,
        limit=VMEM_LIMIT_EXPERT,
        scratch=[
            pltpu.VMEM((all_taken, width), bf16),
            pltpu.VMEM((all_taken, 2 * hidden), bf16),
            *slab_room,
            pltpu.SemaphoreType.DMA((tiles + chunks,)),
        ],
    )

    def go_home(values, weighted):
        back = [values[0]] + [swap(value, offset) for value, offset in zip(values[1:], PLANE[1:])]
        sums = call(
            functools.partial(unpack_kernel, weighted),
            [shape((tok_dev, width), bf16)] * blocks,
            (by_row, *back),
            flops=2 * rows * slots * width * (PIECES if weighted else 1),
        )
        home = [sums[0]] + [swap(value, offset) for value, offset in zip(sums[1:], far)]
        (result,) = call(sum_kernel, [shape((tok_dev, width), bf16)], home)
        return result

    layer_out = go_home(outs, True)
    backs = call(
        backward_kernel,
        packed_shapes,
        (*grads, for_up, for_gate, *own, *other),
        flops=flops,
        in_specs=[whole] * 6 + [in_place] * 6,
        limit=VMEM_LIMIT_EXPERT,
        scratch=[
            pltpu.VMEM((all_taken, width), bf16),
            pltpu.VMEM((all_taken, 4 * hidden), bf16),
            *slab_room,
            pltpu.SemaphoreType.DMA((2 + chunks,)),
        ],
    )
    token_grad = go_home(backs, False)
    return layer_out, token_grad


def solution(mesh):
    rows = P(("groups", "expert"), None)
    slabs = P("expert", None, None)
    return jax.shard_map(
        on_device,
        mesh=mesh,
        in_specs=(rows, rows, rows, rows, slabs, slabs, slabs),
        out_specs=(rows, rows),
        check_vma=False,
    )
```

```python
import functools
import math

import jax
import jax.numpy as jnp
from jax import lax
from jax.experimental import pallas as pl
from jax.experimental.pallas import tpu as pltpu
from jax.sharding import PartitionSpec as P

CORE, PLANE, FAR = 1, (0, 2, 4, 6), 8
f32, bf16 = jnp.float32, jnp.bfloat16
CONTRACT_COLS = (((1,), (1,)), ((), ()))
LANES = 128
PIECES = 3
VMEM_LIMIT = 16 * 1024 * 1024


def swap(value, offset):
    devices = lax.axis_size("expert")
    return lax.ppermute(value, "expert", [(i, i ^ offset) for i in range(devices)])


def after(value, *others):
    return lax.optimization_barrier((value, *others))[0]


def padded(count):
    return -(-count // LANES) * LANES


def chunk_of(width):
    return 512 if width % 512 == 0 else LANES


def column_chunks(width):
    return [slice(at, at + chunk_of(width)) for at in range(0, width, chunk_of(width))]


def call(body, outs, args, flops=0, scratch=(), in_specs=None):
    size = sum(math.prod(a.shape) * a.dtype.itemsize for a in (*args, *outs))
    whole = pl.BlockSpec(memory_space=pltpu.VMEM)
    return pl.pallas_call(
        body,
        out_shape=outs,
        in_specs=[whole] * len(args) if in_specs is None else in_specs,
        out_specs=[whole] * len(outs),
        scratch_shapes=scratch,
        compiler_params=pltpu.CompilerParams(vmem_limit_bytes=VMEM_LIMIT),
        cost_estimate=pl.CostEstimate(flops=flops, bytes_accessed=size, transcendentals=0),
    )(*args)


def code_kernel(experts, tokens, ids, gates, out):
    rows, width = tokens.shape
    gate_width = out.shape[1] - width
    line = lax.broadcasted_iota(jnp.int32, (gate_width, rows), 0)
    rest = jnp.zeros(line.shape, f32)
    for k in range(ids.shape[0]):
        rest = jnp.where(ids[k : k + 1] == line % experts, gates[k : k + 1], rest)
    columns = jnp.zeros(line.shape, f32)
    for number in range(PIECES):
        piece = rest.astype(bf16).astype(f32)
        columns = jnp.where(line // experts == number, piece, columns)
        rest = rest - piece
    out[:, width:] = columns.T.astype(bf16)
    for at in range(0, width, LANES):
        block = tokens[:, at : at + LANES].astype(f32)
        scale = jnp.max(jnp.abs(block), axis=1, keepdims=True) + 1e-06
        scale = scale.astype(bf16).astype(f32)
        quantized = (block / scale).astype(bf16).astype(f32)
        out[:, at : at + LANES] = (quantized * scale).astype(bf16)


def pack_tokens_kernel(experts, capacity, chip, *refs):
    *blocks, first, second, third, fourth, by_row, by_slot = refs
    tok_dev = blocks[0].shape[0]
    rows, slots = by_row.shape
    width = first.shape[1]
    taken = slots_of(len(blocks), capacity)
    columns = jnp.concatenate([block[:, width:].astype(f32) for block in blocks], axis=0)
    lane = lax.broadcasted_iota(jnp.int32, columns.shape, 1)
    pick = lax.broadcasted_iota(jnp.int32, (rows, LANES), 1)
    gates, named = [], jnp.zeros((rows, LANES), f32)
    for number in range(len(PLANE)):
        mine = (lane % experts == (chip[0] ^ number)) & (lane < PIECES * experts)
        gates.append(jnp.sum(jnp.where(mine, columns, 0.0), axis=1, keepdims=True))
        named = jnp.where((pick == number) & (gates[-1] > 0.0), 1.0, named)
    row = lax.broadcasted_iota(jnp.int32, (rows, rows), 0)
    other = lax.broadcasted_iota(jnp.int32, (rows, rows), 1)
    earlier = (row // tok_dev == other // tok_dev) & (other < row)
    earlier = jnp.where(earlier, 1.0, 0.0).astype(bf16)
    counts = jnp.dot(earlier, named.astype(bf16), preferred_element_type=f32)
    slot = lax.broadcasted_iota(jnp.int32, (rows, slots), 1)
    start = lax.broadcasted_iota(jnp.int32, (rows, 1), 0) // tok_dev * capacity
    weights = jnp.zeros((rows, slots), f32)
    for number, gate in enumerate(gates):
        count = jnp.sum(jnp.where(pick == number, counts, 0.0), axis=1, keepdims=True)
        place = number * taken + start + count.astype(jnp.int32)
        weights = jnp.where(slot == place, gate, weights)
    by_row[...] = weights
    by_slot[...] = weights.T
    chosen = jnp.where(by_slot[...] > 0.0, 1.0, 0.0).astype(bf16)
    for part in column_chunks(width):
        held = jnp.concatenate([block[:, part] for block in blocks], axis=0)
        packed = jnp.dot(chosen, held, preferred_element_type=f32)
        for number, out in enumerate((first, second, third, fourth)):
            out[:, part] = packed[number * taken : (number + 1) * taken].astype(bf16)


def pack_cots_kernel(capacity, by_slot, *refs):
    *blocks, first, second, third, fourth = refs
    width = first.shape[1]
    taken = slots_of(len(blocks), capacity)
    gate = jnp.sum(by_slot[...], axis=1, keepdims=True)
    chosen = jnp.where(by_slot[...] > 0.0, 1.0, 0.0).astype(bf16)
    for part in column_chunks(width):
        held = jnp.concatenate([block[:, part] for block in blocks], axis=0)
        packed = gate * jnp.dot(chosen, held, preferred_element_type=f32)
        for number, out in enumerate((first, second, third, fourth)):
            out[:, part] = packed[number * taken : (number + 1) * taken].astype(bf16)


def slots_of(blocks, capacity):
    return blocks * capacity


def joined(refs, part, height, kind=bf16):
    taken = [ref[:, part].astype(f32) for ref in refs]
    rest = height - sum(value.shape[0] for value in taken)
    if rest:
        taken.append(jnp.zeros((rest, taken[0].shape[1]), f32))
    return jnp.concatenate(taken, axis=0).astype(kind)


def unpack_kernel(weighted, by_row, first, second, third, fourth, *outs):
    rows, slots = by_row.shape
    tok_dev = outs[0].shape[0]
    if weighted:
        matrices, rest = [], by_row[...]
        for _ in range(PIECES):
            matrices.append(rest.astype(bf16))
            rest = rest - matrices[-1].astype(f32)
    else:
        matrices = [jnp.where(by_row[...] > 0.0, 1.0, 0.0).astype(bf16)]
    for part in column_chunks(first.shape[1]):
        packed = joined((first, second, third, fourth), part, slots)
        total = jnp.dot(matrices[0], packed, preferred_element_type=f32)
        for matrix in matrices[1:]:
            total = total + jnp.dot(matrix, packed, preferred_element_type=f32)
        for number, out in enumerate(outs):
            out[:, part] = total[number * tok_dev : (number + 1) * tok_dev].astype(bf16)


def sum_kernel(*refs):
    *blocks, out = refs
    for part in column_chunks(out.shape[1]):
        total = blocks[0][:, part].astype(f32)
        for block in blocks[1:]:
            total = total + block[:, part].astype(f32)
        out[:, part] = total.astype(bf16)


def forward_kernel(x0, x1, x2, x3, g0, u0, d0, g1, u1, d1, *refs):
    o0, o1, o2, o3, for_up, for_gate, x, hidden = refs
    rows, width = x.shape
    units = g0.shape[2]
    for part in column_chunks(width):
        x[:, part] = joined((x0, x1, x2, x3), part, rows)

    for slab, (gate_w, up_w) in enumerate(((g0, u0), (g1, u1))):
        at = slice(slab * units, (slab + 1) * units)
        pre_gate = jnp.dot(x[...], gate_w[0], preferred_element_type=f32)
        pre_up = jnp.dot(x[...], up_w[0], preferred_element_type=f32)
        sigma = jax.nn.sigmoid(pre_gate)
        activated = pre_gate * sigma
        hidden[:, at] = (activated * pre_up).astype(bf16)
        for_up[:, at] = activated
        for_gate[:, at] = pre_up * sigma * (1.0 + pre_gate * (1.0 - sigma))

    @pl.loop(0, width // chunk_of(width))
    def _(number):
        part = pl.ds(pl.multiple_of(number * chunk_of(width), LANES), chunk_of(width))
        total = jnp.dot(hidden[:, :units], d0[0, :, part], preferred_element_type=f32)
        total = total + jnp.dot(hidden[:, units:], d1[0, :, part], preferred_element_type=f32)
        store_packed(total, (o0, o1, o2, o3), part)


def store_packed(total, outs, at):
    taken = outs[0].shape[0]
    for number, out in enumerate(outs):
        out[:, at] = total[number * taken : (number + 1) * taken].astype(bf16)


def backward_kernel(x0, x1, x2, x3, for_up, for_gate, g0, u0, d0, g1, u1, d1, *refs):
    o0, o1, o2, o3, x, gate_grad, up_grad = refs
    rows, width = x.shape
    units = g0.shape[2]
    for part in column_chunks(width):
        x[:, part] = joined((x0, x1, x2, x3), part, rows)

    def transposed(left, right):
        return lax.dot_general(left, right, CONTRACT_COLS, preferred_element_type=f32)

    for slab, down_w in enumerate((d0, d1)):
        at = slice(slab * units, (slab + 1) * units)
        hidden_grad = transposed(x[...], down_w[0])
        gate_grad[:, at] = (hidden_grad * for_gate[:, at]).astype(bf16)
        up_grad[:, at] = (hidden_grad * for_up[:, at]).astype(bf16)

    @pl.loop(0, width // chunk_of(width))
    def _(number):
        part = pl.ds(pl.multiple_of(number * chunk_of(width), LANES), chunk_of(width))
        total = transposed(gate_grad[:, :units], g0[0, part])
        total = total + transposed(up_grad[:, :units], u0[0, part])
        total = total + transposed(gate_grad[:, units:], g1[0, part])
        total = total + transposed(up_grad[:, units:], u1[0, part])
        store_packed(total, (o0, o1, o2, o3), part)


def on_device(tokens, expert_ids, gate_values, cotangent, gate_weight, up_weight, down_weight):
    tok_dev, top = expert_ids.shape
    width, hidden = gate_weight.shape[1:]
    devices = lax.axis_size("expert")
    experts = devices // 2
    capacity = min(tok_dev, tok_dev * top * 5 // (4 * experts))
    far = range(FAR, devices, FAR)
    blocks = devices // FAR
    taken = slots_of(blocks, capacity)
    rows, slots = blocks * tok_dev, padded(len(PLANE) * taken)
    chip = (lax.axis_index("expert") // 2).reshape(1).astype(jnp.int32)
    shape = jax.ShapeDtypeStruct
    packed_shapes = [shape((taken, width), bf16)] * len(PLANE)

    own = (gate_weight, up_weight, down_weight)
    other = tuple(swap(slab, CORE) for slab in own)

    (coded,) = call(
        functools.partial(code_kernel, experts),
        [shape((tok_dev, width + padded(PIECES * experts)), bf16)],
        (tokens, expert_ids.T, gate_values.T),
    )
    held, offset = {0: coded}, devices // 2
    while offset >= FAR:
        held.update({at ^ offset: swap(value, offset) for at, value in held.items()})
        offset //= 2
    held = [held[at] for at in sorted(held)]

    whole = pl.BlockSpec(memory_space=pltpu.VMEM)
    *packed, by_row, by_slot = call(
        functools.partial(pack_tokens_kernel, experts, capacity),
        packed_shapes + [shape((rows, slots), f32), shape((slots, rows), f32)],
        (chip, *held),
        in_specs=[pl.BlockSpec(memory_space=pltpu.SMEM)] + [whole] * blocks,
        flops=2 * rows * slots * width,
    )
    far_cots = swap(after(cotangent, held[blocks // 2], other[0]), devices // 2)
    packed = packed_tokens = [after(value, *other[:2]) for value in packed]
    packed[-1] = after(packed[-1], far_cots)
    x = [packed[0]] + [swap(value, offset) for value, offset in zip(packed[1:], PLANE[1:])]

    cots, offset = {0: cotangent, blocks // 2: far_cots}, devices // 4
    while offset >= FAR:
        wait = other[2] if offset == FAR else cotangent
        ready = {at: after(value, wait) for at, value in cots.items()}
        cots.update({at ^ offset // FAR: swap(value, offset) for at, value in ready.items()})
        offset //= 2
    cots = [cots[at] for at in sorted(cots)]

    packed = call(
        functools.partial(pack_cots_kernel, capacity),
        packed_shapes,
        (by_slot, *cots),
        flops=2 * rows * slots * width,
    )
    grads = [packed[0]] + [swap(value, offset) for value, offset in zip(packed[1:], PLANE[1:])]

    all_taken = len(PLANE) * taken
    flops = 2 * 3 * all_taken * width * 2 * hidden
    own = [after(slab, packed_tokens[0]) for slab in own]
    *outs, for_up, for_gate = call(
        forward_kernel,
        packed_shapes + [shape((all_taken, 2 * hidden), f32)] * 2,
        (*x, *own, *other),
        flops=flops,
        scratch=[
            pltpu.VMEM((all_taken, width), bf16),
            pltpu.VMEM((all_taken, 2 * hidden), bf16),
        ],
    )

    def go_home(values, weighted):
        back = [values[0]] + [swap(value, offset) for value, offset in zip(values[1:], PLANE[1:])]
        sums = call(
            functools.partial(unpack_kernel, weighted),
            [shape((tok_dev, width), bf16)] * blocks,
            (by_row, *back),
            flops=2 * rows * slots * width * (PIECES if weighted else 1),
        )
        home = [sums[0]] + [swap(value, offset) for value, offset in zip(sums[1:], far)]
        (result,) = call(sum_kernel, [shape((tok_dev, width), bf16)], home)
        return result

    layer_out = go_home(outs, True)
    backs = call(
        backward_kernel,
        packed_shapes,
        (*grads, for_up, for_gate, *own, *other),
        flops=flops,
        scratch=[
            pltpu.VMEM((all_taken, width), bf16),
            pltpu.VMEM((all_taken, 2 * hidden), bf16),
            pltpu.VMEM((all_taken, 2 * hidden), bf16),
        ],
    )
    token_grad = go_home(backs, False)
    return layer_out, token_grad


def solution(mesh):
    rows = P(("groups", "expert"), None)
    slabs = P("expert", None, None)
    return jax.shard_map(
        on_device,
        mesh=mesh,
        in_specs=(rows, rows, rows, rows, slabs, slabs, slabs),
        out_specs=(rows, rows),
        check_vma=False,
    )
```

```python
import functools
import math

import jax
import jax.numpy as jnp
from jax import lax
from jax.experimental import pallas as pl
from jax.experimental.pallas import tpu as pltpu
from jax.sharding import PartitionSpec as P

CORE, PLANE, FAR = 1, (0, 2, 4, 6), 8
f32, bf16 = jnp.float32, jnp.bfloat16
CONTRACT_COLS = (((1,), (1,)), ((), ()))
LANES = 128
PIECES = 3
VMEM_LIMIT = 16 * 1024 * 1024
VMEM_LIMIT_EXPERT = 48 * 1024 * 1024


def swap(value, offset):
    devices = lax.axis_size("expert")
    return lax.ppermute(value, "expert", [(i, i ^ offset) for i in range(devices)])


def after(value, *others):
    return lax.optimization_barrier((value, *others))[0]


def padded(count):
    return -(-count // LANES) * LANES


def chunk_of(width):
    return 512 if width % 512 == 0 else LANES


def back_chunk(width):
    return width // 2 if width % (2 * LANES) == 0 else LANES


def column_chunks(width):
    return [slice(at, at + chunk_of(width)) for at in range(0, width, chunk_of(width))]


def call(body, outs, args, flops=0, scratch=(), in_specs=None, limit=VMEM_LIMIT):
    size = sum(math.prod(a.shape) * a.dtype.itemsize for a in (*args, *outs))
    whole = pl.BlockSpec(memory_space=pltpu.VMEM)
    return pl.pallas_call(
        body,
        out_shape=outs,
        in_specs=[whole] * len(args) if in_specs is None else in_specs,
        out_specs=[whole] * len(outs),
        scratch_shapes=scratch,
        compiler_params=pltpu.CompilerParams(vmem_limit_bytes=limit),
        cost_estimate=pl.CostEstimate(flops=flops, bytes_accessed=size, transcendentals=0),
    )(*args)


def streams(triples):
    copies = [pltpu.make_async_copy(*triple) for triple in triples]
    for copy in copies:
        copy.start()
    return copies


def await_place(place, sem):
    pltpu.make_async_copy(place, place, sem).wait()


def code_kernel(experts, tokens, ids, gates, out):
    rows, width = tokens.shape
    gate_width = out.shape[1] - width
    line = lax.broadcasted_iota(jnp.int32, (gate_width, rows), 0)
    rest = jnp.zeros(line.shape, f32)
    for k in range(ids.shape[0]):
        rest = jnp.where(ids[k : k + 1] == line % experts, gates[k : k + 1], rest)
    columns = jnp.zeros(line.shape, f32)
    for number in range(PIECES):
        piece = rest.astype(bf16).astype(f32)
        columns = jnp.where(line // experts == number, piece, columns)
        rest = rest - piece
    out[:, width:] = columns.T.astype(bf16)
    for at in range(0, width, LANES):
        block = tokens[:, at : at + LANES].astype(f32)
        scale = jnp.max(jnp.abs(block), axis=1, keepdims=True) + 1e-06
        scale = scale.astype(bf16).astype(f32)
        quantized = (block / scale).astype(bf16).astype(f32)
        out[:, at : at + LANES] = (quantized * scale).astype(bf16)


def pack_tokens_kernel(experts, capacity, chip, *refs):
    *blocks, first, second, third, fourth, by_row, by_slot = refs
    tok_dev = blocks[0].shape[0]
    rows, slots = by_row.shape
    width = first.shape[1]
    taken = slots_of(len(blocks), capacity)
    columns = jnp.concatenate([block[:, width:].astype(f32) for block in blocks], axis=0)
    lane = lax.broadcasted_iota(jnp.int32, columns.shape, 1)
    pick = lax.broadcasted_iota(jnp.int32, (rows, LANES), 1)
    gates, named = [], jnp.zeros((rows, LANES), f32)
    for number in range(len(PLANE)):
        mine = (lane % experts == (chip[0] ^ number)) & (lane < PIECES * experts)
        gates.append(jnp.sum(jnp.where(mine, columns, 0.0), axis=1, keepdims=True))
        named = jnp.where((pick == number) & (gates[-1] > 0.0), 1.0, named)
    row = lax.broadcasted_iota(jnp.int32, (rows, rows), 0)
    other = lax.broadcasted_iota(jnp.int32, (rows, rows), 1)
    earlier = (row // tok_dev == other // tok_dev) & (other < row)
    earlier = jnp.where(earlier, 1.0, 0.0).astype(bf16)
    counts = jnp.dot(earlier, named.astype(bf16), preferred_element_type=f32)
    slot = lax.broadcasted_iota(jnp.int32, (rows, slots), 1)
    start = lax.broadcasted_iota(jnp.int32, (rows, 1), 0) // tok_dev * capacity
    weights = jnp.zeros((rows, slots), f32)
    for number, gate in enumerate(gates):
        count = jnp.sum(jnp.where(pick == number, counts, 0.0), axis=1, keepdims=True)
        place = number * taken + start + count.astype(jnp.int32)
        weights = jnp.where(slot == place, gate, weights)
    by_row[...] = weights
    by_slot[...] = weights.T
    chosen = jnp.where(by_slot[...] > 0.0, 1.0, 0.0).astype(bf16)
    for part in column_chunks(width):
        held = jnp.concatenate([block[:, part] for block in blocks], axis=0)
        packed = jnp.dot(chosen, held, preferred_element_type=f32)
        for number, out in enumerate((first, second, third, fourth)):
            out[:, part] = packed[number * taken : (number + 1) * taken].astype(bf16)


def pack_cots_kernel(capacity, by_slot, *refs):
    *blocks, first, second, third, fourth = refs
    width = first.shape[1]
    taken = slots_of(len(blocks), capacity)
    gate = jnp.sum(by_slot[...], axis=1, keepdims=True)
    chosen = jnp.where(by_slot[...] > 0.0, 1.0, 0.0).astype(bf16)
    for part in column_chunks(width):
        held = jnp.concatenate([block[:, part] for block in blocks], axis=0)
        packed = gate * jnp.dot(chosen, held, preferred_element_type=f32)
        for number, out in enumerate((first, second, third, fourth)):
            out[:, part] = packed[number * taken : (number + 1) * taken].astype(bf16)


def slots_of(blocks, capacity):
    return blocks * capacity


def joined(refs, part, height, kind=bf16):
    taken = [ref[:, part].astype(f32) for ref in refs]
    rest = height - sum(value.shape[0] for value in taken)
    if rest:
        taken.append(jnp.zeros((rest, taken[0].shape[1]), f32))
    return jnp.concatenate(taken, axis=0).astype(kind)


def unpack_kernel(weighted, by_row, first, second, third, fourth, *outs):
    rows, slots = by_row.shape
    tok_dev = outs[0].shape[0]
    if weighted:
        matrices, rest = [], by_row[...]
        for _ in range(PIECES):
            matrices.append(rest.astype(bf16))
            rest = rest - matrices[-1].astype(f32)
    else:
        matrices = [jnp.where(by_row[...] > 0.0, 1.0, 0.0).astype(bf16)]
    for part in column_chunks(first.shape[1]):
        packed = joined((first, second, third, fourth), part, slots)
        total = jnp.dot(matrices[0], packed, preferred_element_type=f32)
        for matrix in matrices[1:]:
            total = total + jnp.dot(matrix, packed, preferred_element_type=f32)
        for number, out in enumerate(outs):
            out[:, part] = total[number * tok_dev : (number + 1) * tok_dev].astype(bf16)


def sum_kernel(*refs):
    *blocks, out = refs
    for part in column_chunks(out.shape[1]):
        total = blocks[0][:, part].astype(f32)
        for block in blocks[1:]:
            total = total + block[:, part].astype(f32)
        out[:, part] = total.astype(bf16)


def forward_kernel(tile, x0, x1, x2, x3, *refs):
    *slabs, o0, o1, o2, o3, for_up, for_gate, x, hidden, into, back, sems = refs
    rows, width = x.shape
    units = back.shape[0] // 2
    chunk, tiles, chunks = back_chunk(width), 2 * units // tile, width // back_chunk(width)
    triples = []
    for number in range(tiles):
        slab, at = divmod(number * tile, units)
        for half, source in enumerate(slabs[3 * slab : 3 * slab + 2]):
            place = into.at[:, pl.ds((2 * number + half) * tile, tile)]
            triples.append((source.at[0, :, pl.ds(at, tile)], place, sems.at[number]))
    for number in range(chunks):
        columns = pl.ds(number * chunk, chunk)
        for slab in range(2):
            place = back.at[pl.ds(slab * units, units), columns]
            source = slabs[3 * slab + 2].at[0, :, columns]
            triples.append((source, place, sems.at[tiles + number]))
    streams(triples)
    for part in column_chunks(width):
        x[:, part] = joined((x0, x1, x2, x3), part, rows)

    @pl.loop(0, tiles)
    def _(number):
        columns = pl.ds(pl.multiple_of(number * 2 * tile, 2 * tile), 2 * tile)
        await_place(into.at[:, columns], sems.at[number])
        pre = jnp.dot(x[...], into[:, columns], preferred_element_type=f32)
        pre_gate, pre_up = pre[:, :tile], pre[:, tile:]
        sigma = jax.nn.sigmoid(pre_gate)
        activated = pre_gate * sigma
        at = pl.ds(pl.multiple_of(number * tile, tile), tile)
        hidden[:, at] = (activated * pre_up).astype(bf16)
        for_up[:, at] = activated
        for_gate[:, at] = pre_up * sigma * (1.0 + pre_gate * (1.0 - sigma))

    @pl.loop(0, chunks)
    def _(number):
        part = pl.ds(pl.multiple_of(number * chunk, chunk), chunk)
        await_place(back.at[:, part], sems.at[tiles + number])
        total = jnp.dot(hidden[...], back[:, part], preferred_element_type=f32)
        store_packed(total, (o0, o1, o2, o3), part)


def store_packed(total, outs, at):
    taken = outs[0].shape[0]
    for number, out in enumerate(outs):
        out[:, at] = total[number * taken : (number + 1) * taken].astype(bf16)


def backward_kernel(x0, x1, x2, x3, for_up, for_gate, *refs):
    *slabs, o0, o1, o2, o3, x, grads, into, back, sems = refs
    rows, width = x.shape
    units = back.shape[0] // 2
    chunk, chunks = back_chunk(width), width // back_chunk(width)
    triples = []
    for slab in range(2):
        place = back.at[pl.ds(slab * units, units)]
        triples.append((slabs[3 * slab + 2].at[0], place, sems.at[slab]))
    for number in range(chunks):
        lines = pl.ds(number * chunk, chunk)
        for column, matrix in enumerate((0, 1, 3, 4)):
            place = into.at[lines, pl.ds(column * units, units)]
            triples.append((slabs[matrix].at[0, lines], place, sems.at[2 + number]))
    streams(triples)
    for part in column_chunks(width):
        x[:, part] = joined((x0, x1, x2, x3), part, rows)

    @pl.loop(0, 2)
    def _(slab):
        at = pl.ds(pl.multiple_of(slab * units, units), units)
        await_place(back.at[at], sems.at[slab])
        hidden_grad = lax.dot_general(x[...], back[at], CONTRACT_COLS, preferred_element_type=f32)
        start = pl.multiple_of(2 * slab * units, 2 * units)
        gate_at, up_at = pl.ds(start, units), pl.ds(start + units, units)
        grads[:, gate_at] = (hidden_grad * for_gate[:, at]).astype(bf16)
        grads[:, up_at] = (hidden_grad * for_up[:, at]).astype(bf16)

    @pl.loop(0, chunks)
    def _(number):
        part = pl.ds(pl.multiple_of(number * chunk, chunk), chunk)
        await_place(into.at[part], sems.at[2 + number])
        total = lax.dot_general(
            grads[...], into[part], CONTRACT_COLS, preferred_element_type=f32
        )
        store_packed(total, (o0, o1, o2, o3), part)


def on_device(tokens, expert_ids, gate_values, cotangent, gate_weight, up_weight, down_weight):
    tok_dev, top = expert_ids.shape
    width, hidden = gate_weight.shape[1:]
    devices = lax.axis_size("expert")
    experts = devices // 2
    capacity = min(tok_dev, tok_dev * top * 5 // (4 * experts))
    far = range(FAR, devices, FAR)
    blocks = devices // FAR
    taken = slots_of(blocks, capacity)
    rows, slots = blocks * tok_dev, padded(len(PLANE) * taken)
    chip = (lax.axis_index("expert") // 2).reshape(1).astype(jnp.int32)
    shape = jax.ShapeDtypeStruct
    packed_shapes = [shape((taken, width), bf16)] * len(PLANE)

    own = (gate_weight, up_weight, down_weight)
    other = tuple(swap(slab, CORE) for slab in own)

    in_place = pl.BlockSpec(memory_space=pltpu.HBM)
    (coded,) = call(
        functools.partial(code_kernel, experts),
        [shape((tok_dev, width + padded(PIECES * experts)), bf16)],
        (tokens, expert_ids.T, gate_values.T),
    )
    held, offset = {0: coded}, devices // 2
    while offset >= FAR:
        held.update({at ^ offset: swap(value, offset) for at, value in held.items()})
        offset //= 2
    held = [held[at] for at in sorted(held)]

    whole = pl.BlockSpec(memory_space=pltpu.VMEM)
    *packed, by_row, by_slot = call(
        functools.partial(pack_tokens_kernel, experts, capacity),
        packed_shapes + [shape((rows, slots), f32), shape((slots, rows), f32)],
        (chip, *held),
        in_specs=[pl.BlockSpec(memory_space=pltpu.SMEM)] + [whole] * blocks,
        flops=2 * rows * slots * width,
    )
    far_cots = swap(after(cotangent, held[blocks // 2], other[0]), devices // 2)
    packed = [after(value, *other[:2]) for value in packed]
    packed[-1] = after(packed[-1], far_cots)
    x = [packed[0]] + [swap(value, offset) for value, offset in zip(packed[1:], PLANE[1:])]

    cots, offset = {0: cotangent, blocks // 2: far_cots}, devices // 4
    while offset >= FAR:
        wait = other[2] if offset == FAR else cotangent
        ready = {at: after(value, wait) for at, value in cots.items()}
        cots.update({at ^ offset // FAR: swap(value, offset) for at, value in ready.items()})
        offset //= 2
    cots = [cots[at] for at in sorted(cots)]

    packed = call(
        functools.partial(pack_cots_kernel, capacity),
        packed_shapes,
        (by_slot, *cots),
        flops=2 * rows * slots * width,
    )
    grads = [packed[0]] + [swap(value, offset) for value, offset in zip(packed[1:], PLANE[1:])]

    all_taken = len(PLANE) * taken
    tile = hidden
    tiles, chunks = 2 * hidden // tile, width // back_chunk(width)
    slab_room = [pltpu.VMEM((width, 4 * hidden), bf16), pltpu.VMEM((2 * hidden, width), bf16)]
    flops = 2 * 3 * all_taken * width * 2 * hidden
    *outs, for_up, for_gate = call(
        functools.partial(forward_kernel, tile),
        packed_shapes + [shape((all_taken, 2 * hidden), f32)] * 2,
        (*x, *own, *other),
        flops=flops,
        in_specs=[whole] * 4 + [in_place] * 6,
        limit=VMEM_LIMIT_EXPERT,
        scratch=[
            pltpu.VMEM((all_taken, width), bf16),
            pltpu.VMEM((all_taken, 2 * hidden), bf16),
            *slab_room,
            pltpu.SemaphoreType.DMA((tiles + chunks,)),
        ],
    )

    def go_home(values, weighted):
        back = [values[0]] + [swap(value, offset) for value, offset in zip(values[1:], PLANE[1:])]
        sums = call(
            functools.partial(unpack_kernel, weighted),
            [shape((tok_dev, width), bf16)] * blocks,
            (by_row, *back),
            flops=2 * rows * slots * width * (PIECES if weighted else 1),
        )
        home = [sums[0]] + [swap(value, offset) for value, offset in zip(sums[1:], far)]
        (result,) = call(sum_kernel, [shape((tok_dev, width), bf16)], home)
        return result

    layer_out = go_home(outs, True)
    backs = call(
        backward_kernel,
        packed_shapes,
        (*grads, for_up, for_gate, *own, *other),
        flops=flops,
        in_specs=[whole] * 6 + [in_place] * 6,
        limit=VMEM_LIMIT_EXPERT,
        scratch=[
            pltpu.VMEM((all_taken, width), bf16),
            pltpu.VMEM((all_taken, 4 * hidden), bf16),
            *slab_room,
            pltpu.SemaphoreType.DMA((2 + chunks,)),
        ],
    )
    token_grad = go_home(backs, False)
    return layer_out, token_grad


def solution(mesh):
    rows = P(("groups", "expert"), None)
    slabs = P("expert", None, None)
    return jax.shard_map(
        on_device,
        mesh=mesh,
        in_specs=(rows, rows, rows, rows, slabs, slabs, slabs),
        out_specs=(rows, rows),
        check_vma=False,
    )
```

```python
import functools
import math

import jax
import jax.numpy as jnp
from jax import lax
from jax.experimental import pallas as pl
from jax.experimental.pallas import tpu as pltpu
from jax.sharding import PartitionSpec as P

CORE, PLANE, FAR = 1, (0, 2, 4, 6), 8
f32, bf16 = jnp.float32, jnp.bfloat16
CONTRACT_COLS = (((1,), (1,)), ((), ()))
LANES = 128
PIECES = 3
VMEM_LIMIT = 16 * 1024 * 1024


def swap(value, offset):
    devices = lax.axis_size("expert")
    return lax.ppermute(value, "expert", [(i, i ^ offset) for i in range(devices)])


def after(value, *others):
    return lax.optimization_barrier((value, *others))[0]


def padded(count):
    return -(-count // LANES) * LANES


def chunk_of(width):
    return 512 if width % 512 == 0 else LANES


def back_chunk(width):
    return width // 2 if width % (2 * LANES) == 0 else LANES


def column_chunks(width):
    return [slice(at, at + chunk_of(width)) for at in range(0, width, chunk_of(width))]


def call(body, outs, args, flops=0, scratch=(), in_specs=None, limit=VMEM_LIMIT):
    size = sum(math.prod(a.shape) * a.dtype.itemsize for a in (*args, *outs))
    whole = pl.BlockSpec(memory_space=pltpu.VMEM)
    return pl.pallas_call(
        body,
        out_shape=outs,
        in_specs=[whole] * len(args) if in_specs is None else in_specs,
        out_specs=[whole] * len(outs),
        scratch_shapes=scratch,
        compiler_params=pltpu.CompilerParams(vmem_limit_bytes=limit),
        cost_estimate=pl.CostEstimate(flops=flops, bytes_accessed=size, transcendentals=0),
    )(*args)


def code_kernel(experts, tokens, ids, gates, out):
    rows, width = tokens.shape
    gate_width = out.shape[1] - width
    line = lax.broadcasted_iota(jnp.int32, (gate_width, rows), 0)
    rest = jnp.zeros(line.shape, f32)
    for k in range(ids.shape[0]):
        rest = jnp.where(ids[k : k + 1] == line % experts, gates[k : k + 1], rest)
    columns = jnp.zeros(line.shape, f32)
    for number in range(PIECES):
        piece = rest.astype(bf16).astype(f32)
        columns = jnp.where(line // experts == number, piece, columns)
        rest = rest - piece
    out[:, width:] = columns.T.astype(bf16)
    for at in range(0, width, LANES):
        block = tokens[:, at : at + LANES].astype(f32)
        scale = jnp.max(jnp.abs(block), axis=1, keepdims=True) + 1e-06
        scale = scale.astype(bf16).astype(f32)
        quantized = (block / scale).astype(bf16).astype(f32)
        out[:, at : at + LANES] = (quantized * scale).astype(bf16)


def pack_tokens_kernel(experts, capacity, chip, *refs):
    *blocks, first, second, third, fourth, by_row, by_slot = refs
    tok_dev = blocks[0].shape[0]
    rows, slots = by_row.shape
    width = first.shape[1]
    taken = slots_of(len(blocks), capacity)
    columns = jnp.concatenate([block[:, width:].astype(f32) for block in blocks], axis=0)
    lane = lax.broadcasted_iota(jnp.int32, columns.shape, 1)
    pick = lax.broadcasted_iota(jnp.int32, (rows, LANES), 1)
    gates, named = [], jnp.zeros((rows, LANES), f32)
    for number in range(len(PLANE)):
        mine = (lane % experts == (chip[0] ^ number)) & (lane < PIECES * experts)
        gates.append(jnp.sum(jnp.where(mine, columns, 0.0), axis=1, keepdims=True))
        named = jnp.where((pick == number) & (gates[-1] > 0.0), 1.0, named)
    row = lax.broadcasted_iota(jnp.int32, (rows, rows), 0)
    other = lax.broadcasted_iota(jnp.int32, (rows, rows), 1)
    earlier = (row // tok_dev == other // tok_dev) & (other < row)
    earlier = jnp.where(earlier, 1.0, 0.0).astype(bf16)
    counts = jnp.dot(earlier, named.astype(bf16), preferred_element_type=f32)
    slot = lax.broadcasted_iota(jnp.int32, (rows, slots), 1)
    start = lax.broadcasted_iota(jnp.int32, (rows, 1), 0) // tok_dev * capacity
    weights = jnp.zeros((rows, slots), f32)
    for number, gate in enumerate(gates):
        count = jnp.sum(jnp.where(pick == number, counts, 0.0), axis=1, keepdims=True)
        place = number * taken + start + count.astype(jnp.int32)
        weights = jnp.where(slot == place, gate, weights)
    by_row[...] = weights
    by_slot[...] = weights.T
    chosen = jnp.where(by_slot[...] > 0.0, 1.0, 0.0).astype(bf16)
    for part in column_chunks(width):
        held = jnp.concatenate([block[:, part] for block in blocks], axis=0)
        packed = jnp.dot(chosen, held, preferred_element_type=f32)
        for number, out in enumerate((first, second, third, fourth)):
            out[:, part] = packed[number * taken : (number + 1) * taken].astype(bf16)


def pack_cots_kernel(capacity, by_slot, *refs):
    *blocks, first, second, third, fourth = refs
    width = first.shape[1]
    taken = slots_of(len(blocks), capacity)
    gate = jnp.sum(by_slot[...], axis=1, keepdims=True)
    chosen = jnp.where(by_slot[...] > 0.0, 1.0, 0.0).astype(bf16)
    for part in column_chunks(width):
        held = jnp.concatenate([block[:, part] for block in blocks], axis=0)
        packed = gate * jnp.dot(chosen, held, preferred_element_type=f32)
        for number, out in enumerate((first, second, third, fourth)):
            out[:, part] = packed[number * taken : (number + 1) * taken].astype(bf16)


def slots_of(blocks, capacity):
    return blocks * capacity


def joined(refs, part, height, kind=bf16):
    taken = [ref[:, part].astype(f32) for ref in refs]
    rest = height - sum(value.shape[0] for value in taken)
    if rest:
        taken.append(jnp.zeros((rest, taken[0].shape[1]), f32))
    return jnp.concatenate(taken, axis=0).astype(kind)


def unpack_kernel(weighted, by_row, first, second, third, fourth, *outs):
    rows, slots = by_row.shape
    tok_dev = outs[0].shape[0]
    if weighted:
        matrices, rest = [], by_row[...]
        for _ in range(PIECES):
            matrices.append(rest.astype(bf16))
            rest = rest - matrices[-1].astype(f32)
    else:
        matrices = [jnp.where(by_row[...] > 0.0, 1.0, 0.0).astype(bf16)]
    for part in column_chunks(first.shape[1]):
        packed = joined((first, second, third, fourth), part, slots)
        total = jnp.dot(matrices[0], packed, preferred_element_type=f32)
        for matrix in matrices[1:]:
            total = total + jnp.dot(matrix, packed, preferred_element_type=f32)
        for number, out in enumerate(outs):
            out[:, part] = total[number * tok_dev : (number + 1) * tok_dev].astype(bf16)


def sum_kernel(*refs):
    *blocks, out = refs
    for part in column_chunks(out.shape[1]):
        total = blocks[0][:, part].astype(f32)
        for block in blocks[1:]:
            total = total + block[:, part].astype(f32)
        out[:, part] = total.astype(bf16)


def join_kernel(x0, x1, x2, x3, out):
    for part in column_chunks(out.shape[1]):
        out[:, part] = joined((x0, x1, x2, x3), part, out.shape[0])


def forward(x, slabs):
    kept, total = [], 0.0
    for gate_w, up_w, down_w in slabs:
        pre_gate = jnp.dot(x, gate_w[0], preferred_element_type=f32)
        pre_up = jnp.dot(x, up_w[0], preferred_element_type=f32)
        sigma = jax.nn.sigmoid(pre_gate)
        activated = pre_gate * sigma
        kept.append((activated, pre_up * sigma * (1.0 + pre_gate * (1.0 - sigma))))
        hidden = (activated * pre_up).astype(bf16)
        total = total + jnp.dot(hidden, down_w[0], preferred_element_type=f32)
    return total.astype(bf16), kept


def backward(cots, kept, slabs):
    total = 0.0
    for (for_up, for_gate), (gate_w, up_w, down_w) in zip(kept, slabs):
        hidden_grad = lax.dot_general(cots, down_w[0], CONTRACT_COLS, preferred_element_type=f32)
        for grad, weight in ((hidden_grad * for_gate, gate_w), (hidden_grad * for_up, up_w)):
            total = total + lax.dot_general(
                grad.astype(bf16), weight[0], CONTRACT_COLS, preferred_element_type=f32
            )
    return total.astype(bf16)


def on_device(tokens, expert_ids, gate_values, cotangent, gate_weight, up_weight, down_weight):
    tok_dev, top = expert_ids.shape
    width, hidden = gate_weight.shape[1:]
    devices = lax.axis_size("expert")
    experts = devices // 2
    capacity = min(tok_dev, tok_dev * top * 5 // (4 * experts))
    far = range(FAR, devices, FAR)
    blocks = devices // FAR
    taken = slots_of(blocks, capacity)
    rows, slots = blocks * tok_dev, padded(len(PLANE) * taken)
    chip = (lax.axis_index("expert") // 2).reshape(1).astype(jnp.int32)
    shape = jax.ShapeDtypeStruct
    packed_shapes = [shape((taken, width), bf16)] * len(PLANE)

    own = (gate_weight, up_weight, down_weight)
    other = tuple(swap(slab, CORE) for slab in own)

    (coded,) = call(
        functools.partial(code_kernel, experts),
        [shape((tok_dev, width + padded(PIECES * experts)), bf16)],
        (tokens, expert_ids.T, gate_values.T),
    )
    held, offset = {0: coded}, devices // 2
    while offset >= FAR:
        held.update({at ^ offset: swap(value, offset) for at, value in held.items()})
        offset //= 2
    held = [held[at] for at in sorted(held)]

    whole = pl.BlockSpec(memory_space=pltpu.VMEM)
    *packed, by_row, by_slot = call(
        functools.partial(pack_tokens_kernel, experts, capacity),
        packed_shapes + [shape((rows, slots), f32), shape((slots, rows), f32)],
        (chip, *held),
        in_specs=[pl.BlockSpec(memory_space=pltpu.SMEM)] + [whole] * blocks,
        flops=2 * rows * slots * width,
    )
    far_cots = swap(after(cotangent, held[blocks // 2], other[0]), devices // 2)
    packed = [after(value, *other[:2]) for value in packed]
    packed[-1] = after(packed[-1], far_cots)
    x = [packed[0]] + [swap(value, offset) for value, offset in zip(packed[1:], PLANE[1:])]

    cots, offset = {0: cotangent, blocks // 2: far_cots}, devices // 4
    while offset >= FAR:
        wait = other[2] if offset == FAR else cotangent
        ready = {at: after(value, wait) for at, value in cots.items()}
        cots.update({at ^ offset // FAR: swap(value, offset) for at, value in ready.items()})
        offset //= 2
    cots = [cots[at] for at in sorted(cots)]

    packed = call(
        functools.partial(pack_cots_kernel, capacity),
        packed_shapes,
        (by_slot, *cots),
        flops=2 * rows * slots * width,
    )
    grads = [packed[0]] + [swap(value, offset) for value, offset in zip(packed[1:], PLANE[1:])]

    def join(parts):
        return call(join_kernel, [shape((len(PLANE) * taken, width), bf16)], parts)[0]

    def split(total):
        return [total[at : at + taken] for at in range(0, len(PLANE) * taken, taken)]

    out, kept = forward(join(x), (other, own))
    outs = split(out)

    def go_home(values, weighted):
        back = [values[0]] + [swap(value, offset) for value, offset in zip(values[1:], PLANE[1:])]
        sums = call(
            functools.partial(unpack_kernel, weighted),
            [shape((tok_dev, width), bf16)] * blocks,
            (by_row, *back),
            flops=2 * rows * slots * width * (PIECES if weighted else 1),
        )
        home = [sums[0]] + [swap(value, offset) for value, offset in zip(sums[1:], far)]
        (result,) = call(sum_kernel, [shape((tok_dev, width), bf16)], home)
        return result

    layer_out = go_home(outs, True)
    backs = split(backward(join(grads), kept, (other, own)))
    token_grad = go_home(backs, False)
    return layer_out, token_grad


def solution(mesh):
    rows = P(("groups", "expert"), None)
    slabs = P("expert", None, None)
    return jax.shard_map(
        on_device,
        mesh=mesh,
        in_specs=(rows, rows, rows, rows, slabs, slabs, slabs),
        out_specs=(rows, rows),
        check_vma=False,
    )
```

```python
import functools
import math

import jax
import jax.numpy as jnp
from jax import lax
from jax.experimental import pallas as pl
from jax.experimental.pallas import tpu as pltpu
from jax.sharding import PartitionSpec as P

CORE, PLANE, FAR = 1, (0, 2, 4, 6), 8
f32, bf16 = jnp.float32, jnp.bfloat16
CONTRACT_COLS = (((1,), (1,)), ((), ()))
LANES = 128
PIECES = 3
VMEM_LIMIT = 16 * 1024 * 1024
VMEM_LIMIT_EXPERT = 48 * 1024 * 1024


def swap(value, offset):
    devices = lax.axis_size("expert")
    return lax.ppermute(value, "expert", [(i, i ^ offset) for i in range(devices)])


def after(value, *others):
    return lax.optimization_barrier((value, *others))[0]


def padded(count):
    return -(-count // LANES) * LANES


def chunk_of(width):
    return 512 if width % 512 == 0 else LANES


def back_chunk(width):
    return width // 2 if width % (2 * LANES) == 0 else LANES


def column_chunks(width):
    return [slice(at, at + chunk_of(width)) for at in range(0, width, chunk_of(width))]


def call(body, outs, args, flops=0, scratch=(), in_specs=None, limit=VMEM_LIMIT):
    size = sum(math.prod(a.shape) * a.dtype.itemsize for a in (*args, *outs))
    whole = pl.BlockSpec(memory_space=pltpu.VMEM)
    return pl.pallas_call(
        body,
        out_shape=outs,
        in_specs=[whole] * len(args) if in_specs is None else in_specs,
        out_specs=[whole] * len(outs),
        scratch_shapes=scratch,
        compiler_params=pltpu.CompilerParams(vmem_limit_bytes=limit),
        cost_estimate=pl.CostEstimate(flops=flops, bytes_accessed=size, transcendentals=0),
    )(*args)


def streams(triples):
    copies = [pltpu.make_async_copy(*triple) for triple in triples]
    for copy in copies:
        copy.start()
    return copies


def await_place(place, sem):
    pltpu.make_async_copy(place, place, sem).wait()


def code_kernel(experts, tokens, ids, gates, out):
    rows, width = tokens.shape
    gate_width = out.shape[1] - width
    line = lax.broadcasted_iota(jnp.int32, (gate_width, rows), 0)
    rest = jnp.zeros(line.shape, f32)
    for k in range(ids.shape[0]):
        rest = jnp.where(ids[k : k + 1] == line % experts, gates[k : k + 1], rest)
    columns = jnp.zeros(line.shape, f32)
    for number in range(PIECES):
        piece = rest.astype(bf16).astype(f32)
        columns = jnp.where(line // experts == number, piece, columns)
        rest = rest - piece
    out[:, width:] = columns.T.astype(bf16)
    for at in range(0, width, LANES):
        block = tokens[:, at : at + LANES].astype(f32)
        scale = jnp.max(jnp.abs(block), axis=1, keepdims=True) + 1e-06
        scale = scale.astype(bf16).astype(f32)
        quantized = (block / scale).astype(bf16).astype(f32)
        out[:, at : at + LANES] = (quantized * scale).astype(bf16)


def pack_tokens_kernel(experts, capacity, chip, *refs):
    *blocks, first, second, third, fourth, by_row, by_slot = refs
    tok_dev = blocks[0].shape[0]
    rows, slots = by_row.shape
    width = first.shape[1]
    taken = slots_of(len(blocks), capacity)
    columns = jnp.concatenate([block[:, width:].astype(f32) for block in blocks], axis=0)
    lane = lax.broadcasted_iota(jnp.int32, columns.shape, 1)
    pick = lax.broadcasted_iota(jnp.int32, (rows, LANES), 1)
    gates, named = [], jnp.zeros((rows, LANES), f32)
    for number in range(len(PLANE)):
        mine = (lane % experts == (chip[0] ^ number)) & (lane < PIECES * experts)
        gates.append(jnp.sum(jnp.where(mine, columns, 0.0), axis=1, keepdims=True))
        named = jnp.where((pick == number) & (gates[-1] > 0.0), 1.0, named)
    row = lax.broadcasted_iota(jnp.int32, (rows, rows), 0)
    other = lax.broadcasted_iota(jnp.int32, (rows, rows), 1)
    earlier = (row // tok_dev == other // tok_dev) & (other < row)
    earlier = jnp.where(earlier, 1.0, 0.0).astype(bf16)
    counts = jnp.dot(earlier, named.astype(bf16), preferred_element_type=f32)
    slot = lax.broadcasted_iota(jnp.int32, (rows, slots), 1)
    start = lax.broadcasted_iota(jnp.int32, (rows, 1), 0) // tok_dev * capacity
    weights = jnp.zeros((rows, slots), f32)
    for number, gate in enumerate(gates):
        count = jnp.sum(jnp.where(pick == number, counts, 0.0), axis=1, keepdims=True)
        place = number * taken + start + count.astype(jnp.int32)
        weights = jnp.where(slot == place, gate, weights)
    by_row[...] = weights
    by_slot[...] = weights.T
    chosen = jnp.where(by_slot[...] > 0.0, 1.0, 0.0).astype(bf16)
    for part in column_chunks(width):
        held = jnp.concatenate([block[:, part] for block in blocks], axis=0)
        packed = jnp.dot(chosen, held, preferred_element_type=f32)
        for number, out in enumerate((first, second, third, fourth)):
            out[:, part] = packed[number * taken : (number + 1) * taken].astype(bf16)


def pack_cots_kernel(capacity, by_slot, *refs):
    *blocks, first, second, third, fourth = refs
    width = first.shape[1]
    taken = slots_of(len(blocks), capacity)
    gate = jnp.sum(by_slot[...], axis=1, keepdims=True)
    chosen = jnp.where(by_slot[...] > 0.0, 1.0, 0.0).astype(bf16)
    for part in column_chunks(width):
        held = jnp.concatenate([block[:, part] for block in blocks], axis=0)
        packed = gate * jnp.dot(chosen, held, preferred_element_type=f32)
        for number, out in enumerate((first, second, third, fourth)):
            out[:, part] = packed[number * taken : (number + 1) * taken].astype(bf16)


def slots_of(blocks, capacity):
    return blocks * capacity


def joined(refs, part, height, kind=bf16):
    taken = [ref[:, part].astype(f32) for ref in refs]
    rest = height - sum(value.shape[0] for value in taken)
    if rest:
        taken.append(jnp.zeros((rest, taken[0].shape[1]), f32))
    return jnp.concatenate(taken, axis=0).astype(kind)


def unpack_kernel(weighted, by_row, first, second, third, fourth, *outs):
    rows, slots = by_row.shape
    tok_dev = outs[0].shape[0]
    if weighted:
        matrices, rest = [], by_row[...]
        for _ in range(PIECES):
            matrices.append(rest.astype(bf16))
            rest = rest - matrices[-1].astype(f32)
    else:
        matrices = [jnp.where(by_row[...] > 0.0, 1.0, 0.0).astype(bf16)]
    for part in column_chunks(first.shape[1]):
        packed = joined((first, second, third, fourth), part, slots)
        total = jnp.dot(matrices[0], packed, preferred_element_type=f32)
        for matrix in matrices[1:]:
            total = total + jnp.dot(matrix, packed, preferred_element_type=f32)
        for number, out in enumerate(outs):
            out[:, part] = total[number * tok_dev : (number + 1) * tok_dev].astype(bf16)


def sum_kernel(*refs):
    *blocks, out = refs
    for part in column_chunks(out.shape[1]):
        total = blocks[0][:, part].astype(f32)
        for block in blocks[1:]:
            total = total + block[:, part].astype(f32)
        out[:, part] = total.astype(bf16)


def forward_kernel(tile, x0, x1, x2, x3, *refs):
    *slabs, o0, o1, o2, o3, for_up, for_gate, x, hidden, into, back, sems = refs
    rows, width = x.shape
    units = back.shape[0] // 2
    chunk, tiles, chunks = back_chunk(width), 2 * units // tile, width // back_chunk(width)
    triples = []
    for number in range(tiles):
        slab, at = divmod(number * tile, units)
        for half, source in enumerate(slabs[3 * slab : 3 * slab + 2]):
            place = into.at[:, pl.ds((2 * number + half) * tile, tile)]
            triples.append((source.at[0, :, pl.ds(at, tile)], place, sems.at[number]))
    for number in range(chunks):
        columns = pl.ds(number * chunk, chunk)
        for slab in range(2):
            place = back.at[pl.ds(slab * units, units), columns]
            source = slabs[3 * slab + 2].at[0, :, columns]
            triples.append((source, place, sems.at[tiles + number]))
    streams(triples)
    for part in column_chunks(width):
        x[:, part] = joined((x0, x1, x2, x3), part, rows)

    @pl.loop(0, tiles)
    def _(number):
        columns = pl.ds(pl.multiple_of(number * 2 * tile, 2 * tile), 2 * tile)
        await_place(into.at[:, columns], sems.at[number])
        pre = jnp.dot(x[...], into[:, columns], preferred_element_type=f32)
        pre_gate, pre_up = pre[:, :tile], pre[:, tile:]
        sigma = jax.nn.sigmoid(pre_gate)
        activated = pre_gate * sigma
        at = pl.ds(pl.multiple_of(number * tile, tile), tile)
        hidden[:, at] = (activated * pre_up).astype(bf16)
        for_up[:, at] = activated
        for_gate[:, at] = pre_up * sigma * (1.0 + pre_gate * (1.0 - sigma))

    @pl.loop(0, chunks)
    def _(number):
        part = pl.ds(pl.multiple_of(number * chunk, chunk), chunk)
        await_place(back.at[:, part], sems.at[tiles + number])
        total = jnp.dot(hidden[...], back[:, part], preferred_element_type=f32)
        store_packed(total, (o0, o1, o2, o3), part)


def store_packed(total, outs, at):
    taken = outs[0].shape[0]
    for number, out in enumerate(outs):
        out[:, at] = total[number * taken : (number + 1) * taken].astype(bf16)


def backward_kernel(x0, x1, x2, x3, for_up, for_gate, *refs):
    *slabs, o0, o1, o2, o3, x, grads, into, back, sems = refs
    rows, width = x.shape
    units = back.shape[0] // 2
    chunk, chunks = back_chunk(width), width // back_chunk(width)
    triples = []
    for slab in range(2):
        place = back.at[pl.ds(slab * units, units)]
        triples.append((slabs[3 * slab + 2].at[0], place, sems.at[slab]))
    for number in range(chunks):
        lines = pl.ds(number * chunk, chunk)
        for column, matrix in enumerate((0, 1, 3, 4)):
            place = into.at[lines, pl.ds(column * units, units)]
            triples.append((slabs[matrix].at[0, lines], place, sems.at[2 + number]))
    streams(triples)
    for part in column_chunks(width):
        x[:, part] = joined((x0, x1, x2, x3), part, rows)

    @pl.loop(0, 2)
    def _(slab):
        at = pl.ds(pl.multiple_of(slab * units, units), units)
        await_place(back.at[at], sems.at[slab])
        hidden_grad = lax.dot_general(x[...], back[at], CONTRACT_COLS, preferred_element_type=f32)
        start = pl.multiple_of(2 * slab * units, 2 * units)
        gate_at, up_at = pl.ds(start, units), pl.ds(start + units, units)
        grads[:, gate_at] = (hidden_grad * for_gate[:, at]).astype(bf16)
        grads[:, up_at] = (hidden_grad * for_up[:, at]).astype(bf16)

    @pl.loop(0, chunks)
    def _(number):
        part = pl.ds(pl.multiple_of(number * chunk, chunk), chunk)
        await_place(into.at[part], sems.at[2 + number])
        total = lax.dot_general(
            grads[...], into[part], CONTRACT_COLS, preferred_element_type=f32
        )
        store_packed(total, (o0, o1, o2, o3), part)


def on_device(tokens, expert_ids, gate_values, cotangent, gate_weight, up_weight, down_weight):
    tok_dev, top = expert_ids.shape
    width, hidden = gate_weight.shape[1:]
    devices = lax.axis_size("expert")
    experts = devices // 2
    capacity = min(tok_dev, tok_dev * top * 5 // (4 * experts))
    far = range(FAR, devices, FAR)
    blocks = devices // FAR
    taken = slots_of(blocks, capacity)
    rows, slots = blocks * tok_dev, padded(len(PLANE) * taken)
    chip = (lax.axis_index("expert") // 2).reshape(1).astype(jnp.int32)
    shape = jax.ShapeDtypeStruct
    packed_shapes = [shape((taken, width), bf16)] * len(PLANE)

    own = (gate_weight, up_weight, down_weight)
    other = tuple(swap(slab, CORE) for slab in own)

    in_place = pl.BlockSpec(memory_space=pltpu.HBM)
    (coded,) = call(
        functools.partial(code_kernel, experts),
        [shape((tok_dev, width + padded(PIECES * experts)), bf16)],
        (tokens, expert_ids.T, gate_values.T),
    )
    held, offset = {0: coded}, devices // 2
    while offset >= FAR:
        held.update({at ^ offset: swap(value, offset) for at, value in held.items()})
        offset //= 2
    held = [held[at] for at in sorted(held)]

    whole = pl.BlockSpec(memory_space=pltpu.VMEM)
    *packed, by_row, by_slot = call(
        functools.partial(pack_tokens_kernel, experts, capacity),
        packed_shapes + [shape((rows, slots), f32), shape((slots, rows), f32)],
        (chip, *held),
        in_specs=[pl.BlockSpec(memory_space=pltpu.SMEM)] + [whole] * blocks,
        flops=2 * rows * slots * width,
    )
    ready = after(cotangent, held[blocks // 2], *other[:2])
    far_cots, near_cots = swap(ready, devices // 2), swap(ready, FAR)
    packed[2] = after(packed[2], near_cots)
    packed[3] = after(packed[3], far_cots)
    x = [packed[0]] + [swap(value, offset) for value, offset in zip(packed[1:], PLANE[1:])]

    cots, offset = {0: cotangent, blocks // 2: far_cots}, devices // 4
    while offset >= FAR:
        near = {0: near_cots} if offset == FAR else {}
        wait = other[2] if offset == FAR else cotangent
        ready = {at: after(value, wait) for at, value in cots.items() if at not in near}
        near.update({at: swap(value, offset) for at, value in ready.items()})
        cots.update({at ^ offset // FAR: value for at, value in near.items()})
        offset //= 2
    cots = [cots[at] for at in sorted(cots)]

    packed = call(
        functools.partial(pack_cots_kernel, capacity),
        packed_shapes,
        (by_slot, *cots),
        flops=2 * rows * slots * width,
    )
    grads = [packed[0]] + [swap(value, offset) for value, offset in zip(packed[1:], PLANE[1:])]

    all_taken = len(PLANE) * taken
    tile = hidden
    tiles, chunks = 2 * hidden // tile, width // back_chunk(width)
    slab_room = [pltpu.VMEM((width, 4 * hidden), bf16), pltpu.VMEM((2 * hidden, width), bf16)]
    flops = 2 * 3 * all_taken * width * 2 * hidden
    *outs, for_up, for_gate = call(
        functools.partial(forward_kernel, tile),
        packed_shapes + [shape((all_taken, 2 * hidden), f32)] * 2,
        (*x, *own, *other),
        flops=flops,
        in_specs=[whole] * 4 + [in_place] * 6,
        limit=VMEM_LIMIT_EXPERT,
        scratch=[
            pltpu.VMEM((all_taken, width), bf16),
            pltpu.VMEM((all_taken, 2 * hidden), bf16),
            *slab_room,
            pltpu.SemaphoreType.DMA((tiles + chunks,)),
        ],
    )

    def go_home(values, weighted):
        back = [values[0]] + [swap(value, offset) for value, offset in zip(values[1:], PLANE[1:])]
        sums = call(
            functools.partial(unpack_kernel, weighted),
            [shape((tok_dev, width), bf16)] * blocks,
            (by_row, *back),
            flops=2 * rows * slots * width * (PIECES if weighted else 1),
        )
        home = [sums[0]] + [swap(value, offset) for value, offset in zip(sums[1:], far)]
        (result,) = call(sum_kernel, [shape((tok_dev, width), bf16)], home)
        return result

    layer_out = go_home(outs, True)
    backs = call(
        backward_kernel,
        packed_shapes,
        (*grads, for_up, for_gate, *own, *other),
        flops=flops,
        in_specs=[whole] * 6 + [in_place] * 6,
        limit=VMEM_LIMIT_EXPERT,
        scratch=[
            pltpu.VMEM((all_taken, width), bf16),
            pltpu.VMEM((all_taken, 4 * hidden), bf16),
            *slab_room,
            pltpu.SemaphoreType.DMA((2 + chunks,)),
        ],
    )
    token_grad = go_home(backs, False)
    return layer_out, token_grad


def solution(mesh):
    rows = P(("groups", "expert"), None)
    slabs = P("expert", None, None)
    return jax.shard_map(
        on_device,
        mesh=mesh,
        in_specs=(rows, rows, rows, rows, slabs, slabs, slabs),
        out_specs=(rows, rows),
        check_vma=False,
    )
```

```python
import functools
import math

import jax
import jax.numpy as jnp
from jax import lax
from jax.experimental import pallas as pl
from jax.experimental.pallas import tpu as pltpu
from jax.sharding import PartitionSpec as P

CORE, PLANE, FAR = 1, (0, 2, 4, 6), 8
f32, bf16 = jnp.float32, jnp.bfloat16
CONTRACT_COLS = (((1,), (1,)), ((), ()))
LANES = 128
PIECES = 3
VMEM_LIMIT = 16 * 1024 * 1024
VMEM_LIMIT_EXPERT = 38 * 1024 * 1024


def swap(value, offset):
    devices = lax.axis_size("expert")
    return lax.ppermute(value, "expert", [(i, i ^ offset) for i in range(devices)])


def after(value, *others):
    return lax.optimization_barrier((value, *others))[0]


def padded(count):
    return -(-count // LANES) * LANES


def chunk_of(width):
    return 512 if width % 512 == 0 else LANES


def back_chunk(width):
    return width // 2 if width % (2 * LANES) == 0 else LANES


def column_chunks(width):
    return [slice(at, at + chunk_of(width)) for at in range(0, width, chunk_of(width))]


def call(body, outs, args, flops=0, scratch=(), in_specs=None, limit=VMEM_LIMIT):
    size = sum(math.prod(a.shape) * a.dtype.itemsize for a in (*args, *outs))
    whole = pl.BlockSpec(memory_space=pltpu.VMEM)
    return pl.pallas_call(
        body,
        out_shape=outs,
        in_specs=[whole] * len(args) if in_specs is None else in_specs,
        out_specs=[whole] * len(outs),
        scratch_shapes=scratch,
        compiler_params=pltpu.CompilerParams(vmem_limit_bytes=limit),
        cost_estimate=pl.CostEstimate(flops=flops, bytes_accessed=size, transcendentals=0),
    )(*args)


def streams(triples):
    copies = [pltpu.make_async_copy(*triple) for triple in triples]
    for copy in copies:
        copy.start()
    return copies


def await_place(place, sem):
    pltpu.make_async_copy(place, place, sem).wait()


def code_kernel(experts, tokens, ids, gates, out):
    rows, width = tokens.shape
    gate_width = out.shape[1] - width
    line = lax.broadcasted_iota(jnp.int32, (gate_width, rows), 0)
    rest = jnp.zeros(line.shape, f32)
    for k in range(ids.shape[0]):
        rest = jnp.where(ids[k : k + 1] == line % experts, gates[k : k + 1], rest)
    columns = jnp.zeros(line.shape, f32)
    for number in range(PIECES):
        piece = rest.astype(bf16).astype(f32)
        columns = jnp.where(line // experts == number, piece, columns)
        rest = rest - piece
    out[:, width:] = columns.T.astype(bf16)
    for at in range(0, width, LANES):
        block = tokens[:, at : at + LANES].astype(f32)
        scale = jnp.max(jnp.abs(block), axis=1, keepdims=True) + 1e-06
        scale = scale.astype(bf16).astype(f32)
        quantized = (block / scale).astype(bf16).astype(f32)
        out[:, at : at + LANES] = (quantized * scale).astype(bf16)


def pack_tokens_kernel(experts, capacity, chip, *refs):
    *blocks, first, second, third, fourth, by_row, by_slot = refs
    tok_dev = blocks[0].shape[0]
    rows, slots = by_row.shape
    width = first.shape[1]
    taken = slots_of(len(blocks), capacity)
    columns = jnp.concatenate([block[:, width:].astype(f32) for block in blocks], axis=0)
    lane = lax.broadcasted_iota(jnp.int32, columns.shape, 1)
    pick = lax.broadcasted_iota(jnp.int32, (rows, LANES), 1)
    gates, named = [], jnp.zeros((rows, LANES), f32)
    for number in range(len(PLANE)):
        mine = (lane % experts == (chip[0] ^ number)) & (lane < PIECES * experts)
        gates.append(jnp.sum(jnp.where(mine, columns, 0.0), axis=1, keepdims=True))
        named = jnp.where((pick == number) & (gates[-1] > 0.0), 1.0, named)
    row = lax.broadcasted_iota(jnp.int32, (rows, rows), 0)
    other = lax.broadcasted_iota(jnp.int32, (rows, rows), 1)
    earlier = (row // tok_dev == other // tok_dev) & (other < row)
    earlier = jnp.where(earlier, 1.0, 0.0).astype(bf16)
    counts = jnp.dot(earlier, named.astype(bf16), preferred_element_type=f32)
    slot = lax.broadcasted_iota(jnp.int32, (rows, slots), 1)
    start = lax.broadcasted_iota(jnp.int32, (rows, 1), 0) // tok_dev * capacity
    weights = jnp.zeros((rows, slots), f32)
    for number, gate in enumerate(gates):
        count = jnp.sum(jnp.where(pick == number, counts, 0.0), axis=1, keepdims=True)
        place = number * taken + start + count.astype(jnp.int32)
        weights = jnp.where(slot == place, gate, weights)
    by_row[...] = weights
    by_slot[...] = weights.T
    chosen = jnp.where(by_slot[...] > 0.0, 1.0, 0.0).astype(bf16)
    for part in column_chunks(width):
        held = jnp.concatenate([block[:, part] for block in blocks], axis=0)
        packed = jnp.dot(chosen, held, preferred_element_type=f32)
        for number, out in enumerate((first, second, third, fourth)):
            out[:, part] = packed[number * taken : (number + 1) * taken].astype(bf16)


def pack_cots_kernel(capacity, by_slot, *refs):
    *blocks, first, second, third, fourth = refs
    width = first.shape[1]
    taken = slots_of(len(blocks), capacity)
    gate = jnp.sum(by_slot[...], axis=1, keepdims=True)
    chosen = jnp.where(by_slot[...] > 0.0, 1.0, 0.0).astype(bf16)
    for part in column_chunks(width):
        held = jnp.concatenate([block[:, part] for block in blocks], axis=0)
        packed = gate * jnp.dot(chosen, held, preferred_element_type=f32)
        for number, out in enumerate((first, second, third, fourth)):
            out[:, part] = packed[number * taken : (number + 1) * taken].astype(bf16)


def slots_of(blocks, capacity):
    return blocks * capacity


def joined(refs, part, height, kind=bf16):
    taken = [ref[:, part].astype(f32) for ref in refs]
    rest = height - sum(value.shape[0] for value in taken)
    if rest:
        taken.append(jnp.zeros((rest, taken[0].shape[1]), f32))
    return jnp.concatenate(taken, axis=0).astype(kind)


def unpack_kernel(weighted, by_row, first, second, third, fourth, *outs):
    rows, slots = by_row.shape
    tok_dev = outs[0].shape[0]
    if weighted:
        matrices, rest = [], by_row[...]
        for _ in range(PIECES):
            matrices.append(rest.astype(bf16))
            rest = rest - matrices[-1].astype(f32)
    else:
        matrices = [jnp.where(by_row[...] > 0.0, 1.0, 0.0).astype(bf16)]
    for part in column_chunks(first.shape[1]):
        packed = joined((first, second, third, fourth), part, slots)
        total = jnp.dot(matrices[0], packed, preferred_element_type=f32)
        for matrix in matrices[1:]:
            total = total + jnp.dot(matrix, packed, preferred_element_type=f32)
        for number, out in enumerate(outs):
            out[:, part] = total[number * tok_dev : (number + 1) * tok_dev].astype(bf16)


def sum_kernel(*refs):
    *blocks, out = refs
    for part in column_chunks(out.shape[1]):
        total = blocks[0][:, part].astype(f32)
        for block in blocks[1:]:
            total = total + block[:, part].astype(f32)
        out[:, part] = total.astype(bf16)


def forward_kernel(x0, x1, x2, x3, g1, u1, d1, g0, u0, d0, *refs):
    o0, o1, o2, o3, for_up, for_gate, x, hidden, into, back, sems = refs
    rows, width = x.shape
    units = back.shape[0]
    chunk = back_chunk(width)
    streams(own_slab(g0, u0, into, sems.at[0]) + [(d0.at[0], back, sems.at[1])])
    for part in column_chunks(width):
        x[:, part] = joined((x0, x1, x2, x3), part, rows)

    def activate(pre_gate, pre_up, at):
        sigma = jax.nn.sigmoid(pre_gate)
        activated = pre_gate * sigma
        hidden[:, at] = (activated * pre_up).astype(bf16)
        for_up[:, at] = activated
        for_gate[:, at] = pre_up * sigma * (1.0 + pre_gate * (1.0 - sigma))

    pre_gate = jnp.dot(x[...], g1[0], preferred_element_type=f32)
    pre_up = jnp.dot(x[...], u1[0], preferred_element_type=f32)
    activate(pre_gate, pre_up, slice(units, 2 * units))
    await_place(into, sems.at[0])
    pre = jnp.dot(x[...], into[...], preferred_element_type=f32)
    activate(pre[:, :units], pre[:, units:], slice(0, units))
    await_place(back, sems.at[1])

    @pl.loop(0, width // chunk)
    def _(number):
        part = pl.ds(pl.multiple_of(number * chunk, chunk), chunk)
        total = jnp.dot(hidden[:, units:], d1[0, :, part], preferred_element_type=f32)
        total = total + jnp.dot(hidden[:, :units], back[:, part], preferred_element_type=f32)
        store_packed(total, (o0, o1, o2, o3), part)


def own_slab(gate_w, up_w, into, sem):
    units = gate_w.shape[2]
    places = (into.at[:, pl.ds(0, units)], into.at[:, pl.ds(units, units)])
    return [(source.at[0], place, sem) for source, place in zip((gate_w, up_w), places)]


def store_packed(total, outs, at):
    taken = outs[0].shape[0]
    for number, out in enumerate(outs):
        out[:, at] = total[number * taken : (number + 1) * taken].astype(bf16)


def backward_kernel(x0, x1, x2, x3, for_up, for_gate, g1, u1, d1, g0, u0, d0, *refs):
    o0, o1, o2, o3, x, grads, into, back, sems = refs
    rows, width = x.shape
    units = back.shape[0]
    chunk = back_chunk(width)
    streams([(d0.at[0], back, sems.at[1])] + own_slab(g0, u0, into, sems.at[0]))
    for part in column_chunks(width):
        x[:, part] = joined((x0, x1, x2, x3), part, rows)

    def transposed(left, right):
        return lax.dot_general(left, right, CONTRACT_COLS, preferred_element_type=f32)

    def differentiate(down_w, slab):
        at, start = slice(slab * units, (slab + 1) * units), 2 * slab * units
        hidden_grad = transposed(x[...], down_w)
        grads[:, start : start + units] = (hidden_grad * for_gate[:, at]).astype(bf16)
        grads[:, start + units : start + 2 * units] = (hidden_grad * for_up[:, at]).astype(bf16)

    differentiate(d1[0], 1)
    await_place(back, sems.at[1])
    differentiate(back[...], 0)
    await_place(into, sems.at[0])

    @pl.loop(0, width // chunk)
    def _(number):
        part = pl.ds(pl.multiple_of(number * chunk, chunk), chunk)
        total = transposed(grads[:, : 2 * units], into[part])
        total = total + transposed(grads[:, 2 * units : 3 * units], g1[0, part])
        total = total + transposed(grads[:, 3 * units :], u1[0, part])
        store_packed(total, (o0, o1, o2, o3), part)


def on_device(tokens, expert_ids, gate_values, cotangent, gate_weight, up_weight, down_weight):
    tok_dev, top = expert_ids.shape
    width, hidden = gate_weight.shape[1:]
    devices = lax.axis_size("expert")
    experts = devices // 2
    capacity = min(tok_dev, tok_dev * top * 5 // (4 * experts))
    far = range(FAR, devices, FAR)
    blocks = devices // FAR
    taken = slots_of(blocks, capacity)
    rows, slots = blocks * tok_dev, padded(len(PLANE) * taken)
    chip = (lax.axis_index("expert") // 2).reshape(1).astype(jnp.int32)
    shape = jax.ShapeDtypeStruct
    packed_shapes = [shape((taken, width), bf16)] * len(PLANE)

    own = (gate_weight, up_weight, down_weight)
    other = tuple(swap(slab, CORE) for slab in own)

    in_place = pl.BlockSpec(memory_space=pltpu.HBM)
    (coded,) = call(
        functools.partial(code_kernel, experts),
        [shape((tok_dev, width + padded(PIECES * experts)), bf16)],
        (tokens, expert_ids.T, gate_values.T),
    )
    held, offset = {0: coded}, devices // 2
    while offset >= FAR:
        held.update({at ^ offset: swap(value, offset) for at, value in held.items()})
        offset //= 2
    held = [held[at] for at in sorted(held)]

    whole = pl.BlockSpec(memory_space=pltpu.VMEM)
    *packed, by_row, by_slot = call(
        functools.partial(pack_tokens_kernel, experts, capacity),
        packed_shapes + [shape((rows, slots), f32), shape((slots, rows), f32)],
        (chip, *held),
        in_specs=[pl.BlockSpec(memory_space=pltpu.SMEM)] + [whole] * blocks,
        flops=2 * rows * slots * width,
    )
    far_cots = swap(after(cotangent, held[blocks // 2], other[0]), devices // 2)
    packed = [after(value, *other[:2]) for value in packed]
    packed[-1] = after(packed[-1], far_cots)
    x = [packed[0]] + [swap(value, offset) for value, offset in zip(packed[1:], PLANE[1:])]

    cots, offset = {0: cotangent, blocks // 2: far_cots}, devices // 4
    while offset >= FAR:
        wait = other[2] if offset == FAR else cotangent
        ready = {at: after(value, wait) for at, value in cots.items()}
        cots.update({at ^ offset // FAR: swap(value, offset) for at, value in ready.items()})
        offset //= 2
    cots = [cots[at] for at in sorted(cots)]

    packed = call(
        functools.partial(pack_cots_kernel, capacity),
        packed_shapes,
        (by_slot, *cots),
        flops=2 * rows * slots * width,
    )
    grads = [packed[0]] + [swap(value, offset) for value, offset in zip(packed[1:], PLANE[1:])]

    all_taken = len(PLANE) * taken
    slab_room = [
        pltpu.VMEM((width, 2 * hidden), bf16),
        pltpu.VMEM((hidden, width), bf16),
        pltpu.SemaphoreType.DMA((2,)),
    ]
    flops = 2 * 3 * all_taken * width * 2 * hidden
    *outs, for_up, for_gate = call(
        forward_kernel,
        packed_shapes + [shape((all_taken, 2 * hidden), f32)] * 2,
        (*x, *other, *own),
        flops=flops,
        in_specs=[whole] * 7 + [in_place] * 3,
        limit=VMEM_LIMIT_EXPERT,
        scratch=[
            pltpu.VMEM((all_taken, width), bf16),
            pltpu.VMEM((all_taken, 2 * hidden), bf16),
            *slab_room,
        ],
    )

    def go_home(values, weighted):
        back = [values[0]] + [swap(value, offset) for value, offset in zip(values[1:], PLANE[1:])]
        sums = call(
            functools.partial(unpack_kernel, weighted),
            [shape((tok_dev, width), bf16)] * blocks,
            (by_row, *back),
            flops=2 * rows * slots * width * (PIECES if weighted else 1),
        )
        home = [sums[0]] + [swap(value, offset) for value, offset in zip(sums[1:], far)]
        (result,) = call(sum_kernel, [shape((tok_dev, width), bf16)], home)
        return result

    layer_out = go_home(outs, True)
    backs = call(
        backward_kernel,
        packed_shapes,
        (*grads, for_up, for_gate, *other, *own),
        flops=flops,
        in_specs=[whole] * 9 + [in_place] * 3,
        limit=VMEM_LIMIT_EXPERT,
        scratch=[
            pltpu.VMEM((all_taken, width), bf16),
            pltpu.VMEM((all_taken, 4 * hidden), bf16),
            *slab_room,
        ],
    )
    token_grad = go_home(backs, False)
    return layer_out, token_grad


def solution(mesh):
    rows = P(("groups", "expert"), None)
    slabs = P("expert", None, None)
    return jax.shard_map(
        on_device,
        mesh=mesh,
        in_specs=(rows, rows, rows, rows, slabs, slabs, slabs),
        out_specs=(rows, rows),
        check_vma=False,
    )
```

```python
import functools
import math

import jax
import jax.numpy as jnp
from jax import lax
from jax.experimental import pallas as pl
from jax.experimental.pallas import tpu as pltpu
from jax.sharding import PartitionSpec as P

CORE, PLANE, FAR = 1, (0, 2, 4, 6), 8
f32, bf16 = jnp.float32, jnp.bfloat16
CONTRACT_COLS = (((1,), (1,)), ((), ()))
LANES = 128
PIECES = 3
VMEM_LIMIT = 16 * 1024 * 1024
VMEM_LIMIT_EXPERT = 38 * 1024 * 1024


def swap(value, offset):
    devices = lax.axis_size("expert")
    return lax.ppermute(value, "expert", [(i, i ^ offset) for i in range(devices)])


def after(value, *others):
    return lax.optimization_barrier((value, *others))[0]


def padded(count):
    return -(-count // LANES) * LANES


def chunk_of(width):
    return 512 if width % 512 == 0 else LANES


def column_chunks(width):
    return [slice(at, at + chunk_of(width)) for at in range(0, width, chunk_of(width))]


def call(body, outs, args, flops=0, scratch=(), in_specs=None, limit=VMEM_LIMIT):
    size = sum(math.prod(a.shape) * a.dtype.itemsize for a in (*args, *outs))
    whole = pl.BlockSpec(memory_space=pltpu.VMEM)
    return pl.pallas_call(
        body,
        out_shape=outs,
        in_specs=[whole] * len(args) if in_specs is None else in_specs,
        out_specs=[whole] * len(outs),
        scratch_shapes=scratch,
        compiler_params=pltpu.CompilerParams(vmem_limit_bytes=limit),
        cost_estimate=pl.CostEstimate(flops=flops, bytes_accessed=size, transcendentals=0),
    )(*args)


def streams(triples):
    copies = [pltpu.make_async_copy(*triple) for triple in triples]
    for copy in copies:
        copy.start()
    return copies


def await_place(place, sem):
    pltpu.make_async_copy(place, place, sem).wait()


def code_kernel(experts, tokens, ids, gates, out):
    rows, width = tokens.shape
    gate_width = out.shape[1] - width
    line = lax.broadcasted_iota(jnp.int32, (gate_width, rows), 0)
    rest = jnp.zeros(line.shape, f32)
    for k in range(ids.shape[0]):
        rest = jnp.where(ids[k : k + 1] == line % experts, gates[k : k + 1], rest)
    columns = jnp.zeros(line.shape, f32)
    for number in range(PIECES):
        piece = rest.astype(bf16).astype(f32)
        columns = jnp.where(line // experts == number, piece, columns)
        rest = rest - piece
    out[:, width:] = columns.T.astype(bf16)
    for at in range(0, width, LANES):
        block = tokens[:, at : at + LANES].astype(f32)
        scale = jnp.max(jnp.abs(block), axis=1, keepdims=True) + 1e-06
        scale = scale.astype(bf16).astype(f32)
        quantized = (block / scale).astype(bf16).astype(f32)
        out[:, at : at + LANES] = (quantized * scale).astype(bf16)


def pack_tokens_kernel(experts, capacity, chip, *refs):
    *blocks, first, second, third, fourth, by_row, by_slot = refs
    tok_dev = blocks[0].shape[0]
    rows, slots = by_row.shape
    width = first.shape[1]
    taken = slots_of(len(blocks), capacity)
    columns = jnp.concatenate([block[:, width:].astype(f32) for block in blocks], axis=0)
    lane = lax.broadcasted_iota(jnp.int32, columns.shape, 1)
    pick = lax.broadcasted_iota(jnp.int32, (rows, LANES), 1)
    gates, named = [], jnp.zeros((rows, LANES), f32)
    for number in range(len(PLANE)):
        mine = (lane % experts == (chip[0] ^ number)) & (lane < PIECES * experts)
        gates.append(jnp.sum(jnp.where(mine, columns, 0.0), axis=1, keepdims=True))
        named = jnp.where((pick == number) & (gates[-1] > 0.0), 1.0, named)
    row = lax.broadcasted_iota(jnp.int32, (rows, rows), 0)
    other = lax.broadcasted_iota(jnp.int32, (rows, rows), 1)
    earlier = (row // tok_dev == other // tok_dev) & (other < row)
    earlier = jnp.where(earlier, 1.0, 0.0).astype(bf16)
    counts = jnp.dot(earlier, named.astype(bf16), preferred_element_type=f32)
    slot = lax.broadcasted_iota(jnp.int32, (rows, slots), 1)
    start = lax.broadcasted_iota(jnp.int32, (rows, 1), 0) // tok_dev * capacity
    weights = jnp.zeros((rows, slots), f32)
    for number, gate in enumerate(gates):
        count = jnp.sum(jnp.where(pick == number, counts, 0.0), axis=1, keepdims=True)
        place = number * taken + start + count.astype(jnp.int32)
        weights = jnp.where(slot == place, gate, weights)
    by_row[...] = weights
    by_slot[...] = weights.T
    chosen = jnp.where(by_slot[...] > 0.0, 1.0, 0.0).astype(bf16)
    for part in column_chunks(width):
        held = jnp.concatenate([block[:, part] for block in blocks], axis=0)
        packed = jnp.dot(chosen, held, preferred_element_type=f32)
        for number, out in enumerate((first, second, third, fourth)):
            out[:, part] = packed[number * taken : (number + 1) * taken].astype(bf16)


def pack_cots_kernel(capacity, by_slot, *refs):
    *blocks, first, second, third, fourth = refs
    width = first.shape[1]
    taken = slots_of(len(blocks), capacity)
    gate = jnp.sum(by_slot[...], axis=1, keepdims=True)
    chosen = jnp.where(by_slot[...] > 0.0, 1.0, 0.0).astype(bf16)
    for part in column_chunks(width):
        held = jnp.concatenate([block[:, part] for block in blocks], axis=0)
        packed = gate * jnp.dot(chosen, held, preferred_element_type=f32)
        for number, out in enumerate((first, second, third, fourth)):
            out[:, part] = packed[number * taken : (number + 1) * taken].astype(bf16)


def slots_of(blocks, capacity):
    return blocks * capacity


def joined(refs, part, height, kind=bf16):
    taken = [ref[:, part].astype(f32) for ref in refs]
    rest = height - sum(value.shape[0] for value in taken)
    if rest:
        taken.append(jnp.zeros((rest, taken[0].shape[1]), f32))
    return jnp.concatenate(taken, axis=0).astype(kind)


def unpack_kernel(weighted, by_row, first, second, third, fourth, *outs):
    rows, slots = by_row.shape
    tok_dev = outs[0].shape[0]
    if weighted:
        matrices, rest = [], by_row[...]
        for _ in range(PIECES):
            matrices.append(rest.astype(bf16))
            rest = rest - matrices[-1].astype(f32)
    else:
        matrices = [jnp.where(by_row[...] > 0.0, 1.0, 0.0).astype(bf16)]
    for part in column_chunks(first.shape[1]):
        packed = joined((first, second, third, fourth), part, slots)
        total = jnp.dot(matrices[0], packed, preferred_element_type=f32)
        for matrix in matrices[1:]:
            total = total + jnp.dot(matrix, packed, preferred_element_type=f32)
        for number, out in enumerate(outs):
            out[:, part] = total[number * tok_dev : (number + 1) * tok_dev].astype(bf16)


def sum_kernel(*refs):
    *blocks, out = refs
    for part in column_chunks(out.shape[1]):
        total = blocks[0][:, part].astype(f32)
        for block in blocks[1:]:
            total = total + block[:, part].astype(f32)
        out[:, part] = total.astype(bf16)


def forward_kernel(x0, x1, x2, x3, g1, u1, d1, g0, u0, d0, *refs):
    o0, o1, o2, o3, for_up, for_gate, x, hidden, pre, into, back, sems = refs
    rows, width = x.shape
    units = back.shape[0]
    chunk = chunk_of(width)
    streams(own_slab(g0, u0, into, sems.at[0]) + [(d0.at[0], back, sems.at[1])])
    for part in column_chunks(width):
        x[:, part] = joined((x0, x1, x2, x3), part, rows)

    def activate(at):
        pre_gate, pre_up = pre[:, :units], pre[:, units:]
        sigma = jax.nn.sigmoid(pre_gate)
        activated = pre_gate * sigma
        hidden[:, at] = (activated * pre_up).astype(bf16)
        for_up[:, at] = activated
        for_gate[:, at] = pre_up * sigma * (1.0 + pre_gate * (1.0 - sigma))

    def contract(left, right):
        return jnp.dot(left, right, preferred_element_type=f32)

    def project(dots):
        pre[...] = jnp.zeros_like(pre)

        @pl.loop(0, width // chunk)
        def _(number):
            part = pl.ds(pl.multiple_of(number * chunk, chunk), chunk)
            dots(x[:, part], part)

    def other_slab(rows_part, part):
        pre[:, :units] += contract(rows_part, g1[0, part])
        pre[:, units:] += contract(rows_part, u1[0, part])

    def this_slab(rows_part, part):
        pre[:, :units] += contract(rows_part, into[part, :units])
        pre[:, units:] += contract(rows_part, into[part, units:])

    project(other_slab)
    activate(slice(units, 2 * units))
    await_place(into, sems.at[0])
    project(this_slab)
    activate(slice(0, units))
    await_place(back, sems.at[1])

    @pl.loop(0, width // chunk)
    def _(number):
        part = pl.ds(pl.multiple_of(number * chunk, chunk), chunk)
        total = jnp.dot(hidden[:, units:], d1[0, :, part], preferred_element_type=f32)
        total = total + jnp.dot(hidden[:, :units], back[:, part], preferred_element_type=f32)
        store_packed(total, (o0, o1, o2, o3), part)


def own_slab(gate_w, up_w, into, sem):
    units = gate_w.shape[2]
    places = (into.at[:, pl.ds(0, units)], into.at[:, pl.ds(units, units)])
    return [(source.at[0], place, sem) for source, place in zip((gate_w, up_w), places)]


def store_packed(total, outs, at):
    taken = outs[0].shape[0]
    for number, out in enumerate(outs):
        out[:, at] = total[number * taken : (number + 1) * taken].astype(bf16)


def backward_kernel(x0, x1, x2, x3, for_up, for_gate, g1, u1, d1, g0, u0, d0, *refs):
    o0, o1, o2, o3, x, grads, hidden_grad, into, back, sems = refs
    rows, width = x.shape
    units = back.shape[0]
    chunk = chunk_of(width)
    streams([(d0.at[0], back, sems.at[1])] + own_slab(g0, u0, into, sems.at[0]))
    for part in column_chunks(width):
        x[:, part] = joined((x0, x1, x2, x3), part, rows)

    def transposed(left, right):
        return lax.dot_general(left, right, CONTRACT_COLS, preferred_element_type=f32)

    def differentiate(down_at, slab):
        at, start = slice(slab * units, (slab + 1) * units), 2 * slab * units
        hidden_grad[...] = jnp.zeros_like(hidden_grad)

        @pl.loop(0, width // chunk)
        def _(number):
            part = pl.ds(pl.multiple_of(number * chunk, chunk), chunk)
            hidden_grad[...] += transposed(x[:, part], down_at(part))

        wide = hidden_grad[...]
        grads[:, start : start + units] = (wide * for_gate[:, at]).astype(bf16)
        grads[:, start + units : start + 2 * units] = (wide * for_up[:, at]).astype(bf16)

    differentiate(lambda part: d1[0, :, part], 1)
    await_place(back, sems.at[1])
    differentiate(lambda part: back[:, part], 0)
    await_place(into, sems.at[0])

    @pl.loop(0, width // chunk)
    def _(number):
        part = pl.ds(pl.multiple_of(number * chunk, chunk), chunk)
        total = transposed(grads[:, : 2 * units], into[part])
        total = total + transposed(grads[:, 2 * units : 3 * units], g1[0, part])
        total = total + transposed(grads[:, 3 * units :], u1[0, part])
        store_packed(total, (o0, o1, o2, o3), part)


def on_device(tokens, expert_ids, gate_values, cotangent, gate_weight, up_weight, down_weight):
    tok_dev, top = expert_ids.shape
    width, hidden = gate_weight.shape[1:]
    devices = lax.axis_size("expert")
    experts = devices // 2
    capacity = min(tok_dev, tok_dev * top * 5 // (4 * experts))
    far = range(FAR, devices, FAR)
    blocks = devices // FAR
    taken = slots_of(blocks, capacity)
    rows, slots = blocks * tok_dev, padded(len(PLANE) * taken)
    chip = (lax.axis_index("expert") // 2).reshape(1).astype(jnp.int32)
    shape = jax.ShapeDtypeStruct
    packed_shapes = [shape((taken, width), bf16)] * len(PLANE)

    own = (gate_weight, up_weight, down_weight)
    other = tuple(swap(slab, CORE) for slab in own)

    in_place = pl.BlockSpec(memory_space=pltpu.HBM)
    (coded,) = call(
        functools.partial(code_kernel, experts),
        [shape((tok_dev, width + padded(PIECES * experts)), bf16)],
        (tokens, expert_ids.T, gate_values.T),
    )
    held, offset = {0: coded}, devices // 2
    while offset >= FAR:
        held.update({at ^ offset: swap(value, offset) for at, value in held.items()})
        offset //= 2
    held = [held[at] for at in sorted(held)]

    whole = pl.BlockSpec(memory_space=pltpu.VMEM)
    *packed, by_row, by_slot = call(
        functools.partial(pack_tokens_kernel, experts, capacity),
        packed_shapes + [shape((rows, slots), f32), shape((slots, rows), f32)],
        (chip, *held),
        in_specs=[pl.BlockSpec(memory_space=pltpu.SMEM)] + [whole] * blocks,
        flops=2 * rows * slots * width,
    )
    far_cots = swap(after(cotangent, held[blocks // 2], other[0]), devices // 2)
    packed = [after(value, *other[:2]) for value in packed]
    packed[-1] = after(packed[-1], far_cots)
    x = [packed[0]] + [swap(value, offset) for value, offset in zip(packed[1:], PLANE[1:])]

    cots, offset = {0: cotangent, blocks // 2: far_cots}, devices // 4
    while offset >= FAR:
        wait = other[2] if offset == FAR else cotangent
        ready = {at: after(value, wait) for at, value in cots.items()}
        cots.update({at ^ offset // FAR: swap(value, offset) for at, value in ready.items()})
        offset //= 2
    cots = [cots[at] for at in sorted(cots)]

    packed = call(
        functools.partial(pack_cots_kernel, capacity),
        packed_shapes,
        (by_slot, *cots),
        flops=2 * rows * slots * width,
    )
    grads = [packed[0]] + [swap(value, offset) for value, offset in zip(packed[1:], PLANE[1:])]

    all_taken = len(PLANE) * taken
    slab_room = [
        pltpu.VMEM((width, 2 * hidden), bf16),
        pltpu.VMEM((hidden, width), bf16),
        pltpu.SemaphoreType.DMA((2,)),
    ]
    flops = 2 * 3 * all_taken * width * 2 * hidden
    *outs, for_up, for_gate = call(
        forward_kernel,
        packed_shapes + [shape((all_taken, 2 * hidden), f32)] * 2,
        (*x, *other, *own),
        flops=flops,
        in_specs=[whole] * 7 + [in_place] * 3,
        limit=VMEM_LIMIT_EXPERT,
        scratch=[
            pltpu.VMEM((all_taken, width), bf16),
            pltpu.VMEM((all_taken, 2 * hidden), bf16),
            pltpu.VMEM((all_taken, 2 * hidden), f32),
            *slab_room,
        ],
    )

    def go_home(values, weighted):
        back = [values[0]] + [swap(value, offset) for value, offset in zip(values[1:], PLANE[1:])]
        sums = call(
            functools.partial(unpack_kernel, weighted),
            [shape((tok_dev, width), bf16)] * blocks,
            (by_row, *back),
            flops=2 * rows * slots * width * (PIECES if weighted else 1),
        )
        home = [sums[0]] + [swap(value, offset) for value, offset in zip(sums[1:], far)]
        (result,) = call(sum_kernel, [shape((tok_dev, width), bf16)], home)
        return result

    layer_out = go_home(outs, True)
    backs = call(
        backward_kernel,
        packed_shapes,
        (*grads, for_up, for_gate, *other, *own),
        flops=flops,
        in_specs=[whole] * 9 + [in_place] * 3,
        limit=VMEM_LIMIT_EXPERT,
        scratch=[
            pltpu.VMEM((all_taken, width), bf16),
            pltpu.VMEM((all_taken, 4 * hidden), bf16),
            pltpu.VMEM((all_taken, hidden), f32),
            *slab_room,
        ],
    )
    token_grad = go_home(backs, False)
    return layer_out, token_grad


def solution(mesh):
    rows = P(("groups", "expert"), None)
    slabs = P("expert", None, None)
    return jax.shard_map(
        on_device,
        mesh=mesh,
        in_specs=(rows, rows, rows, rows, slabs, slabs, slabs),
        out_specs=(rows, rows),
        check_vma=False,
    )
```

```python
import functools
import math

import jax
import jax.numpy as jnp
from jax import lax
from jax.experimental import pallas as pl
from jax.experimental.pallas import tpu as pltpu
from jax.sharding import PartitionSpec as P

CORE, PLANE, FAR = 1, (0, 2, 4, 6), 8
f32, bf16 = jnp.float32, jnp.bfloat16
CONTRACT_COLS = (((1,), (1,)), ((), ()))
LANES = 128
PIECES = 3
VMEM_LIMIT = 16 * 1024 * 1024
VMEM_LIMIT_EXPERT = 48 * 1024 * 1024


def swap(value, offset):
    devices = lax.axis_size("expert")
    return lax.ppermute(value, "expert", [(i, i ^ offset) for i in range(devices)])


def after(value, *others):
    return lax.optimization_barrier((value, *others))[0]


def padded(count):
    return -(-count // LANES) * LANES


def chunk_of(width):
    return 512 if width % 512 == 0 else LANES


def back_chunk(width):
    return width // 2 if width % (2 * LANES) == 0 else LANES


def column_chunks(width):
    return [slice(at, at + chunk_of(width)) for at in range(0, width, chunk_of(width))]


def call(body, outs, args, flops=0, scratch=(), in_specs=None, limit=VMEM_LIMIT):
    size = sum(math.prod(a.shape) * a.dtype.itemsize for a in (*args, *outs))
    whole = pl.BlockSpec(memory_space=pltpu.VMEM)
    return pl.pallas_call(
        body,
        out_shape=outs,
        in_specs=[whole] * len(args) if in_specs is None else in_specs,
        out_specs=[whole] * len(outs),
        scratch_shapes=scratch,
        compiler_params=pltpu.CompilerParams(vmem_limit_bytes=limit),
        cost_estimate=pl.CostEstimate(flops=flops, bytes_accessed=size, transcendentals=0),
    )(*args)


def streams(triples):
    copies = [pltpu.make_async_copy(*triple) for triple in triples]
    for copy in copies:
        copy.start()
    return copies


def await_place(place, sem):
    pltpu.make_async_copy(place, place, sem).wait()


def code_kernel(experts, tokens, ids, gates, out):
    rows, width = tokens.shape
    gate_width = out.shape[1] - width
    line = lax.broadcasted_iota(jnp.int32, (gate_width, rows), 0)
    rest = jnp.zeros(line.shape, f32)
    for k in range(ids.shape[0]):
        rest = jnp.where(ids[k : k + 1] == line % experts, gates[k : k + 1], rest)
    columns = jnp.zeros(line.shape, f32)
    for number in range(PIECES):
        piece = rest.astype(bf16).astype(f32)
        columns = jnp.where(line // experts == number, piece, columns)
        rest = rest - piece
    out[:, width:] = columns.T.astype(bf16)
    for at in range(0, width, LANES):
        block = tokens[:, at : at + LANES].astype(f32)
        scale = jnp.max(jnp.abs(block), axis=1, keepdims=True) + 1e-06
        scale = scale.astype(bf16).astype(f32)
        quantized = (block / scale).astype(bf16).astype(f32)
        out[:, at : at + LANES] = (quantized * scale).astype(bf16)


def pack_tokens_kernel(experts, capacity, chip, *refs):
    *blocks, first, second, third, fourth, by_row, by_slot = refs
    tok_dev = blocks[0].shape[0]
    rows, slots = by_row.shape
    width = first.shape[1]
    taken = slots_of(len(blocks), capacity)
    columns = jnp.concatenate([block[:, width:].astype(f32) for block in blocks], axis=0)
    lane = lax.broadcasted_iota(jnp.int32, columns.shape, 1)
    pick = lax.broadcasted_iota(jnp.int32, (rows, LANES), 1)
    gates, named = [], jnp.zeros((rows, LANES), f32)
    for number in range(len(PLANE)):
        mine = (lane % experts == (chip[0] ^ number)) & (lane < PIECES * experts)
        gates.append(jnp.sum(jnp.where(mine, columns, 0.0), axis=1, keepdims=True))
        named = jnp.where((pick == number) & (gates[-1] > 0.0), 1.0, named)
    row = lax.broadcasted_iota(jnp.int32, (rows, rows), 0)
    other = lax.broadcasted_iota(jnp.int32, (rows, rows), 1)
    earlier = (row // tok_dev == other // tok_dev) & (other < row)
    earlier = jnp.where(earlier, 1.0, 0.0).astype(bf16)
    counts = jnp.dot(earlier, named.astype(bf16), preferred_element_type=f32)
    slot = lax.broadcasted_iota(jnp.int32, (rows, slots), 1)
    start = lax.broadcasted_iota(jnp.int32, (rows, 1), 0) // tok_dev * capacity
    weights = jnp.zeros((rows, slots), f32)
    for number, gate in enumerate(gates):
        count = jnp.sum(jnp.where(pick == number, counts, 0.0), axis=1, keepdims=True)
        place = number * taken + start + count.astype(jnp.int32)
        weights = jnp.where(slot == place, gate, weights)
    by_row[...] = weights
    by_slot[...] = weights.T
    chosen = jnp.where(by_slot[...] > 0.0, 1.0, 0.0).astype(bf16)
    for part in column_chunks(width):
        held = jnp.concatenate([block[:, part] for block in blocks], axis=0)
        packed = jnp.dot(chosen, held, preferred_element_type=f32)
        for number, out in enumerate((first, second, third, fourth)):
            out[:, part] = packed[number * taken : (number + 1) * taken].astype(bf16)


def pack_cots_kernel(capacity, by_slot, *refs):
    *blocks, first, second, third, fourth = refs
    width = first.shape[1]
    taken = slots_of(len(blocks), capacity)
    gate = jnp.sum(by_slot[...], axis=1, keepdims=True)
    chosen = jnp.where(by_slot[...] > 0.0, 1.0, 0.0).astype(bf16)
    for part in column_chunks(width):
        held = jnp.concatenate([block[:, part] for block in blocks], axis=0)
        packed = gate * jnp.dot(chosen, held, preferred_element_type=f32)
        for number, out in enumerate((first, second, third, fourth)):
            out[:, part] = packed[number * taken : (number + 1) * taken].astype(bf16)


def slots_of(blocks, capacity):
    return blocks * capacity


def joined(refs, part, height, kind=bf16):
    taken = [ref[:, part].astype(f32) for ref in refs]
    rest = height - sum(value.shape[0] for value in taken)
    if rest:
        taken.append(jnp.zeros((rest, taken[0].shape[1]), f32))
    return jnp.concatenate(taken, axis=0).astype(kind)


def unpack_kernel(weighted, by_row, first, second, third, fourth, *outs):
    rows, slots = by_row.shape
    tok_dev = outs[0].shape[0]
    if weighted:
        matrices, rest = [], by_row[...]
        for _ in range(PIECES):
            matrices.append(rest.astype(bf16))
            rest = rest - matrices[-1].astype(f32)
    else:
        matrices = [jnp.where(by_row[...] > 0.0, 1.0, 0.0).astype(bf16)]
    for part in column_chunks(first.shape[1]):
        packed = joined((first, second, third, fourth), part, slots)
        total = jnp.dot(matrices[0], packed, preferred_element_type=f32)
        for matrix in matrices[1:]:
            total = total + jnp.dot(matrix, packed, preferred_element_type=f32)
        for number, out in enumerate(outs):
            out[:, part] = total[number * tok_dev : (number + 1) * tok_dev].astype(bf16)


def sum_kernel(*refs):
    *blocks, out = refs
    for part in column_chunks(out.shape[1]):
        total = blocks[0][:, part].astype(f32)
        for block in blocks[1:]:
            total = total + block[:, part].astype(f32)
        out[:, part] = total.astype(bf16)


def forward_kernel(tile, x0, x1, x2, x3, *refs):
    *slabs, o0, o1, o2, o3, for_up, for_gate, x, hidden, into, back, sems = refs
    rows, width = x.shape
    units = back.shape[0] // 2
    chunk, tiles, chunks = back_chunk(width), 2 * units // tile, width // back_chunk(width)
    triples = []
    for number in range(tiles):
        slab, at = divmod(number * tile, units)
        for half, source in enumerate(slabs[3 * slab : 3 * slab + 2]):
            place = into.at[:, pl.ds((2 * number + half) * tile, tile)]
            triples.append((source.at[0, :, pl.ds(at, tile)], place, sems.at[number]))
    for number in range(chunks):
        columns = pl.ds(number * chunk, chunk)
        for slab in range(2):
            place = back.at[pl.ds(slab * units, units), columns]
            source = slabs[3 * slab + 2].at[0, :, columns]
            triples.append((source, place, sems.at[tiles + number]))
    streams(triples)
    for part in column_chunks(width):
        x[:, part] = joined((x0, x1, x2, x3), part, rows)

    @pl.loop(0, tiles)
    def _(number):
        columns = pl.ds(pl.multiple_of(number * 2 * tile, 2 * tile), 2 * tile)
        await_place(into.at[:, columns], sems.at[number])
        pre = jnp.dot(x[...], into[:, columns], preferred_element_type=f32)
        pre_gate, pre_up = pre[:, :tile], pre[:, tile:]
        sigma = jax.nn.sigmoid(pre_gate)
        activated = pre_gate * sigma
        at = pl.ds(pl.multiple_of(number * tile, tile), tile)
        hidden[:, at] = (activated * pre_up).astype(bf16)
        for_up[:, at] = activated
        for_gate[:, at] = pre_up * sigma * (1.0 + pre_gate * (1.0 - sigma))

    @pl.loop(0, chunks)
    def _(number):
        part = pl.ds(pl.multiple_of(number * chunk, chunk), chunk)
        await_place(back.at[:, part], sems.at[tiles + number])
        total = jnp.dot(hidden[...], back[:, part], preferred_element_type=f32)
        store_packed(total, (o0, o1, o2, o3), part)


def store_packed(total, outs, at):
    taken = outs[0].shape[0]
    for number, out in enumerate(outs):
        out[:, at] = total[number * taken : (number + 1) * taken].astype(bf16)


def backward_kernel(x0, x1, x2, x3, for_up, for_gate, *refs):
    *slabs, o0, o1, o2, o3, x, grads, into, back, sems = refs
    rows, width = x.shape
    units = back.shape[0] // 2
    chunk, chunks = back_chunk(width), width // back_chunk(width)
    triples = []
    for slab in range(2):
        place = back.at[pl.ds(slab * units, units)]
        triples.append((slabs[3 * slab + 2].at[0], place, sems.at[0]))
    for number in range(chunks):
        lines = pl.ds(number * chunk, chunk)
        for column, matrix in enumerate((0, 1, 3, 4)):
            place = into.at[lines, pl.ds(column * units, units)]
            triples.append((slabs[matrix].at[0, lines], place, sems.at[1 + number]))
    streams(triples)
    for part in column_chunks(width):
        x[:, part] = joined((x0, x1, x2, x3), part, rows)

    await_place(back, sems.at[0])
    hidden_grad = lax.dot_general(x[...], back[...], CONTRACT_COLS, preferred_element_type=f32)
    for slab in range(2):
        at = slice(slab * units, (slab + 1) * units)
        start = 2 * slab * units
        grads[:, start : start + units] = (hidden_grad[:, at] * for_gate[:, at]).astype(bf16)
        up_at = slice(start + units, start + 2 * units)
        grads[:, up_at] = (hidden_grad[:, at] * for_up[:, at]).astype(bf16)

    @pl.loop(0, chunks)
    def _(number):
        part = pl.ds(pl.multiple_of(number * chunk, chunk), chunk)
        await_place(into.at[part], sems.at[1 + number])
        total = lax.dot_general(
            grads[...], into[part], CONTRACT_COLS, preferred_element_type=f32
        )
        store_packed(total, (o0, o1, o2, o3), part)


def on_device(tokens, expert_ids, gate_values, cotangent, gate_weight, up_weight, down_weight):
    tok_dev, top = expert_ids.shape
    width, hidden = gate_weight.shape[1:]
    devices = lax.axis_size("expert")
    experts = devices // 2
    capacity = min(tok_dev, tok_dev * top * 5 // (4 * experts))
    far = range(FAR, devices, FAR)
    blocks = devices // FAR
    taken = slots_of(blocks, capacity)
    rows, slots = blocks * tok_dev, padded(len(PLANE) * taken)
    chip = (lax.axis_index("expert") // 2).reshape(1).astype(jnp.int32)
    shape = jax.ShapeDtypeStruct
    packed_shapes = [shape((taken, width), bf16)] * len(PLANE)

    own = (gate_weight, up_weight, down_weight)
    other = tuple(swap(slab, CORE) for slab in own)

    in_place = pl.BlockSpec(memory_space=pltpu.HBM)
    (coded,) = call(
        functools.partial(code_kernel, experts),
        [shape((tok_dev, width + padded(PIECES * experts)), bf16)],
        (tokens, expert_ids.T, gate_values.T),
    )
    held, offset = {0: coded}, devices // 2
    while offset >= FAR:
        held.update({at ^ offset: swap(value, offset) for at, value in held.items()})
        offset //= 2
    held = [held[at] for at in sorted(held)]

    whole = pl.BlockSpec(memory_space=pltpu.VMEM)
    *packed, by_row, by_slot = call(
        functools.partial(pack_tokens_kernel, experts, capacity),
        packed_shapes + [shape((rows, slots), f32), shape((slots, rows), f32)],
        (chip, *held),
        in_specs=[pl.BlockSpec(memory_space=pltpu.SMEM)] + [whole] * blocks,
        flops=2 * rows * slots * width,
    )
    far_cots = swap(after(cotangent, held[blocks // 2], other[0]), devices // 2)
    packed = [after(value, *other[:2]) for value in packed]
    packed[-1] = after(packed[-1], far_cots)
    x = [packed[0]] + [swap(value, offset) for value, offset in zip(packed[1:], PLANE[1:])]

    cots, offset = {0: cotangent, blocks // 2: far_cots}, devices // 4
    while offset >= FAR:
        wait = other[2] if offset == FAR else cotangent
        ready = {at: after(value, wait) for at, value in cots.items()}
        cots.update({at ^ offset // FAR: swap(value, offset) for at, value in ready.items()})
        offset //= 2
    cots = [cots[at] for at in sorted(cots)]

    packed = call(
        functools.partial(pack_cots_kernel, capacity),
        packed_shapes,
        (by_slot, *cots),
        flops=2 * rows * slots * width,
    )
    grads = [packed[0]] + [swap(value, offset) for value, offset in zip(packed[1:], PLANE[1:])]

    all_taken = len(PLANE) * taken
    tile = hidden
    tiles, chunks = 2 * hidden // tile, width // back_chunk(width)
    slab_room = [pltpu.VMEM((width, 4 * hidden), bf16), pltpu.VMEM((2 * hidden, width), bf16)]
    flops = 2 * 3 * all_taken * width * 2 * hidden
    *outs, for_up, for_gate = call(
        functools.partial(forward_kernel, tile),
        packed_shapes + [shape((all_taken, 2 * hidden), f32)] * 2,
        (*x, *own, *other),
        flops=flops,
        in_specs=[whole] * 4 + [in_place] * 6,
        limit=VMEM_LIMIT_EXPERT,
        scratch=[
            pltpu.VMEM((all_taken, width), bf16),
            pltpu.VMEM((all_taken, 2 * hidden), bf16),
            *slab_room,
            pltpu.SemaphoreType.DMA((tiles + chunks,)),
        ],
    )

    def go_home(values, weighted):
        back = [values[0]] + [swap(value, offset) for value, offset in zip(values[1:], PLANE[1:])]
        sums = call(
            functools.partial(unpack_kernel, weighted),
            [shape((tok_dev, width), bf16)] * blocks,
            (by_row, *back),
            flops=2 * rows * slots * width * (PIECES if weighted else 1),
        )
        home = [sums[0]] + [swap(value, offset) for value, offset in zip(sums[1:], far)]
        (result,) = call(sum_kernel, [shape((tok_dev, width), bf16)], home)
        return result

    layer_out = go_home(outs, True)
    backs = call(
        backward_kernel,
        packed_shapes,
        (*grads, for_up, for_gate, *own, *other),
        flops=flops,
        in_specs=[whole] * 6 + [in_place] * 6,
        limit=VMEM_LIMIT_EXPERT,
        scratch=[
            pltpu.VMEM((all_taken, width), bf16),
            pltpu.VMEM((all_taken, 4 * hidden), bf16),
            *slab_room,
            pltpu.SemaphoreType.DMA((1 + chunks,)),
        ],
    )
    token_grad = go_home(backs, False)
    return layer_out, token_grad


def solution(mesh):
    rows = P(("groups", "expert"), None)
    slabs = P("expert", None, None)
    return jax.shard_map(
        on_device,
        mesh=mesh,
        in_specs=(rows, rows, rows, rows, slabs, slabs, slabs),
        out_specs=(rows, rows),
        check_vma=False,
    )
```

```python
import functools
import math

import jax
import jax.numpy as jnp
from jax import lax
from jax.experimental import pallas as pl
from jax.experimental.pallas import tpu as pltpu
from jax.sharding import PartitionSpec as P

CORE, PLANE, FAR = 1, (0, 2, 4, 6), 8
f32, bf16 = jnp.float32, jnp.bfloat16
CONTRACT_COLS = (((1,), (1,)), ((), ()))
LANES = 128
PIECES = 3
VMEM_LIMIT = 16 * 1024 * 1024
VMEM_LIMIT_EXPERT = 48 * 1024 * 1024


def swap(value, offset):
    devices = lax.axis_size("expert")
    return lax.ppermute(value, "expert", [(i, i ^ offset) for i in range(devices)])


def after(value, *others):
    return lax.optimization_barrier((value, *others))[0]


def padded(count):
    return -(-count // LANES) * LANES


def chunk_of(width):
    return 512 if width % 512 == 0 else LANES


def back_chunk(width):
    return width // 2 if width % (2 * LANES) == 0 else LANES


def column_chunks(width):
    return [slice(at, at + chunk_of(width)) for at in range(0, width, chunk_of(width))]


def call(body, outs, args, flops=0, scratch=(), in_specs=None, limit=VMEM_LIMIT):
    size = sum(math.prod(a.shape) * a.dtype.itemsize for a in (*args, *outs))
    whole = pl.BlockSpec(memory_space=pltpu.VMEM)
    return pl.pallas_call(
        body,
        out_shape=outs,
        in_specs=[whole] * len(args) if in_specs is None else in_specs,
        out_specs=[whole] * len(outs),
        scratch_shapes=scratch,
        compiler_params=pltpu.CompilerParams(vmem_limit_bytes=limit),
        cost_estimate=pl.CostEstimate(flops=flops, bytes_accessed=size, transcendentals=0),
    )(*args)


def streams(triples):
    for triple in triples:
        pltpu.make_async_copy(*triple).start()


def await_place(place, sem):
    pltpu.make_async_copy(place, place, sem).wait()


def code_kernel(experts, tokens, ids, gates, out):
    rows, width = tokens.shape
    gate_width = out.shape[1] - width
    line = lax.broadcasted_iota(jnp.int32, (gate_width, rows), 0)
    rest = jnp.zeros(line.shape, f32)
    for k in range(ids.shape[0]):
        rest = jnp.where(ids[k : k + 1] == line % experts, gates[k : k + 1], rest)
    columns = jnp.zeros(line.shape, f32)
    for number in range(PIECES):
        piece = rest.astype(bf16).astype(f32)
        columns = jnp.where(line // experts == number, piece, columns)
        rest = rest - piece
    out[:, width:] = columns.T.astype(bf16)
    for at in range(0, width, LANES):
        block = tokens[:, at : at + LANES].astype(f32)
        scale = jnp.max(jnp.abs(block), axis=1, keepdims=True) + 1e-06
        scale = scale.astype(bf16).astype(f32)
        quantized = (block / scale).astype(bf16).astype(f32)
        out[:, at : at + LANES] = (quantized * scale).astype(bf16)


def pack_tokens_kernel(experts, capacity, chip, *refs):
    *blocks, first, second, third, fourth, by_row, by_slot = refs
    tok_dev = blocks[0].shape[0]
    rows, slots = by_row.shape
    width = first.shape[1]
    taken = slots_of(len(blocks), capacity)
    columns = jnp.concatenate([block[:, width:].astype(f32) for block in blocks], axis=0)
    lane = lax.broadcasted_iota(jnp.int32, columns.shape, 1)
    pick = lax.broadcasted_iota(jnp.int32, (rows, LANES), 1)
    gates, named = [], jnp.zeros((rows, LANES), f32)
    for number in range(len(PLANE)):
        mine = (lane % experts == (chip[0] ^ number)) & (lane < PIECES * experts)
        gates.append(jnp.sum(jnp.where(mine, columns, 0.0), axis=1, keepdims=True))
        named = jnp.where((pick == number) & (gates[-1] > 0.0), 1.0, named)
    row = lax.broadcasted_iota(jnp.int32, (rows, rows), 0)
    other = lax.broadcasted_iota(jnp.int32, (rows, rows), 1)
    earlier = (row // tok_dev == other // tok_dev) & (other < row)
    earlier = jnp.where(earlier, 1.0, 0.0).astype(bf16)
    counts = jnp.dot(earlier, named.astype(bf16), preferred_element_type=f32)
    slot = lax.broadcasted_iota(jnp.int32, (rows, slots), 1)
    start = lax.broadcasted_iota(jnp.int32, (rows, 1), 0) // tok_dev * capacity
    weights = jnp.zeros((rows, slots), f32)
    for number, gate in enumerate(gates):
        count = jnp.sum(jnp.where(pick == number, counts, 0.0), axis=1, keepdims=True)
        place = number * taken + start + count.astype(jnp.int32)
        weights = jnp.where(slot == place, gate, weights)
    by_row[...] = weights
    by_slot[...] = weights.T
    chosen = jnp.where(by_slot[...] > 0.0, 1.0, 0.0).astype(bf16)
    for part in column_chunks(width):
        held = jnp.concatenate([block[:, part] for block in blocks], axis=0)
        packed = jnp.dot(chosen, held, preferred_element_type=f32)
        for number, out in enumerate((first, second, third, fourth)):
            out[:, part] = packed[number * taken : (number + 1) * taken].astype(bf16)


def pack_cots_kernel(capacity, by_slot, *refs):
    *blocks, first, second, third, fourth = refs
    width = first.shape[1]
    taken = slots_of(len(blocks), capacity)
    gate = jnp.sum(by_slot[...], axis=1, keepdims=True)
    chosen = jnp.where(by_slot[...] > 0.0, 1.0, 0.0).astype(bf16)
    for part in column_chunks(width):
        held = jnp.concatenate([block[:, part] for block in blocks], axis=0)
        packed = gate * jnp.dot(chosen, held, preferred_element_type=f32)
        for number, out in enumerate((first, second, third, fourth)):
            out[:, part] = packed[number * taken : (number + 1) * taken].astype(bf16)


def slots_of(blocks, capacity):
    return blocks * capacity


def joined(refs, part, height, kind=bf16):
    taken = [ref[:, part].astype(f32) for ref in refs]
    rest = height - sum(value.shape[0] for value in taken)
    if rest:
        taken.append(jnp.zeros((rest, taken[0].shape[1]), f32))
    return jnp.concatenate(taken, axis=0).astype(kind)


def unpack_kernel(weighted, by_row, first, second, third, fourth, *outs):
    rows, slots = by_row.shape
    tok_dev = outs[0].shape[0]
    if weighted:
        matrices, rest = [], by_row[...]
        for _ in range(PIECES):
            matrices.append(rest.astype(bf16))
            rest = rest - matrices[-1].astype(f32)
    else:
        matrices = [jnp.where(by_row[...] > 0.0, 1.0, 0.0).astype(bf16)]
    for part in column_chunks(first.shape[1]):
        packed = joined((first, second, third, fourth), part, slots)
        total = jnp.dot(matrices[0], packed, preferred_element_type=f32)
        for matrix in matrices[1:]:
            total = total + jnp.dot(matrix, packed, preferred_element_type=f32)
        for number, out in enumerate(outs):
            out[:, part] = total[number * tok_dev : (number + 1) * tok_dev].astype(bf16)


def sum_kernel(*refs):
    *blocks, out = refs
    for part in column_chunks(out.shape[1]):
        total = blocks[0][:, part].astype(f32)
        for block in blocks[1:]:
            total = total + block[:, part].astype(f32)
        out[:, part] = total.astype(bf16)


def forward_kernel(tile, x0, x1, x2, x3, *refs):
    *slabs, o0, o1, o2, o3, for_up, for_gate, x, hidden, into, back, sems = refs
    rows, width = x.shape
    units = back.shape[0] // 2
    chunk, tiles, chunks = back_chunk(width), 2 * units // tile, width // back_chunk(width)
    triples, later = [], []
    for number in range(tiles):
        slab, at = divmod(number * tile, units)
        for half, source in enumerate(slabs[3 * slab : 3 * slab + 2]):
            place = into.at[:, pl.ds((2 * number + half) * tile, tile)]
            triples.append((source.at[0, :, pl.ds(at, tile)], place, sems.at[number]))
    for number in range(chunks):
        columns = pl.ds(number * chunk, chunk)
        for slab in range(2):
            place = back.at[pl.ds(slab * units, units), columns]
            source = slabs[3 * slab + 2].at[0, :, columns]
            later.append((source, place, sems.at[tiles + number]))
    streams(triples[:2])
    for part in column_chunks(width):
        x[:, part] = joined((x0, x1, x2, x3), part, rows)
    streams(triples[2:])

    @pl.loop(0, tiles)
    def _(number):
        columns = pl.ds(pl.multiple_of(number * 2 * tile, 2 * tile), 2 * tile)
        await_place(into.at[:, columns], sems.at[number])

        @pl.when(number == 0)
        def _():
            streams(later)

        pre = jnp.dot(x[...], into[:, columns], preferred_element_type=f32)
        pre_gate, pre_up = pre[:, :tile], pre[:, tile:]
        sigma = jax.nn.sigmoid(pre_gate)
        activated = pre_gate * sigma
        at = pl.ds(pl.multiple_of(number * tile, tile), tile)
        hidden[:, at] = (activated * pre_up).astype(bf16)
        for_up[:, at] = activated
        for_gate[:, at] = pre_up * sigma * (1.0 + pre_gate * (1.0 - sigma))

    @pl.loop(0, chunks)
    def _(number):
        part = pl.ds(pl.multiple_of(number * chunk, chunk), chunk)
        await_place(back.at[:, part], sems.at[tiles + number])
        total = jnp.dot(hidden[...], back[:, part], preferred_element_type=f32)
        store_packed(total, (o0, o1, o2, o3), part)


def store_packed(total, outs, at):
    taken = outs[0].shape[0]
    for number, out in enumerate(outs):
        out[:, at] = total[number * taken : (number + 1) * taken].astype(bf16)


def backward_kernel(x0, x1, x2, x3, for_up, for_gate, *refs):
    *slabs, o0, o1, o2, o3, x, grads, into, back, sems = refs
    rows, width = x.shape
    units = back.shape[0] // 2
    chunk, chunks = back_chunk(width), width // back_chunk(width)
    triples, later = [], []
    for slab in range(2):
        place = back.at[pl.ds(slab * units, units)]
        triples.append((slabs[3 * slab + 2].at[0], place, sems.at[slab]))
    for number in range(chunks):
        lines = pl.ds(number * chunk, chunk)
        for column, matrix in enumerate((0, 1, 3, 4)):
            place = into.at[lines, pl.ds(column * units, units)]
            later.append((slabs[matrix].at[0, lines], place, sems.at[2 + number]))
    streams(triples)
    for part in column_chunks(width):
        x[:, part] = joined((x0, x1, x2, x3), part, rows)

    @pl.loop(0, 2)
    def _(slab):
        at = pl.ds(pl.multiple_of(slab * units, units), units)
        await_place(back.at[at], sems.at[slab])
        half = len(later) // 2 // 4 * 4 or len(later)
        pl.when(slab == 0)(functools.partial(streams, later[:half]))
        pl.when(slab == 1)(functools.partial(streams, later[half:]))
        hidden_grad = lax.dot_general(x[...], back[at], CONTRACT_COLS, preferred_element_type=f32)
        start = pl.multiple_of(2 * slab * units, 2 * units)
        gate_at, up_at = pl.ds(start, units), pl.ds(start + units, units)
        grads[:, gate_at] = (hidden_grad * for_gate[:, at]).astype(bf16)
        grads[:, up_at] = (hidden_grad * for_up[:, at]).astype(bf16)

    @pl.loop(0, chunks)
    def _(number):
        part = pl.ds(pl.multiple_of(number * chunk, chunk), chunk)
        await_place(into.at[part], sems.at[2 + number])
        total = lax.dot_general(
            grads[...], into[part], CONTRACT_COLS, preferred_element_type=f32
        )
        store_packed(total, (o0, o1, o2, o3), part)


def on_device(tokens, expert_ids, gate_values, cotangent, gate_weight, up_weight, down_weight):
    tok_dev, top = expert_ids.shape
    width, hidden = gate_weight.shape[1:]
    devices = lax.axis_size("expert")
    experts = devices // 2
    capacity = min(tok_dev, tok_dev * top * 5 // (4 * experts))
    far = range(FAR, devices, FAR)
    blocks = devices // FAR
    taken = slots_of(blocks, capacity)
    rows, slots = blocks * tok_dev, padded(len(PLANE) * taken)
    chip = (lax.axis_index("expert") // 2).reshape(1).astype(jnp.int32)
    shape = jax.ShapeDtypeStruct
    packed_shapes = [shape((taken, width), bf16)] * len(PLANE)

    own = (gate_weight, up_weight, down_weight)
    other = tuple(swap(slab, CORE) for slab in own)

    in_place = pl.BlockSpec(memory_space=pltpu.HBM)
    (coded,) = call(
        functools.partial(code_kernel, experts),
        [shape((tok_dev, width + padded(PIECES * experts)), bf16)],
        (tokens, expert_ids.T, gate_values.T),
    )
    held, offset = {0: coded}, devices // 2
    while offset >= FAR:
        held.update({at ^ offset: swap(value, offset) for at, value in held.items()})
        offset //= 2
    held = [held[at] for at in sorted(held)]

    whole = pl.BlockSpec(memory_space=pltpu.VMEM)
    *packed, by_row, by_slot = call(
        functools.partial(pack_tokens_kernel, experts, capacity),
        packed_shapes + [shape((rows, slots), f32), shape((slots, rows), f32)],
        (chip, *held),
        in_specs=[pl.BlockSpec(memory_space=pltpu.SMEM)] + [whole] * blocks,
        flops=2 * rows * slots * width,
    )
    far_cots = swap(after(cotangent, held[blocks // 2], other[0]), devices // 2)
    packed = [after(value, *other[:2]) for value in packed]
    packed[-1] = after(packed[-1], far_cots)
    x = [packed[0]] + [swap(value, offset) for value, offset in zip(packed[1:], PLANE[1:])]

    cots, offset = {0: cotangent, blocks // 2: far_cots}, devices // 4
    while offset >= FAR:
        wait = other[2] if offset == FAR else cotangent
        ready = {at: after(value, wait) for at, value in cots.items()}
        cots.update({at ^ offset // FAR: swap(value, offset) for at, value in ready.items()})
        offset //= 2
    cots = [cots[at] for at in sorted(cots)]

    packed = call(
        functools.partial(pack_cots_kernel, capacity),
        packed_shapes,
        (by_slot, *cots),
        flops=2 * rows * slots * width,
    )
    grads = [packed[0]] + [swap(value, offset) for value, offset in zip(packed[1:], PLANE[1:])]

    all_taken = len(PLANE) * taken
    tile = hidden
    tiles, chunks = 2 * hidden // tile, width // back_chunk(width)
    slab_room = [pltpu.VMEM((width, 4 * hidden), bf16), pltpu.VMEM((2 * hidden, width), bf16)]
    flops = 2 * 3 * all_taken * width * 2 * hidden
    *outs, for_up, for_gate = call(
        functools.partial(forward_kernel, tile),
        packed_shapes + [shape((all_taken, 2 * hidden), f32)] * 2,
        (*x, *own, *other),
        flops=flops,
        in_specs=[whole] * 4 + [in_place] * 6,
        limit=VMEM_LIMIT_EXPERT,
        scratch=[
            pltpu.VMEM((all_taken, width), bf16),
            pltpu.VMEM((all_taken, 2 * hidden), bf16),
            *slab_room,
            pltpu.SemaphoreType.DMA((tiles + chunks,)),
        ],
    )

    def go_home(values, weighted):
        back = [values[0]] + [swap(value, offset) for value, offset in zip(values[1:], PLANE[1:])]
        sums = call(
            functools.partial(unpack_kernel, weighted),
            [shape((tok_dev, width), bf16)] * blocks,
            (by_row, *back),
            flops=2 * rows * slots * width * (PIECES if weighted else 1),
        )
        home = [sums[0]] + [swap(value, offset) for value, offset in zip(sums[1:], far)]
        (result,) = call(sum_kernel, [shape((tok_dev, width), bf16)], home)
        return result

    layer_out = go_home(outs, True)
    backs = call(
        backward_kernel,
        packed_shapes,
        (*grads, for_up, for_gate, *own, *other),
        flops=flops,
        in_specs=[whole] * 6 + [in_place] * 6,
        limit=VMEM_LIMIT_EXPERT,
        scratch=[
            pltpu.VMEM((all_taken, width), bf16),
            pltpu.VMEM((all_taken, 4 * hidden), bf16),
            *slab_room,
            pltpu.SemaphoreType.DMA((2 + chunks,)),
        ],
    )
    token_grad = go_home(backs, False)
    return layer_out, token_grad


def solution(mesh):
    rows = P(("groups", "expert"), None)
    slabs = P("expert", None, None)
    return jax.shard_map(
        on_device,
        mesh=mesh,
        in_specs=(rows, rows, rows, rows, slabs, slabs, slabs),
        out_specs=(rows, rows),
        check_vma=False,
    )
```

```python
import functools
import math

import jax
import jax.numpy as jnp
from jax import lax
from jax.experimental import pallas as pl
from jax.experimental.pallas import tpu as pltpu
from jax.sharding import PartitionSpec as P

CORE, PLANE, FAR = 1, (0, 2, 4, 6), 8
f32, bf16 = jnp.float32, jnp.bfloat16
CONTRACT_COLS = (((1,), (1,)), ((), ()))
LANES = 128
PIECES = 3
VMEM_LIMIT = 16 * 1024 * 1024
VMEM_LIMIT_EXPERT = 48 * 1024 * 1024


def swap(value, offset):
    devices = lax.axis_size("expert")
    return lax.ppermute(value, "expert", [(i, i ^ offset) for i in range(devices)])


def after(value, *others):
    return lax.optimization_barrier((value, *others))[0]


def padded(count):
    return -(-count // LANES) * LANES


def chunk_of(width):
    return 512 if width % 512 == 0 else LANES


def back_chunk(width):
    return width // 2 if width % (2 * LANES) == 0 else LANES


def column_chunks(width):
    return [slice(at, at + chunk_of(width)) for at in range(0, width, chunk_of(width))]


def call(body, outs, args, flops=0, scratch=(), in_specs=None, limit=VMEM_LIMIT):
    size = sum(math.prod(a.shape) * a.dtype.itemsize for a in (*args, *outs))
    whole = pl.BlockSpec(memory_space=pltpu.VMEM)
    return pl.pallas_call(
        body,
        out_shape=outs,
        in_specs=[whole] * len(args) if in_specs is None else in_specs,
        out_specs=[whole] * len(outs),
        scratch_shapes=scratch,
        compiler_params=pltpu.CompilerParams(vmem_limit_bytes=limit),
        cost_estimate=pl.CostEstimate(flops=flops, bytes_accessed=size, transcendentals=0),
    )(*args)


def streams(triples):
    copies = [pltpu.make_async_copy(*triple) for triple in triples]
    for copy in copies:
        copy.start()
    return copies


def await_place(place, sem):
    pltpu.make_async_copy(place, place, sem).wait()


def code_kernel(experts, tokens, routes, out):
    rows, width = tokens.shape
    gate_width = out.shape[1] - width
    line = lax.broadcasted_iota(jnp.int32, (gate_width, rows), 0)
    rest = jnp.zeros(line.shape, f32)
    place, top = (line % experts).astype(f32), routes.shape[0] // 2
    for k in range(top):
        rest = jnp.where(routes[k : k + 1] == place, routes[top + k : top + k + 1], rest)
    columns = jnp.zeros(line.shape, f32)
    for number in range(PIECES):
        piece = rest.astype(bf16).astype(f32)
        columns = jnp.where(line // experts == number, piece, columns)
        rest = rest - piece
    out[:, width:] = columns.T.astype(bf16)
    for at in range(0, width, LANES):
        block = tokens[:, at : at + LANES].astype(f32)
        scale = jnp.max(jnp.abs(block), axis=1, keepdims=True) + 1e-06
        scale = scale.astype(bf16).astype(f32)
        quantized = (block / scale).astype(bf16).astype(f32)
        out[:, at : at + LANES] = (quantized * scale).astype(bf16)


def pack_tokens_kernel(experts, capacity, chip, *refs):
    *blocks, first, second, third, fourth, by_row, by_slot = refs
    tok_dev = blocks[0].shape[0]
    rows, slots = by_row.shape
    width = first.shape[1]
    taken = slots_of(len(blocks), capacity)
    columns = jnp.concatenate([block[:, width:].astype(f32) for block in blocks], axis=0)
    lane = lax.broadcasted_iota(jnp.int32, columns.shape, 1)
    pick = lax.broadcasted_iota(jnp.int32, (rows, LANES), 1)
    gates, named = [], jnp.zeros((rows, LANES), f32)
    for number in range(len(PLANE)):
        mine = (lane % experts == (chip[0] ^ number)) & (lane < PIECES * experts)
        gates.append(jnp.sum(jnp.where(mine, columns, 0.0), axis=1, keepdims=True))
        named = jnp.where((pick == number) & (gates[-1] > 0.0), 1.0, named)
    row = lax.broadcasted_iota(jnp.int32, (rows, rows), 0)
    other = lax.broadcasted_iota(jnp.int32, (rows, rows), 1)
    earlier = (row // tok_dev == other // tok_dev) & (other < row)
    earlier = jnp.where(earlier, 1.0, 0.0).astype(bf16)
    counts = jnp.dot(earlier, named.astype(bf16), preferred_element_type=f32)
    slot = lax.broadcasted_iota(jnp.int32, (rows, slots), 1)
    start = lax.broadcasted_iota(jnp.int32, (rows, 1), 0) // tok_dev * capacity
    weights = jnp.zeros((rows, slots), f32)
    for number, gate in enumerate(gates):
        count = jnp.sum(jnp.where(pick == number, counts, 0.0), axis=1, keepdims=True)
        place = number * taken + start + count.astype(jnp.int32)
        weights = jnp.where(slot == place, gate, weights)
    by_row[...] = weights
    by_slot[...] = weights.T
    chosen = jnp.where(by_slot[...] > 0.0, 1.0, 0.0).astype(bf16)
    for part in column_chunks(width):
        held = jnp.concatenate([block[:, part] for block in blocks], axis=0)
        packed = jnp.dot(chosen, held, preferred_element_type=f32)
        for number, out in enumerate((first, second, third, fourth)):
            out[:, part] = packed[number * taken : (number + 1) * taken].astype(bf16)


def pack_cots_kernel(capacity, by_slot, *refs):
    *blocks, first, second, third, fourth = refs
    width = first.shape[1]
    taken = slots_of(len(blocks), capacity)
    gate = jnp.sum(by_slot[...], axis=1, keepdims=True)
    chosen = jnp.where(by_slot[...] > 0.0, 1.0, 0.0).astype(bf16)
    for part in column_chunks(width):
        held = jnp.concatenate([block[:, part] for block in blocks], axis=0)
        packed = gate * jnp.dot(chosen, held, preferred_element_type=f32)
        for number, out in enumerate((first, second, third, fourth)):
            out[:, part] = packed[number * taken : (number + 1) * taken].astype(bf16)


def slots_of(blocks, capacity):
    return blocks * capacity


def joined(refs, part, height, kind=bf16):
    taken = [ref[:, part].astype(f32) for ref in refs]
    rest = height - sum(value.shape[0] for value in taken)
    if rest:
        taken.append(jnp.zeros((rest, taken[0].shape[1]), f32))
    return jnp.concatenate(taken, axis=0).astype(kind)


def unpack_kernel(weighted, by_row, first, second, third, fourth, *outs):
    rows, slots = by_row.shape
    tok_dev = outs[0].shape[0]
    if weighted:
        matrices, rest = [], by_row[...]
        for _ in range(PIECES):
            matrices.append(rest.astype(bf16))
            rest = rest - matrices[-1].astype(f32)
    else:
        matrices = [jnp.where(by_row[...] > 0.0, 1.0, 0.0).astype(bf16)]
    for part in column_chunks(first.shape[1]):
        packed = joined((first, second, third, fourth), part, slots)
        total = jnp.dot(matrices[0], packed, preferred_element_type=f32)
        for matrix in matrices[1:]:
            total = total + jnp.dot(matrix, packed, preferred_element_type=f32)
        for number, out in enumerate(outs):
            out[:, part] = total[number * tok_dev : (number + 1) * tok_dev].astype(bf16)


def sum_kernel(*refs):
    *blocks, out = refs
    for part in column_chunks(out.shape[1]):
        total = blocks[0][:, part].astype(f32)
        for block in blocks[1:]:
            total = total + block[:, part].astype(f32)
        out[:, part] = total.astype(bf16)


def forward_kernel(tile, x0, x1, x2, x3, *refs):
    *slabs, o0, o1, o2, o3, for_up, for_gate, x, hidden, into, back, sems = refs
    rows, width = x.shape
    units = back.shape[0] // 2
    chunk, tiles, chunks = back_chunk(width), 2 * units // tile, width // back_chunk(width)
    triples = []
    for number in range(tiles):
        slab, at = divmod(number * tile, units)
        for half, source in enumerate(slabs[3 * slab : 3 * slab + 2]):
            place = into.at[:, pl.ds((2 * number + half) * tile, tile)]
            triples.append((source.at[0, :, pl.ds(at, tile)], place, sems.at[number]))
    for number in range(chunks):
        columns = pl.ds(number * chunk, chunk)
        for slab in range(2):
            place = back.at[pl.ds(slab * units, units), columns]
            source = slabs[3 * slab + 2].at[0, :, columns]
            triples.append((source, place, sems.at[tiles + number]))
    streams(triples)
    for part in column_chunks(width):
        x[:, part] = joined((x0, x1, x2, x3), part, rows)

    @pl.loop(0, tiles)
    def _(number):
        columns = pl.ds(pl.multiple_of(number * 2 * tile, 2 * tile), 2 * tile)
        await_place(into.at[:, columns], sems.at[number])
        pre = jnp.dot(x[...], into[:, columns], preferred_element_type=f32)
        pre_gate, pre_up = pre[:, :tile], pre[:, tile:]
        sigma = jax.nn.sigmoid(pre_gate)
        activated = pre_gate * sigma
        at = pl.ds(pl.multiple_of(number * tile, tile), tile)
        hidden[:, at] = (activated * pre_up).astype(bf16)
        for_up[:, at] = activated
        for_gate[:, at] = pre_up * sigma * (1.0 + pre_gate * (1.0 - sigma))

    @pl.loop(0, chunks)
    def _(number):
        part = pl.ds(pl.multiple_of(number * chunk, chunk), chunk)
        await_place(back.at[:, part], sems.at[tiles + number])
        total = jnp.dot(hidden[...], back[:, part], preferred_element_type=f32)
        store_packed(total, (o0, o1, o2, o3), part)


def store_packed(total, outs, at):
    taken = outs[0].shape[0]
    for number, out in enumerate(outs):
        out[:, at] = total[number * taken : (number + 1) * taken].astype(bf16)


def backward_kernel(x0, x1, x2, x3, for_up, for_gate, *refs):
    *slabs, o0, o1, o2, o3, x, grads, into, back, sems = refs
    rows, width = x.shape
    units = back.shape[0] // 2
    chunk, chunks = back_chunk(width), width // back_chunk(width)
    triples = []
    for slab in range(2):
        place = back.at[pl.ds(slab * units, units)]
        triples.append((slabs[3 * slab + 2].at[0], place, sems.at[slab]))
    for number in range(chunks):
        lines = pl.ds(number * chunk, chunk)
        for column, matrix in enumerate((0, 1, 3, 4)):
            place = into.at[lines, pl.ds(column * units, units)]
            triples.append((slabs[matrix].at[0, lines], place, sems.at[2 + number]))
    streams(triples)
    for part in column_chunks(width):
        x[:, part] = joined((x0, x1, x2, x3), part, rows)

    @pl.loop(0, 2)
    def _(slab):
        at = pl.ds(pl.multiple_of(slab * units, units), units)
        await_place(back.at[at], sems.at[slab])
        hidden_grad = lax.dot_general(x[...], back[at], CONTRACT_COLS, preferred_element_type=f32)
        start = pl.multiple_of(2 * slab * units, 2 * units)
        gate_at, up_at = pl.ds(start, units), pl.ds(start + units, units)
        grads[:, gate_at] = (hidden_grad * for_gate[:, at]).astype(bf16)
        grads[:, up_at] = (hidden_grad * for_up[:, at]).astype(bf16)

    @pl.loop(0, chunks)
    def _(number):
        part = pl.ds(pl.multiple_of(number * chunk, chunk), chunk)
        await_place(into.at[part], sems.at[2 + number])
        total = lax.dot_general(
            grads[...], into[part], CONTRACT_COLS, preferred_element_type=f32
        )
        store_packed(total, (o0, o1, o2, o3), part)


def on_device(tokens, expert_ids, gate_values, cotangent, gate_weight, up_weight, down_weight):
    tok_dev, top = expert_ids.shape
    width, hidden = gate_weight.shape[1:]
    devices = lax.axis_size("expert")
    experts = devices // 2
    capacity = min(tok_dev, tok_dev * top * 5 // (4 * experts))
    far = range(FAR, devices, FAR)
    blocks = devices // FAR
    taken = slots_of(blocks, capacity)
    rows, slots = blocks * tok_dev, padded(len(PLANE) * taken)
    chip = (lax.axis_index("expert") // 2).reshape(1).astype(jnp.int32)
    shape = jax.ShapeDtypeStruct
    packed_shapes = [shape((taken, width), bf16)] * len(PLANE)

    own = (gate_weight, up_weight, down_weight)
    other = tuple(swap(slab, CORE) for slab in own)

    in_place = pl.BlockSpec(memory_space=pltpu.HBM)
    (coded,) = call(
        functools.partial(code_kernel, experts),
        [shape((tok_dev, width + padded(PIECES * experts)), bf16)],
        (tokens, jnp.concatenate([expert_ids.T.astype(f32), gate_values.T], axis=0)),
    )
    held, offset = {0: coded}, devices // 2
    while offset >= FAR:
        held.update({at ^ offset: swap(value, offset) for at, value in held.items()})
        offset //= 2
    held = [held[at] for at in sorted(held)]

    whole = pl.BlockSpec(memory_space=pltpu.VMEM)
    *packed, by_row, by_slot = call(
        functools.partial(pack_tokens_kernel, experts, capacity),
        packed_shapes + [shape((rows, slots), f32), shape((slots, rows), f32)],
        (chip, *held),
        in_specs=[pl.BlockSpec(memory_space=pltpu.SMEM)] + [whole] * blocks,
        flops=2 * rows * slots * width,
    )
    far_cots = swap(after(cotangent, held[blocks // 2], other[0]), devices // 2)
    packed = [after(value, *other[:2]) for value in packed]
    packed[-1] = after(packed[-1], far_cots)
    x = [packed[0]] + [swap(value, offset) for value, offset in zip(packed[1:], PLANE[1:])]

    cots, offset = {0: cotangent, blocks // 2: far_cots}, devices // 4
    while offset >= FAR:
        wait = other[2] if offset == FAR else cotangent
        ready = {at: after(value, wait) for at, value in cots.items()}
        cots.update({at ^ offset // FAR: swap(value, offset) for at, value in ready.items()})
        offset //= 2
    cots = [cots[at] for at in sorted(cots)]

    packed = call(
        functools.partial(pack_cots_kernel, capacity),
        packed_shapes,
        (by_slot, *cots),
        flops=2 * rows * slots * width,
    )
    grads = [packed[0]] + [swap(value, offset) for value, offset in zip(packed[1:], PLANE[1:])]

    all_taken = len(PLANE) * taken
    tile = hidden
    tiles, chunks = 2 * hidden // tile, width // back_chunk(width)
    slab_room = [pltpu.VMEM((width, 4 * hidden), bf16), pltpu.VMEM((2 * hidden, width), bf16)]
    flops = 2 * 3 * all_taken * width * 2 * hidden
    *outs, for_up, for_gate = call(
        functools.partial(forward_kernel, tile),
        packed_shapes + [shape((all_taken, 2 * hidden), f32)] * 2,
        (*x, *own, *other),
        flops=flops,
        in_specs=[whole] * 4 + [in_place] * 6,
        limit=VMEM_LIMIT_EXPERT,
        scratch=[
            pltpu.VMEM((all_taken, width), bf16),
            pltpu.VMEM((all_taken, 2 * hidden), bf16),
            *slab_room,
            pltpu.SemaphoreType.DMA((tiles + chunks,)),
        ],
    )

    def go_home(values, weighted):
        back = [values[0]] + [swap(value, offset) for value, offset in zip(values[1:], PLANE[1:])]
        sums = call(
            functools.partial(unpack_kernel, weighted),
            [shape((tok_dev, width), bf16)] * blocks,
            (by_row, *back),
            flops=2 * rows * slots * width * (PIECES if weighted else 1),
        )
        home = [sums[0]] + [swap(value, offset) for value, offset in zip(sums[1:], far)]
        (result,) = call(sum_kernel, [shape((tok_dev, width), bf16)], home)
        return result

    layer_out = go_home(outs, True)
    backs = call(
        backward_kernel,
        packed_shapes,
        (*grads, for_up, for_gate, *own, *other),
        flops=flops,
        in_specs=[whole] * 6 + [in_place] * 6,
        limit=VMEM_LIMIT_EXPERT,
        scratch=[
            pltpu.VMEM((all_taken, width), bf16),
            pltpu.VMEM((all_taken, 4 * hidden), bf16),
            *slab_room,
            pltpu.SemaphoreType.DMA((2 + chunks,)),
        ],
    )
    token_grad = go_home(backs, False)
    return layer_out, token_grad


def solution(mesh):
    rows = P(("groups", "expert"), None)
    slabs = P("expert", None, None)
    return jax.shard_map(
        on_device,
        mesh=mesh,
        in_specs=(rows, rows, rows, rows, slabs, slabs, slabs),
        out_specs=(rows, rows),
        check_vma=False,
    )
```
